32 devices in a mesh: groups: 2 (over x), dp: 8 (over z, y), tensor: 2 (over core).
Axes of the slice: x: 2, y: 2, z: 4, core: 2. Of those that a mesh axis runs over, the one named last changes fastest.
Arguments:
- tokens: bfloat16 [14336, 8192], P(('groups', 'dp'), 'tensor'), parts along dimension 0, may hold values from -6 to 6
- base_weight: bfloat16 [8192, 1024], P('tensor'), may hold values from -0.0625 to 0.0625
- adapter_down: bfloat16 [32, 8192, 16], P('dp', 'tensor'), may hold values from -0.0625 to 0.0625
- adapter_up: bfloat16 [32, 16, 1024], P('dp', None, 'tensor'), may hold values from -0.75 to 0.75
- out_cotangent: bfloat16 [14336, 1024], P(('groups', 'dp'), 'tensor'), parts along dimension 0, may hold values from -6 to 6
- block_tenant: int32 [112], P(('groups', 'dp')), parts along dimension 0, may hold values from 0 to 31, as said below
- block_valid: int32 [112], P(('groups', 'dp')), parts along dimension 0, may hold values from 1 to 128, as said below
- tenant_slot: int32 [64], P('groups'), parts along dimension 0, may hold values from 0 to 31, as said below
Outputs:
- projected: bfloat16 [14336, 1024], P(('groups', 'dp'), 'tensor'), parts along dimension 0
- grad_tokens: bfloat16 [14336, 8192], P(('groups', 'dp'), 'tensor'), parts along dimension 0
- grad_down: float32 [64, 8192, 16], P(('groups', 'dp'), 'tensor'), parts along dimension 0
- grad_up: float32 [64, 16, 1024], P(('groups', 'dp'), None, 'tensor'), parts along dimension 0
The draws below stay inside these ranges and needn't reach their ends.
There are 2 independent parts, one for each index of `groups`. The reference program is written for one: setup_inputs(seed, part) draws one part's arguments, and reference() takes and returns one part's arrays. A program takes and returns all parts, laid end to end along the dimension named above; an argument that names none is the same for every part. Nothing has to cross between parts.
Inputs may be any that keep to these rules, and one draw needn't show every extreme that they name: `tenant_slot`: a permutation; slot s is held by dp index s // 4. `block_tenant`: among the blocks of one dp index, at most 2 name tenants whose slots are held by one same dp index; some dp index reaches 2 in every draw. `block_valid`: the valid tokens of a block come first in it.
All inputs are finite; a program needn't handle non-finite values.
Results may differ from the reference program's by a relative error of at most 0.0045.
Values may be sent and summed in bfloat16 or wider, within the bound.
No kernel may reach another device: no remote copies, remote signals or barrier semaphores. Data moves between devices by JAX's collectives and lax.ppermute only.
A program may use at most 192 MiB of HBM per device.

```python
import jax
import jax.numpy as jnp

D = 8192
VALUE_WIDTH = 1024
R = 16
TENANT_BLOCK = 128
CAP = 2
TEN_DEV = 4
TOTAL_TOKENS = 7168
TENANTS = 32
NBLK = 56
N_DP = 8


def tenant_layout(key):
    keys = jax.random.split(jax.random.fold_in(key, 7), 6)
    slot_table = jax.random.permutation(keys[0], TENANTS).astype(jnp.int32)
    slot_tenant = jnp.argsort(slot_table).astype(jnp.int32)
    hot_owner = jnp.where(jax.random.permutation(keys[1], N_DP) < 2, 2 * N_DP, 0)
    scores = jax.random.randint(keys[2], (N_DP, N_DP), 0, N_DP) + hot_owner[None, :]
    distinct = scores * N_DP + jnp.arange(N_DP, dtype=jnp.int32)[None, :]
    ranking = jnp.argsort(-distinct, axis=1).astype(jnp.int32)
    offsets = jax.random.randint(keys[3], (N_DP,), 0, 2).at[0].set(0)
    per_device = TOTAL_TOKENS // TENANT_BLOCK // N_DP
    grouping = (jnp.arange(per_device, dtype=jnp.int32)[None, :] + offsets[:, None]) // CAP
    owner_dev = jnp.take_along_axis(ranking, grouping, axis=1)
    local_slot = jax.random.randint(keys[4], (N_DP, per_device), 0, TEN_DEV)
    local_slot = local_slot.at[0, 1].set(local_slot[0, 0])
    tenant_ids = slot_tenant[owner_dev * TEN_DEV + local_slot]
    same_next = jnp.concatenate([tenant_ids[:, 1:] == tenant_ids[:, :-1], jnp.zeros((N_DP, 1), dtype=bool)], axis=1)
    partial_fill = jax.random.randint(keys[5], (N_DP, per_device), 1, TENANT_BLOCK + 1)
    valid_count = jnp.where(same_next, TENANT_BLOCK, partial_fill).astype(jnp.int32)
    return (slot_table, tenant_ids.reshape(-1).astype(jnp.int32), valid_count.reshape(-1))


def draw_tenant_slot(key, part):
    shared = tenant_layout(key)
    return shared[0]


def draw_block_tenant(key, part):
    shared = tenant_layout(key)
    return shared[1]


def draw_block_valid(key, part):
    shared = tenant_layout(key)
    return shared[2]


def shard_levels(key, dims, cuts, smallest, top_value):
    level = 1.0
    for position, blocks in cuts:
        draws = jax.random.uniform(jax.random.fold_in(jax.random.fold_in(key, 6), position), (blocks,), jnp.float32, smallest / len(cuts), top_value / len(cuts))
        level = level * jnp.repeat(jnp.exp(draws), dims[position] // blocks).reshape((-1,) + (1,) * (len(dims) - 1 - position))
    return level


def normal_values(own_key, shape, scale, most, cuts=(), kind=jnp.bfloat16):
    factor_of = shard_levels(own_key, shape, cuts, -0.22, 0.18) if cuts else 1.0
    array = jax.random.normal(own_key, shape, jnp.float32) * scale * factor_of
    return jnp.minimum(jnp.maximum(array, -most), most).astype(kind)


def setup_inputs(seed: int = 0, part: int = 0) -> dict:
    arg_keys = jax.random.split(jax.random.key(seed), 9)
    part_splits = jax.random.split(jax.random.fold_in(arg_keys[8], part), 9)
    tokens = normal_values(part_splits[0], (TOTAL_TOKENS, D), 1.0, 6.0, ((0, 8), (1, 2)))
    base_weight = normal_values(arg_keys[1], (D, VALUE_WIDTH), D ** -0.5, 0.0625, ((0, 2),))
    adapter_down = normal_values(arg_keys[2], (TENANTS, D, R), D ** -0.5, 0.0625, ((0, 8), (1, 2)))
    adapter_up = normal_values(arg_keys[3], (TENANTS, R, VALUE_WIDTH), (4 * R) ** -0.5, 0.75, ((0, 8), (2, 2)))
    out_cotangent = normal_values(part_splits[4], (TOTAL_TOKENS, VALUE_WIDTH), 1.0, 6.0, ((0, 8), (1, 2)))
    block_tenant = draw_block_tenant(jax.random.fold_in(jax.random.fold_in(arg_keys[8], part), 71), part)
    block_valid = draw_block_valid(jax.random.fold_in(jax.random.fold_in(arg_keys[8], part), 71), part)
    tenant_slot = draw_tenant_slot(jax.random.fold_in(jax.random.fold_in(arg_keys[8], part), 71), part)
    return {"tokens": tokens, "base_weight": base_weight, "adapter_down": adapter_down, "adapter_up": adapter_up, "out_cotangent": out_cotangent, "block_tenant": block_tenant, "block_valid": block_valid, "tenant_slot": tenant_slot}


adapter_scale = 2.0


def reference(tokens, base_weight, adapter_down, adapter_up, out_cotangent, block_tenant, block_valid, tenant_slot):
    float_single = jnp.float32
    bfloat_half = jnp.bfloat16
    slots_used = tenant_slot[block_tenant].astype(jnp.int32)
    positions = jnp.arange(TENANT_BLOCK, dtype=jnp.int32)
    validity_mask = (positions[None, :] < block_valid[:, None]).astype(float_single)
    block_down = adapter_down[slots_used].astype(float_single)
    block_up_weight = adapter_up[slots_used].astype(float_single)
    x_blocks = tokens.reshape(NBLK, TENANT_BLOCK, D).astype(float_single)
    frozen_output = jnp.dot(tokens, base_weight, preferred_element_type=float_single).reshape(NBLK, TENANT_BLOCK, VALUE_WIDTH)
    narrowed_rows = jnp.einsum('btd,bdr->btr', x_blocks, block_down).astype(bfloat_half)
    widened_rows = jnp.einsum('btr,brk->btk', narrowed_rows.astype(float_single), block_up_weight)
    projected = (validity_mask[:, :, None] * (frozen_output + adapter_scale * widened_rows)).astype(bfloat_half).reshape(TOTAL_TOKENS, VALUE_WIDTH)
    output_gradient = out_cotangent.reshape(NBLK, TENANT_BLOCK, VALUE_WIDTH) * validity_mask[:, :, None].astype(bfloat_half)
    backward_narrowed = (adapter_scale * jnp.einsum('oml,opl->omp', output_gradient.astype(float_single), block_up_weight)).astype(bfloat_half)
    through = jnp.dot(output_gradient.reshape(TOTAL_TOKENS, VALUE_WIDTH), base_weight.T, preferred_element_type=float_single).reshape(NBLK, TENANT_BLOCK, D)
    grad_tokens = (through + jnp.einsum('btr,bdr->btd', backward_narrowed.astype(float_single), block_down)).astype(bfloat_half).reshape(TOTAL_TOKENS, D)
    down_blocks = jnp.einsum('btd,btr->bdr', x_blocks, backward_narrowed.astype(float_single))
    up_weight_blocks = adapter_scale * jnp.einsum('qsh,qsc->qhc', narrowed_rows.astype(float_single), output_gradient.astype(float_single))
    grad_down = jax.ops.segment_sum(down_blocks, slots_used, num_segments=TENANTS)
    grad_up = jax.ops.segment_sum(up_weight_blocks, slots_used, num_segments=TENANTS)
    return projected, grad_tokens, grad_down, grad_up
```

```python
import jax
import jax.numpy as jnp
from jax import lax
from jax.sharding import PartitionSpec as P

TENANT_BLOCK = 128
CAP = 2
NEAR = 4

adapter_scale = 2.0


def _swap(x, axis):
    return lax.ppermute(x, axis, [(0, 1), (1, 0)])


def _xor(x, n, k):
    return lax.ppermute(x, "dp", [(i, i ^ k) for i in range(n)])


def _owners(slots, ten_dev):
    owner = slots // ten_dev
    n = slots.shape[0]
    earlier = jnp.arange(n)[None, :] < jnp.arange(n)[:, None]
    rank = jnp.sum((owner[None, :] == owner[:, None]) & earlier, axis=1)
    return owner, rank.astype(jnp.int32)


def on_device(
    n_groups,
    n_dp,
    tokens,
    base_weight,
    adapter_down,
    adapter_up,
    out_cotangent,
    block_tenant,
    block_valid,
    tenant_slot,
):
    f32 = jnp.float32
    bf16 = jnp.bfloat16
    i32 = jnp.int32
    nb = block_tenant.shape[0]
    rows, width = tokens.shape
    cols = out_cotangent.shape[1]
    tenants = tenant_slot.shape[0]
    ten_dev, _, rank_dim = adapter_down.shape
    n_far = n_dp // NEAR
    me = lax.axis_index("dp")
    core = lax.axis_index("tensor")
    group = lax.axis_index("groups")

    tenant_match = block_tenant[:, None] == jnp.arange(tenants, dtype=i32)[None, :]
    slots = jnp.sum(jnp.where(tenant_match, tenant_slot[None, :], 0), axis=1).astype(i32)
    valid = jnp.arange(TENANT_BLOCK, dtype=i32)[None, :] < block_valid[:, None]
    valid_rows = valid.reshape(rows, 1)

    grad_out = out_cotangent * valid_rows.astype(bf16)
    grad_other = _swap(grad_out, "tensor")

    down_t = jnp.swapaxes(adapter_down, 1, 2)

    ups = [adapter_up] + [_xor(adapter_up, n_dp, NEAR * j) for j in range(1, n_far)]
    mine = jnp.concatenate(ups, axis=0).reshape(n_far * ten_dev * rank_dim, cols)
    tag = jnp.zeros((16, cols), bf16).at[0, :nb].set(slots.astype(bf16))
    packet = jnp.concatenate([mine, tag], axis=0)
    packets = [packet] + [_xor(packet, n_dp, k) for k in range(1, NEAR)]
    near_slots = [slots] + [p[-16, :nb].astype(i32) for p in packets[1:]]
    all_up = jnp.stack([p[:-16] for p in packets]).reshape(
        NEAR, n_far, ten_dev, rank_dim, cols
    )

    def up_row(s):
        rel = (s // ten_dev) ^ me
        return ((rel % NEAR) * n_far + rel // NEAR) * ten_dev + s % ten_dev

    block_up = jnp.take(
        all_up.reshape(n_dp * ten_dev, rank_dim, cols), up_row(slots), axis=0
    )

    if n_groups == 2 and n_dp == 8:
        quarter = width // 4
        mine_q = group * 2 + me % 2
        own = lax.dynamic_slice_in_dim(down_t, mine_q * quarter, quarter, axis=2)
        to_y = lax.dynamic_slice_in_dim(down_t, (mine_q ^ 1) * quarter, quarter, axis=2)
        shard = jnp.concatenate([own, _xor(to_y, n_dp, 1)], axis=0)
        pair = jnp.concatenate([shard, _xor(shard, n_dp, 4)], axis=0)
        every = jnp.concatenate([pair, _xor(pair, n_dp, 2)], axis=0)

        def down_row(s):
            rel = (s // ten_dev) ^ me
            z = rel // 2
            place = (z % 2) * 4 + (z // 2) * 2 + rel % 2
            return place * ten_dev + s % ten_dev

        both = jnp.stack([slots, near_slots[1]])
        both_x = _swap(both, "groups")
        need_y = jnp.take(every, down_row(near_slots[1]), axis=0)
        need_x = jnp.take(every, down_row(both_x[0]), axis=0)
        need_d = jnp.take(every, down_row(both_x[1]), axis=0)
        got_0 = jnp.take(every, down_row(slots), axis=0)
        got_y = _xor(need_y, n_dp, 1)
        got_x = _swap(need_x, "groups")
        got_d = lax.ppermute(
            need_d,
            ("groups", "dp"),
            [(g * n_dp + d, (1 - g) * n_dp + (d ^ 1)) for g in range(2) for d in range(n_dp)],
        )
        parts = jnp.stack([got_0, got_y, got_x, got_d])
        parts = jnp.take(parts, jnp.arange(4) ^ mine_q, axis=0)
        block_down = jnp.transpose(parts, (1, 2, 0, 3)).reshape(nb * rank_dim, width)
    else:
        every = lax.all_gather(down_t, "dp", axis=0, tiled=True)
        block_down = jnp.take(every, slots, axis=0).reshape(nb * rank_dim, width)

    same_block = (
        jnp.arange(nb)[:, None, None, None] == jnp.arange(nb)[None, None, :, None]
    )

    def pick(full):
        x = full.reshape(nb, TENANT_BLOCK, nb, rank_dim)
        return jnp.sum(jnp.where(same_block, x, 0.0), axis=2)

    def spread(x):
        y = jnp.where(same_block, x[:, :, None, :], jnp.zeros((), x.dtype))
        return y.reshape(rows, nb * rank_dim)

    up_2d = block_up.reshape(nb * rank_dim, cols)
    back_part = pick(
        lax.dot_general(grad_out, up_2d, (((1,), (1,)), ((), ())), preferred_element_type=f32)
    )
    back_shrink = (adapter_scale * (back_part + _swap(back_part, "tensor"))).astype(bf16)

    owner, order = _owners(slots, ten_dev)
    rel = owner ^ me
    place = ((rel % NEAR) * n_far + rel // NEAR) * CAP + order
    sel = (place[None, :] == jnp.arange(n_dp * CAP)[:, None]).astype(bf16)
    back_t = jnp.transpose(back_shrink, (2, 0, 1))
    packed_back = (sel[:, None, :, None] * back_t[None]).reshape(n_dp * CAP * rank_dim, rows)
    near_rows = n_far * CAP * rank_dim
    sends = lax.dot_general(
        packed_back, tokens, (((1,), (0,)), ((), ())), preferred_element_type=f32
    ).astype(bf16)

    hot = []
    for k in range(NEAR):
        o, r = _owners(near_slots[k], ten_dev)
        hit = (
            (o[None, None, :] == (me ^ (NEAR * jnp.arange(n_far)))[:, None, None])
            & (r[None, None, :] == jnp.arange(CAP)[None, :, None])
        )
        local = jnp.sum(jnp.where(hit, near_slots[k][None, None, :] % ten_dev, 0), axis=2)
        hot.append(local)
    hot = jnp.stack(hot, axis=1).reshape(n_far, NEAR * CAP)
    one_hot = (hot[:, None, :] == jnp.arange(ten_dev)[None, :, None]).astype(bf16)
    eye = jnp.eye(rank_dim, dtype=bf16)
    summing = (one_hot[:, :, None, :, None] * eye[None, None, :, None, :]).reshape(
        n_far, ten_dev * rank_dim, NEAR * CAP * rank_dim
    )

    def scatter(sends):
        wide = sends.shape[1]
        packs = sends.reshape(NEAR, near_rows, wide)
        got = [packs[0]] + [_xor(packs[k], n_dp, k) for k in range(1, NEAR)]
        got = [g.reshape(n_far, CAP * rank_dim, wide) for g in got]

        def dense(j):
            stacked = jnp.concatenate([g[j] for g in got], axis=0)
            return jnp.dot(summing[j], stacked, preferred_element_type=f32)

        arrived = [_xor(dense(j).astype(bf16), n_dp, NEAR * j) for j in range(1, n_far)]
        total = dense(0)
        for a in arrived:
            total = total + a.astype(f32)
        return total.reshape(ten_dev, rank_dim, wide)

    grad_down = jnp.swapaxes(scatter(sends), 1, 2)

    w_own = lax.dynamic_slice_in_dim(base_weight, core * cols, cols, axis=1)
    w_other = lax.dynamic_slice_in_dim(base_weight, (1 - core) * cols, cols, axis=1)
    base_other = jnp.dot(tokens, w_other, preferred_element_type=f32).astype(bf16)
    base_own = jnp.dot(tokens, w_own, preferred_element_type=f32)
    base = base_own + _swap(base_other, "tensor").astype(f32)

    shrink_part = pick(
        lax.dot_general(tokens, block_down, (((1,), (1,)), ((), ())), preferred_element_type=f32)
    )
    shrink = (shrink_part + _swap(shrink_part, "tensor")).astype(bf16)
    widened = jnp.dot(spread(shrink), up_2d, preferred_element_type=f32)
    projected = jnp.where(valid_rows, base + adapter_scale * widened, 0.0).astype(bf16)

    shrink_t = jnp.transpose(shrink, (2, 0, 1))
    packed_shrink = (sel[:, None, :, None] * shrink_t[None]).reshape(
        n_dp * CAP * rank_dim, rows
    )
    up_sends = (
        adapter_scale * jnp.dot(packed_shrink, grad_out, preferred_element_type=f32)
    ).astype(bf16)
    grad_up = scatter(up_sends)

    through = lax.dot_general(
        grad_out, w_own, (((1,), (1,)), ((), ())), preferred_element_type=f32
    ) + lax.dot_general(
        grad_other, w_other, (((1,), (1,)), ((), ())), preferred_element_type=f32
    )
    grad_tokens = (
        through + jnp.dot(spread(back_shrink), block_down, preferred_element_type=f32)
    ).astype(bf16)
    return projected, grad_tokens, grad_down, grad_up


def solution(mesh):
    n_groups, n_dp = mesh.shape["groups"], mesh.shape["dp"]
    in_specs = (
        P(("groups", "dp"), "tensor"),
        P("tensor", None),
        P("dp", "tensor", None),
        P("dp", None, "tensor"),
        P(("groups", "dp"), "tensor"),
        P(("groups", "dp")),
        P(("groups", "dp")),
        P("groups"),
    )
    out_specs = (
        P(("groups", "dp"), "tensor"),
        P(("groups", "dp"), "tensor"),
        P(("groups", "dp"), "tensor", None),
        P(("groups", "dp"), None, "tensor"),
    )

    def run(*args):
        return on_device(n_groups, n_dp, *args)

    return jax.shard_map(
        run, mesh=mesh, in_specs=in_specs, out_specs=out_specs, check_vma=False
    )
```

```python
import functools

import jax
import jax.numpy as jnp
from jax import lax
from jax.experimental import pallas as pl
from jax.experimental.pallas import tpu as pltpu
from jax.sharding import PartitionSpec as P

TENANT_BLOCK = 128
CAP = 2
NEAR = 4
VMEM_LIMIT = 48 * 1024 * 1024

adapter_scale = 2.0
f32 = jnp.float32
bf16 = jnp.bfloat16
i32 = jnp.int32

NT = (((1,), (1,)), ((), ()))
TN = (((0,), (0,)), ((), ()))
NN = (((1,), (0,)), ((), ()))


def _dot(a, b, dims):
    return lax.dot_general(a, b, dims, preferred_element_type=f32)


def _swap(x, axis):
    return lax.ppermute(x, axis, [(0, 1), (1, 0)])


def _xor(x, n, k):
    return lax.ppermute(x, "dp", [(i, i ^ k) for i in range(n)])


def _call(body, n_scalars, grid, in_specs, out_specs, out_shape, scratch, flops, moved):
    return pl.pallas_call(
        body,
        grid_spec=pltpu.PrefetchScalarGridSpec(
            num_scalar_prefetch=n_scalars,
            grid=grid,
            in_specs=in_specs,
            out_specs=out_specs,
            scratch_shapes=scratch,
        ),
        out_shape=out_shape,
        compiler_params=pltpu.CompilerParams(vmem_limit_bytes=VMEM_LIMIT),
        cost_estimate=pl.CostEstimate(flops=flops, bytes_accessed=moved, transcendentals=0),
    )


def _whole(shape):
    return pl.BlockSpec(shape, lambda *_: (0,) * len(shape))


class Sizes:
    def __init__(self, n_dp, nb, ten_dev, rank, cols, width):
        self.n_dp, self.nb, self.ten_dev = n_dp, nb, ten_dev
        self.rank, self.cols, self.width = rank, cols, width
        self.n_far = n_dp // NEAR
        self.rows = nb * TENANT_BLOCK
        self.me, self.core, self.quarter = 6 * nb, 6 * nb + 1, 6 * nb + 2
        self.valid = 6 * nb + 3

    def slot(self, info, which, b):
        return info[which * self.nb + b]

    def owner_and_order(self, info, which):
        owners = [self.slot(info, which, b) // self.ten_dev for b in range(self.nb)]
        orders = []
        for b in range(self.nb):
            n = jnp.int32(0)
            for c in range(b):
                n = n + jnp.where(owners[c] == owners[b], 1, 0)
            orders.append(n)
        return owners, orders

    def places(self, info):
        owners, orders = self.owner_and_order(info, 0)
        out = []
        for o, r in zip(owners, orders):
            rel = o ^ info[self.me]
            out.append(((rel % NEAR) * self.n_far + rel // NEAR) * CAP + r)
        return out


def _masked(x, valid):
    row = lax.broadcasted_iota(i32, x.shape, 0)
    return jnp.where(row < valid, x, jnp.zeros((), x.dtype))


def back_kernel(z, info, g_ref, *refs):
    packets, (up_ref, part_ref) = refs[:NEAR], refs[NEAR:]
    t = TENANT_BLOCK
    for b in range(z.nb):
        s = z.slot(info, 0, b)
        rel = (s // z.ten_dev) ^ info[z.me]
        at = pl.multiple_of(((rel // NEAR) * z.ten_dev + s % z.ten_dev) * z.rank, z.rank)
        near = rel % NEAR
        u = packets[0][pl.ds(at, z.rank), :]
        for k in range(1, NEAR):
            u = jnp.where(near == k, packets[k][pl.ds(at, z.rank), :], u)
        up_ref[b * z.rank : (b + 1) * z.rank, :] = u
        g = _masked(g_ref[b * t : (b + 1) * t, :], info[z.valid + b])
        part_ref[:, b * t : (b + 1) * t] = _dot(u, g, NT)


def pack_kernel(z, n_out, info, mine_ref, other_ref, right_ref, *refs):
    outs, packed = refs[:n_out], refs[n_out]
    t = TENANT_BLOCK

    @pl.when(pl.program_id(0) == 0)
    def _():
        packed[...] = jnp.zeros_like(packed)
        for b, place in enumerate(z.places(info)):
            cut = slice(b * t, (b + 1) * t)
            v = (mine_ref[:, cut] + other_ref[:, cut]) * adapter_scale
            packed[pl.ds(pl.multiple_of(place * z.rank, z.rank), z.rank), cut] = v.astype(bf16)

    res = jnp.dot(packed[...], right_ref[...], preferred_element_type=f32).astype(bf16)
    each = res.shape[0] // n_out
    for k in range(n_out):
        outs[k][...] = res[k * each : (k + 1) * each]


def pack_up_kernel(z, n_out, info, mine_ref, other_ref, g_ref, *refs):
    outs, packed, g = refs[:n_out], refs[n_out], refs[n_out + 1]
    t = TENANT_BLOCK
    packed[...] = jnp.zeros_like(packed)
    for b, place in enumerate(z.places(info)):
        cut = slice(b * t, (b + 1) * t)
        v = mine_ref[:, cut] + other_ref[:, cut]
        packed[pl.ds(pl.multiple_of(place * z.rank, z.rank), z.rank), cut] = v.astype(bf16)
        g[cut, :] = _masked(g_ref[cut, :], info[z.valid + b])
    res = adapter_scale * jnp.dot(packed[...], g[...], preferred_element_type=f32)
    each = res.shape[0] // n_out
    for k in range(n_out):
        outs[k][...] = res[k * each : (k + 1) * each].astype(bf16)


def dense_kernel(z, info, *refs):
    got, near_ref, far_refs = refs[:NEAR], refs[NEAR], refs[NEAR + 1 :]
    n = CAP * z.rank
    shape = (z.ten_dev * z.rank, n)
    row = lax.broadcasted_iota(i32, shape, 0)
    col = lax.broadcasted_iota(i32, shape, 1)
    same = (row % z.rank) == (col % z.rank)
    tables = [z.owner_and_order(info, k) for k in range(NEAR)]
    for j in range(z.n_far):
        holder = info[z.me] ^ (NEAR * j)
        total = None
        for k in range(NEAR):
            owners, orders = tables[k]
            local = []
            for r in range(CAP):
                found = jnp.int32(0)
                for b in range(z.nb):
                    hit = (owners[b] == holder) & (orders[b] == r)
                    found = jnp.where(hit, z.slot(info, k, b) % z.ten_dev, found)
                local.append(found)
            wanted = jnp.where(col < z.rank, local[0], local[1])
            one_hot = jnp.where(same & (row // z.rank == wanted), 1.0, 0.0).astype(bf16)
            term = jnp.dot(
                one_hot, got[k][j * n : (j + 1) * n, :], preferred_element_type=f32
            )
            total = term if total is None else total + term
        if j == 0:
            near_ref[...] = total
        else:
            far_refs[j - 1][...] = total.astype(bf16)


def final_kernel(near_ref, *refs):
    total = near_ref[...]
    for r in refs[:-1]:
        total = total + r[...].astype(f32)
    refs[-1][...] = total


def choose_kernel(z, info, pair_ref, far_ref, *outs):
    half = pair_ref.shape[0]
    for which, out in zip((0, 1, 4, 5), outs):
        for b in range(z.nb):
            s = z.slot(info, which, b)
            rel = (s // z.ten_dev) ^ info[z.me]
            line = rel // 2
            at = ((line // 2) * 2 + rel % 2) * z.ten_dev + s % z.ten_dev
            out[b] = jnp.where(line % 2 == 1, far_ref[at % half], pair_ref[at % half])


def other_kernel(info, x_ref, w_ref, out_ref, acc):
    k = pl.program_id(0)

    @pl.when(k == 0)
    def _():
        acc[...] = jnp.zeros_like(acc)

    acc[...] += jnp.dot(x_ref[...], w_ref[...], preferred_element_type=f32)

    @pl.when(k == pl.num_programs(0) - 1)
    def _():
        out_ref[...] = acc[...].astype(bf16)


def shrink_kernel(z, info, x_ref, d_ref, out_ref):
    k = pl.program_id(0)
    t = TENANT_BLOCK
    for b in range(z.nb):
        cut = slice(b * t, (b + 1) * t)
        v = _dot(d_ref[0, b], x_ref[cut, :], NT)

        @pl.when(k == 0)
        def _():
            out_ref[:, cut] = v

        @pl.when(k > 0)
        def _():
            out_ref[:, cut] += v


def projected_kernel(z, info, x_ref, w_ref, base_ref, mine_ref, other_ref, up_ref, out_ref, acc):
    k = pl.program_id(0)
    t = TENANT_BLOCK

    @pl.when(k == 0)
    def _():
        acc[...] = base_ref[...].astype(f32)

    acc[...] += jnp.dot(x_ref[...], w_ref[...], preferred_element_type=f32)

    @pl.when(k == pl.num_programs(0) - 1)
    def _():
        for b in range(z.nb):
            cut = slice(b * t, (b + 1) * t)
            s = (mine_ref[:, cut] + other_ref[:, cut]).astype(bf16)
            wide = _dot(s, up_ref[b * z.rank : (b + 1) * z.rank, :], TN)
            full = acc[cut, :] + adapter_scale * wide
            out_ref[cut, :] = _masked(full, info[z.valid + b]).astype(bf16)


def tokens_kernel(z, info, g_ref, h_ref, w_ref, mine_ref, other_ref, d_ref, out_ref, g_full, back):
    t = TENANT_BLOCK

    @pl.when(pl.program_id(0) == 0)
    def _():
        own = pl.ds(pl.multiple_of(info[z.core] * z.cols, z.cols), z.cols)
        far = pl.ds(pl.multiple_of((1 - info[z.core]) * z.cols, z.cols), z.cols)
        for b in range(z.nb):
            cut = slice(b * t, (b + 1) * t)
            g_full[cut, own] = _masked(g_ref[cut, :], info[z.valid + b])
            g_full[cut, far] = _masked(h_ref[cut, :], info[z.valid + b])
        back[...] = ((mine_ref[...] + other_ref[...]) * adapter_scale).astype(bf16)

    through = _dot(g_full[...], w_ref[...], NT)
    for b in range(z.nb):
        cut = slice(b * t, (b + 1) * t)
        out_ref[cut, :] = (through[cut] + _dot(back[:, cut], d_ref[0, b], TN)).astype(bf16)


def on_device(
    n_groups,
    n_dp,
    tokens,
    base_weight,
    adapter_down,
    adapter_up,
    out_cotangent,
    block_tenant,
    block_valid,
    tenant_slot,
):
    nb = block_tenant.shape[0]
    rows, width = tokens.shape
    cols = out_cotangent.shape[1]
    tenants = tenant_slot.shape[0]
    ten_dev, _, rank = adapter_down.shape
    z = Sizes(n_dp, nb, ten_dev, rank, cols, width)
    n_far = z.n_far
    me = lax.axis_index("dp")
    core = lax.axis_index("tensor")
    group = lax.axis_index("groups")
    shared = n_groups == 2 and n_dp == 8
    n_quarters = 4 if shared else 1
    mine_q = group * 2 + me % 2 if shared else jnp.int32(0)

    far_up = [_xor(adapter_up, n_dp, NEAR * j) for j in range(1, n_far)]
    cotangent_other = _swap(out_cotangent, "tensor")

    tenant_match = block_tenant[:, None] == jnp.arange(tenants, dtype=i32)[None, :]
    slots = jnp.sum(jnp.where(tenant_match, tenant_slot[None, :], 0), axis=1).astype(i32)
    slots_x = _swap(slots, "groups") if shared else slots

    down_t = jnp.swapaxes(adapter_down, 1, 2)
    if shared:
        quarter = width // 4
        own = lax.dynamic_slice_in_dim(down_t, mine_q * quarter, quarter, axis=2)
        to_y = lax.dynamic_slice_in_dim(down_t, (mine_q ^ 1) * quarter, quarter, axis=2)
        shard = jnp.concatenate([own, _xor(to_y, n_dp, 1)], axis=0)
        pair = jnp.concatenate([shard, _xor(shard, n_dp, 4)], axis=0)

    tag = jnp.zeros((16, cols), bf16)
    tag = tag.at[0, :nb].set(slots.astype(bf16)).at[1, :nb].set(slots_x.astype(bf16))
    ups = [u.reshape(ten_dev * rank, cols) for u in [adapter_up] + far_up]
    packet = jnp.concatenate(ups + [tag], axis=0)
    packets = [packet] + [_xor(packet, n_dp, k) for k in range(1, NEAR)]
    tags = [p[-16:-14, :nb].astype(i32) for p in packets]
    info = jnp.concatenate(
        [tags[k][0] for k in range(NEAR)]
        + [tags[0][1], tags[1][1], jnp.stack([me, core, mine_q]), block_valid]
    ).astype(i32)

    part_width = width // n_quarters
    part = (rank, rows)
    block_up, back_part = _call(
        functools.partial(back_kernel, z), 1, (1,),
        [_whole((rows, cols))] + [_whole(packet.shape)] * NEAR,
        [_whole((nb * rank, cols)), _whole(part)],
        [jax.ShapeDtypeStruct((nb * rank, cols), bf16), jax.ShapeDtypeStruct(part, f32)],
        [], 2 * rows * cols * rank * 8, 2 * rows * cols,
    )(info, out_cotangent, *packets)
    back_other = _swap(back_part, "tensor")

    packed_rows = n_dp * CAP * rank
    near_rows = packed_rows // NEAR
    tile = min(1024, part_width)
    sends = _call(
        functools.partial(pack_kernel, z, NEAR), 1, (width // tile,),
        [_whole(part), _whole(part), pl.BlockSpec((rows, tile), lambda i, *_: (0, i))],
        [pl.BlockSpec((near_rows, tile), lambda i, *_: (0, i))] * NEAR,
        [jax.ShapeDtypeStruct((near_rows, width), bf16)] * NEAR,
        [pltpu.VMEM((packed_rows, rows), bf16)],
        2 * packed_rows * rows * width, 2 * rows * width + 2 * packed_rows * width,
    )(info, back_part, back_other, tokens)

    def collect(sends):
        wide = sends[0].shape[1]
        cut = min(wide, tile)
        got = [sends[0]] + [_xor(sends[k], n_dp, k) for k in range(1, NEAR)]
        spec = pl.BlockSpec((ten_dev * rank, cut), lambda i, *_: (0, i))
        dense = _call(
            functools.partial(dense_kernel, z), 1, (wide // cut,),
            [pl.BlockSpec((near_rows, cut), lambda i, *_: (0, i))] * NEAR,
            [spec] * n_far,
            [jax.ShapeDtypeStruct((ten_dev * rank, wide), f32)]
            + [jax.ShapeDtypeStruct((ten_dev * rank, wide), bf16)] * (n_far - 1),
            [], 2 * packed_rows * ten_dev * rank * wide, 2 * packed_rows * wide,
        )(info, *got)
        far = [_xor(dense[j], n_dp, NEAR * j) for j in range(1, n_far)]
        spec = pl.BlockSpec((ten_dev * rank, cut), lambda i: (0, i))
        total = _call(
            final_kernel, 0, (wide // cut,), [spec] * n_far, spec,
            jax.ShapeDtypeStruct((ten_dev * rank, wide), f32),
            [], ten_dev * rank * wide, 10 * ten_dev * rank * wide,
        )(dense[0], *far)
        return total.reshape(ten_dev, rank, wide)

    grad_down = jnp.swapaxes(collect(sends), 1, 2)

    deep = min(1024, width)
    base_other = _call(
        other_kernel, 1, (width // deep,),
        [
            pl.BlockSpec((rows, deep), lambda k, s: (0, k)),
            pl.BlockSpec((deep, cols), lambda k, s: (k, 1 - s[0])),
        ],
        _whole((rows, cols)), jax.ShapeDtypeStruct((rows, cols), bf16),
        [pltpu.VMEM((rows, cols), f32)],
        2 * rows * cols * width, 2 * rows * width + 2 * cols * width,
    )(jnp.full((1,), core, i32), tokens, base_weight)
    base_arrived = _swap(base_other, "tensor")

    if shared:
        every = _xor(pair, n_dp, 2)
        block = (nb, rank, quarter)
        chosen = _call(
            functools.partial(choose_kernel, z), 1, (1,),
            [_whole(pair.shape)] * 2, [_whole(block)] * 4,
            [jax.ShapeDtypeStruct(block, bf16)] * 4,
            [], 0, 6 * pair.size,
        )(info, pair, every)
        got = [
            chosen[0],
            _xor(chosen[1], n_dp, 1),
            _swap(chosen[2], "groups"),
            lax.ppermute(
                chosen[3],
                ("groups", "dp"),
                [(g * n_dp + d, (1 - g) * n_dp + (d ^ 1)) for g in range(2) for d in range(n_dp)],
            ),
        ]
        block_down = jnp.stack(got)
    else:
        every = lax.all_gather(down_t, "dp", axis=0, tiled=True)
        block_down = jnp.take(every, slots, axis=0)[None]

    def down_spec(cut):
        per = part_width // cut
        return pl.BlockSpec(
            (1, nb, rank, cut), lambda i, s: ((i // per) ^ s[z.quarter], 0, 0, i % per)
        )

    cut = min(1024, part_width)
    shrink_part = _call(
        functools.partial(shrink_kernel, z), 1, (width // cut,),
        [pl.BlockSpec((rows, cut), lambda i, s: (0, i)), down_spec(cut)],
        _whole(part), jax.ShapeDtypeStruct(part, f32),
        [], 2 * rows * width * 128, 2 * rows * width,
    )(info, tokens, block_down)
    shrink_other = _swap(shrink_part, "tensor")

    up_sends = _call(
        functools.partial(pack_up_kernel, z, NEAR), 1, (1,),
        [_whole(part), _whole(part), _whole((rows, cols))],
        [_whole((near_rows, cols))] * NEAR,
        [jax.ShapeDtypeStruct((near_rows, cols), bf16)] * NEAR,
        [pltpu.VMEM((packed_rows, rows), bf16), pltpu.VMEM((rows, cols), bf16)],
        2 * packed_rows * rows * cols, 2 * rows * cols + 2 * packed_rows * cols,
    )(info, shrink_part, shrink_other, out_cotangent)
    grad_up = collect(up_sends)

    projected = _call(
        functools.partial(projected_kernel, z), 1, (width // deep,),
        [
            pl.BlockSpec((rows, deep), lambda k, s: (0, k)),
            pl.BlockSpec((deep, cols), lambda k, s: (k, s[z.core])),
            _whole((rows, cols)), _whole(part), _whole(part), _whole((nb * rank, cols)),
        ],
        _whole((rows, cols)), jax.ShapeDtypeStruct((rows, cols), bf16),
        [pltpu.VMEM((rows, cols), f32)],
        2 * rows * cols * width, 2 * rows * width + 2 * cols * width,
    )(info, tokens, base_weight, base_arrived, shrink_part, shrink_other, block_up)

    cut = min(512, part_width)
    grad_tokens = _call(
        functools.partial(tokens_kernel, z), 1, (width // cut,),
        [
            _whole((rows, cols)), _whole((rows, cols)),
            pl.BlockSpec((cut, 2 * cols), lambda i, s: (i, 0)),
            _whole(part), _whole(part), down_spec(cut),
        ],
        pl.BlockSpec((rows, cut), lambda i, s: (0, i)),
        jax.ShapeDtypeStruct((rows, width), bf16),
        [pltpu.VMEM((rows, 2 * cols), bf16), pltpu.VMEM(part, bf16)],
        4 * rows * cols * width, 2 * rows * width + 4 * cols * width,
    )(info, out_cotangent, cotangent_other, base_weight, back_part, back_other, block_down)
    return projected, grad_tokens, grad_down, grad_up


def solution(mesh):
    n_groups, n_dp = mesh.shape["groups"], mesh.shape["dp"]
    in_specs = (
        P(("groups", "dp"), "tensor"),
        P("tensor", None),
        P("dp", "tensor", None),
        P("dp", None, "tensor"),
        P(("groups", "dp"), "tensor"),
        P(("groups", "dp")),
        P(("groups", "dp")),
        P("groups"),
    )
    out_specs = (
        P(("groups", "dp"), "tensor"),
        P(("groups", "dp"), "tensor"),
        P(("groups", "dp"), "tensor", None),
        P(("groups", "dp"), None, "tensor"),
    )

    def run(*args):
        return on_device(n_groups, n_dp, *args)

    return jax.shard_map(
        run, mesh=mesh, in_specs=in_specs, out_specs=out_specs, check_vma=False
    )
```

```python
import functools

import jax
import jax.numpy as jnp
from jax import lax
from jax.experimental import pallas as pl
from jax.experimental.pallas import tpu as pltpu
from jax.sharding import PartitionSpec as P

TENANT_BLOCK = 128
CAP = 2
NEAR = 4
VMEM_LIMIT = 24 * 1024 * 1024

adapter_scale = 2.0
f32 = jnp.float32
bf16 = jnp.bfloat16
i32 = jnp.int32

NT = (((1,), (1,)), ((), ()))
TN = (((0,), (0,)), ((), ()))
NN = (((1,), (0,)), ((), ()))


def _dot(a, b, dims):
    return lax.dot_general(a, b, dims, preferred_element_type=f32)


def _swap(x, axis):
    return lax.ppermute(x, axis, [(0, 1), (1, 0)])


def _xor(x, n, k):
    return lax.ppermute(x, "dp", [(i, i ^ k) for i in range(n)])


def _tie(x, *after):
    return lax.optimization_barrier((x,) + after)[0]


def _div(a, n):
    return a >> (n.bit_length() - 1) if n & (n - 1) == 0 else lax.div(a, jnp.int32(n))


def _rem(a, n):
    return a & (n - 1) if n & (n - 1) == 0 else lax.rem(a, jnp.int32(n))


VMEM = pl.BlockSpec(memory_space=pltpu.VMEM)


def _shape(shape, dtype):
    return jax.ShapeDtypeStruct(shape, dtype)


def _call(body, name, grid, in_specs, out_specs, out_shape, scratch, flops, moved, aliases=None):
    return pl.pallas_call(
        body,
        name=name,
        grid_spec=pltpu.PrefetchScalarGridSpec(
            num_scalar_prefetch=1,
            grid=grid,
            in_specs=in_specs,
            out_specs=out_specs,
            scratch_shapes=scratch,
        ),
        out_shape=out_shape,
        input_output_aliases=aliases or {},
        compiler_params=pltpu.CompilerParams(vmem_limit_bytes=VMEM_LIMIT),
        cost_estimate=pl.CostEstimate(flops=flops, bytes_accessed=moved, transcendentals=0),
    )


def _whole(shape):
    return pl.BlockSpec(shape, lambda *_: (0,) * len(shape))


class Sizes:
    def __init__(self, n_dp, nb, ten_dev, rank, cols, width):
        self.n_dp, self.nb, self.ten_dev = n_dp, nb, ten_dev
        self.rank, self.cols, self.width = rank, cols, width
        self.n_far = n_dp // NEAR
        self.rows = nb * TENANT_BLOCK
        self.me, self.core, self.quarter = 6 * nb, 6 * nb + 1, 6 * nb + 2
        self.valid = 6 * nb + 3

    def block(self, b):
        return slice(b * TENANT_BLOCK, (b + 1) * TENANT_BLOCK)

    def ranks(self, b):
        return slice(b * self.rank, (b + 1) * self.rank)

    def slot(self, info, which, b):
        return info[which * self.nb + b]

    def owner_and_order(self, info, which):
        owners = [_div(self.slot(info, which, b), self.ten_dev) for b in range(self.nb)]
        orders = []
        for b in range(self.nb):
            n = jnp.int32(0)
            for c in range(b):
                n = n + jnp.where(owners[c] == owners[b], 1, 0)
            orders.append(n)
        return owners, orders

    def places(self, info):
        owners, orders = self.owner_and_order(info, 0)
        out = []
        for o, r in zip(owners, orders):
            rel = o ^ info[self.me]
            place = (_rem(rel, NEAR) * self.n_far + _div(rel, NEAR)) * CAP + r
            out.append(pl.ds(pl.multiple_of(place * self.rank, self.rank), self.rank))
        return out


def _masked(x, valid):
    row = lax.broadcasted_iota(i32, x.shape, 0)
    return jnp.where(row < valid, x, jnp.zeros((), x.dtype))


def other_kernel(z, me, x_ref, w_ref, out_ref):
    far = pl.ds(pl.multiple_of((1 - me[0]) * z.cols, z.cols), z.cols)
    out_ref[...] = _dot(x_ref[...], w_ref[:, far], NN).astype(bf16)


def own_kernel(z, info, x_ref, w_ref, g_ref, h_ref, out_ref, full_ref):
    own = pl.ds(pl.multiple_of(info[z.core] * z.cols, z.cols), z.cols)
    far = pl.ds(pl.multiple_of((1 - info[z.core]) * z.cols, z.cols), z.cols)
    out_ref[...] = _dot(x_ref[...], w_ref[:, own], NN)
    for b in range(z.nb):
        cut = z.block(b)
        full_ref[cut, own] = _masked(g_ref[cut, :], info[z.valid + b])
        full_ref[cut, far] = _masked(h_ref[cut, :], info[z.valid + b])


def back_kernel(z, info, g_ref, *refs):
    packets, (up_ref, part_ref) = refs[:NEAR], refs[NEAR:]
    for b in range(z.nb):
        s = z.slot(info, 0, b)
        rel = _div(s, z.ten_dev) ^ info[z.me]
        at = _div(rel, NEAR) * z.ten_dev + _rem(s, z.ten_dev)
        at = pl.ds(pl.multiple_of(at * z.rank, z.rank), z.rank)
        near = _rem(rel, NEAR)
        u = packets[0][at, :]
        for k in range(1, NEAR):
            u = jnp.where(near == k, packets[k][at, :], u)
        up_ref[z.ranks(b), :] = u
        g = _masked(g_ref[z.block(b), :], info[z.valid + b])
        part_ref[:, z.block(b)] = _dot(u, g, NT)


def pack_kernel(z, n_out, start, info, mine_ref, other_ref, x_ref, *refs):
    outs, packed = refs[:n_out], refs[n_out]
    packed[...] = jnp.zeros_like(packed)
    for b, place in enumerate(z.places(info)):
        cut = z.block(b)
        v = (mine_ref[:, cut] + other_ref[:, cut]) * adapter_scale
        packed[place, cut] = v.astype(bf16)
    wide = outs[0].shape[1]
    res = _dot(packed[...], x_ref[:, start : start + wide], NN).astype(bf16)
    each = res.shape[0] // n_out
    for k in range(n_out):
        outs[k][...] = res[k * each : (k + 1) * each]


def pack_up_kernel(z, n_out, info, mine_ref, other_ref, g_ref, *refs):
    outs, packed = refs[:n_out], refs[n_out]
    own = pl.ds(pl.multiple_of(info[z.core] * z.cols, z.cols), z.cols)
    packed[...] = jnp.zeros_like(packed)
    for b, place in enumerate(z.places(info)):
        cut = z.block(b)
        packed[place, cut] = (mine_ref[:, cut] + other_ref[:, cut]).astype(bf16)
    res = (adapter_scale * _dot(packed[...], g_ref[:, own], NN)).astype(bf16)
    each = res.shape[0] // n_out
    for k in range(n_out):
        outs[k][...] = res[k * each : (k + 1) * each]


def dense_kernel(z, info, *refs):
    got, near_ref, far_refs = refs[:NEAR], refs[NEAR], refs[NEAR + 1 :]
    n = CAP * z.rank
    shape = (z.ten_dev * z.rank, n)
    row = lax.broadcasted_iota(i32, shape, 0)
    col = lax.broadcasted_iota(i32, shape, 1)
    same = _rem(row, z.rank) == _rem(col, z.rank)
    row_slot = _div(row, z.rank)
    tables = [z.owner_and_order(info, k) for k in range(NEAR)]
    for j in range(z.n_far):
        holder = info[z.me] ^ (NEAR * j)
        total = None
        for k in range(NEAR):
            owners, orders = tables[k]
            local = []
            for r in range(CAP):
                found = jnp.int32(0)
                for b in range(z.nb):
                    hit = (owners[b] == holder) & (orders[b] == r)
                    found = jnp.where(hit, _rem(z.slot(info, k, b), z.ten_dev), found)
                local.append(found)
            wanted = jnp.where(col < z.rank, local[0], local[1])
            one_hot = jnp.where(same & (row_slot == wanted), 1.0, 0.0).astype(bf16)
            term = _dot(one_hot, got[k][j * n : (j + 1) * n, :], NN)
            total = term if total is None else total + term
        if j == 0:
            near_ref[...] = total
        else:
            far_refs[j - 1][...] = total.astype(bf16)


def final_kernel(n_parts, n_far, info, *refs):
    out = refs[-1]
    at = 0
    for p in range(n_parts):
        near, far = refs[p * n_far], refs[p * n_far + 1 : (p + 1) * n_far]
        total = near[...]
        for r in far:
            total = total + r[...].astype(f32)
        out[:, at : at + total.shape[1]] = total
        at += total.shape[1]


def choose_kernel(z, info, own_ref, near_ref, far_ref, farther_ref, *outs):
    sources = (own_ref, near_ref, far_ref, farther_ref)
    for which, out in zip((0, 1, 4, 5), outs):
        for b in range(z.nb):
            s = z.slot(info, which, b)
            rel = _div(s, z.ten_dev) ^ info[z.me]
            at = _rem(rel, 2) * z.ten_dev + _rem(s, z.ten_dev)
            line = _div(rel, 2)
            v = sources[0][at]
            for k in range(1, 4):
                v = jnp.where(line == k, sources[k][at], v)
            out[z.ranks(b), :] = v


def shrink_kernel(z, n_parts, info, x_ref, *refs):
    parts, (full_ref, out_ref) = refs[:n_parts], refs[n_parts:]
    wide = z.width // n_parts
    total = None
    for j in range(n_parts):
        if n_parts == 1:
            cut = slice(0, wide)
        else:
            cut = pl.ds(pl.multiple_of((info[z.quarter] ^ j) * wide, wide), wide)
        full_ref[:, cut] = parts[j][...]
        term = _dot(x_ref[:, cut], parts[j][...], NT)
        total = term if total is None else total + term
    for b in range(z.nb):
        out_ref[:, z.block(b)] = total[z.block(b), :].T[z.ranks(b), :]


def projected_kernel(z, info, base_ref, far_ref, mine_ref, other_ref, up_ref, out_ref, spread):
    spread[...] = jnp.zeros_like(spread)
    for b in range(z.nb):
        cut = z.block(b)
        spread[z.ranks(b), cut] = (mine_ref[:, cut] + other_ref[:, cut]).astype(bf16)
    wide = _dot(spread[...], up_ref[...], TN)
    for b in range(z.nb):
        cut = z.block(b)
        full = base_ref[cut, :] + far_ref[cut, :].astype(f32) + adapter_scale * wide[cut]
        out_ref[cut, :] = _masked(full, info[z.valid + b]).astype(bf16)


def tokens_kernel(z, first, info, g_ref, w_ref, mine_ref, other_ref, d_ref, *refs):
    out_ref, spread = refs[-2:]
    step = pl.program_id(0)

    @pl.when(step == 0)
    def _():
        spread[...] = jnp.zeros_like(spread)
        for b in range(z.nb):
            cut = z.block(b)
            v = (mine_ref[:, cut] + other_ref[:, cut]) * adapter_scale
            spread[z.ranks(b), cut] = v.astype(bf16)

    wide = out_ref.shape[1]
    cut = pl.ds(pl.multiple_of((first + step) * wide, wide), wide)
    through = _dot(g_ref[...], w_ref[cut, :], NT)
    out_ref[...] = (through + _dot(spread[...], d_ref[:, cut], TN)).astype(bf16)


def on_device(
    n_groups,
    n_dp,
    tokens,
    base_weight,
    adapter_down,
    adapter_up,
    out_cotangent,
    block_tenant,
    block_valid,
    tenant_slot,
):
    nb = block_tenant.shape[0]
    rows, width = tokens.shape
    cols = out_cotangent.shape[1]
    tenants = tenant_slot.shape[0]
    ten_dev, _, rank = adapter_down.shape
    z = Sizes(n_dp, nb, ten_dev, rank, cols, width)
    n_far = z.n_far
    me = lax.axis_index("dp")
    core = lax.axis_index("tensor")
    group = lax.axis_index("groups")
    shared = n_groups == 2 and n_dp == 8
    n_parts = 4 if shared else 1
    mine_q = group * 2 + me % 2 if shared else jnp.int32(0)
    quarter = width // n_parts

    far_up = [_xor(adapter_up, n_dp, NEAR * j) for j in range(1, n_far)]
    down_t = jnp.swapaxes(adapter_down, 1, 2)
    if shared:
        to_y = lax.dynamic_slice_in_dim(down_t, (mine_q ^ 1) * quarter, quarter, axis=2)
        from_y = _xor(to_y, n_dp, 1)
    tenant_match = block_tenant[:, None] == jnp.arange(tenants, dtype=i32)[None, :]
    slots = jnp.sum(jnp.where(tenant_match, tenant_slot[None, :], 0), axis=1).astype(i32)
    slots_x = _swap(slots, "groups") if shared else slots
    cotangent_other = _swap(out_cotangent, "tensor")

    tag = jnp.zeros((16, cols), bf16)
    tag = tag.at[0, :nb].set(slots.astype(bf16)).at[1, :nb].set(slots_x.astype(bf16))
    ups = [u.reshape(ten_dev * rank, cols) for u in [adapter_up] + far_up]
    packet = jnp.concatenate(ups + [tag], axis=0)
    packets = [packet] + [_xor(packet, n_dp, k) for k in range(1, NEAR)]

    gate = packet
    if shared:
        own = lax.dynamic_slice_in_dim(down_t, mine_q * quarter, quarter, axis=2)
        shard = _tie(jnp.concatenate([own, from_y], axis=0), packet)
        shard_far = _xor(shard, n_dp, 4)
        shard_near = _xor(shard, n_dp, 2)
        gate = shard

    base_other = _call(
        functools.partial(other_kernel, z), "base_other", (1,),
        [VMEM, VMEM], _whole((rows, cols)), _shape((rows, cols), bf16), [],
        2 * rows * cols * width, 2 * rows * cols,
    )(_tie(jnp.full((1,), core, i32), gate), tokens, base_weight)
    base_arrived = _swap(base_other, "tensor")

    tags = [p[-16:-14, :nb].astype(i32) for p in packets]
    info = jnp.concatenate(
        [tags[k][0] for k in range(NEAR)]
        + [tags[0][1], tags[1][1], jnp.stack([me, core, mine_q]), block_valid]
    ).astype(i32)

    part = (rank, rows)
    block_up, back_part = _call(
        functools.partial(back_kernel, z), "back", (1,),
        [VMEM] * (1 + NEAR), [VMEM, _whole(part)],
        [_shape((nb * rank, cols), bf16), _shape(part, f32)], [],
        2 * rows * cols * rank * 8, 2 * rows * cols,
    )(_tie(info, base_other), out_cotangent, *packets)
    back_other = _swap(back_part, "tensor")

    packed_rows = n_dp * CAP * rank
    near_rows = packed_rows // NEAR

    def pack(info, start, wide):
        return _call(
            functools.partial(pack_kernel, z, NEAR, start), "pack_down", (1,),
            [VMEM] * 3, [_whole((near_rows, wide))] * NEAR,
            [_shape((near_rows, wide), bf16)] * NEAR,
            [pltpu.VMEM((packed_rows, rows), bf16)],
            2 * packed_rows * rows * wide, 2 * packed_rows * wide,
        )(info, back_part, back_other, tokens)

    def to_near(sends):
        return [sends[0]] + [_xor(sends[k], n_dp, k) for k in range(1, NEAR)]

    def dense(info, got):
        wide = got[0].shape[1]
        out = (ten_dev * rank, wide)
        return _call(
            functools.partial(dense_kernel, z), "dense", (1,),
            [VMEM] * NEAR, [VMEM] + [_whole(out)] * (n_far - 1),
            [_shape(out, f32)] + [_shape(out, bf16)] * (n_far - 1), [],
            2 * packed_rows * ten_dev * rank * wide, 2 * packed_rows * wide,
        )(info, *got)

    def to_far(parts):
        return [parts[0]] + [_xor(parts[j], n_dp, NEAR * j) for j in range(1, n_far)]

    def final(groups):
        wide = sum(g[0].shape[1] for g in groups)
        out = (ten_dev * rank, wide)
        total = _call(
            functools.partial(final_kernel, len(groups), n_far), "final", (1,),
            [VMEM] * (len(groups) * n_far), _whole(out), _shape(out, f32), [],
            ten_dev * rank * wide, 10 * ten_dev * rank * wide,
        )(info, *[a for g in groups for a in g])
        return total.reshape(ten_dev, rank, wide)

    half = width // 2
    sends_a = pack(info, 0, half)
    got_a = to_near(sends_a)
    sends_b = pack(_tie(info, sends_a[0]), half, half)
    got_b = to_near(sends_b)

    if shared:
        farther = _xor(_tie(shard_far, sends_b[0]), n_dp, 2)

    base_own, g_full = _call(
        functools.partial(own_kernel, z), "base_own", (1,),
        [VMEM] * 4, [VMEM, VMEM],
        [_shape((rows, cols), f32), _shape((rows, 2 * cols), bf16)], [],
        2 * rows * cols * width, 12 * rows * cols,
    )(_tie(info, sends_b[0]), tokens, base_weight, out_cotangent, cotangent_other)

    if shared:
        block = (nb * rank, quarter)
        chosen = _call(
            functools.partial(choose_kernel, z), "choose", (1,),
            [VMEM] * 4, [_whole(block)] * 4, [_shape(block, bf16)] * 4, [],
            0, 4 * shard.size,
        )(_tie(info, base_own), shard, shard_near, shard_far, farther)
        got_down = [
            chosen[0],
            _xor(chosen[1], n_dp, 1),
            _swap(chosen[2], "groups"),
            lax.ppermute(
                chosen[3],
                ("groups", "dp"),
                [(g * n_dp + d, (1 - g) * n_dp + (d ^ 1)) for g in range(2) for d in range(n_dp)],
            ),
        ]
        after_choose = chosen[0]
    else:
        every = lax.all_gather(down_t, "dp", axis=0, tiled=True)
        got_down = [jnp.take(every, slots, axis=0).reshape(nb * rank, width)]
        after_choose = base_own

    dense_a = dense(_tie(info, after_choose), got_a)
    far_a = to_far(dense_a)

    block_down, shrink_part = _call(
        functools.partial(shrink_kernel, z, n_parts), "shrink", (1,),
        [VMEM] * (1 + n_parts), [VMEM, _whole(part)],
        [_shape((nb * rank, width), bf16), _shape(part, f32)], [],
        2 * rows * width * 128, 2 * nb * rank * width,
    )(_tie(info, dense_a[1]), tokens, *got_down)
    shrink_other = _swap(shrink_part, "tensor")

    dense_b = dense(_tie(info, shrink_part), got_b)
    far_b = to_far(dense_b)

    up_sends = _call(
        functools.partial(pack_up_kernel, z, NEAR), "pack_up", (1,),
        [VMEM] * 3, [_whole((near_rows, cols))] * NEAR,
        [_shape((near_rows, cols), bf16)] * NEAR,
        [pltpu.VMEM((packed_rows, rows), bf16)],
        2 * packed_rows * rows * cols, 2 * rows * cols + 2 * packed_rows * cols,
    )(_tie(info, dense_b[1]), shrink_part, shrink_other, g_full)
    got_u = to_near(up_sends)

    step = min(1024, width // 4)
    n_steps = width // step

    def token_grads(info, first, count, so_far=None):
        return _call(
            functools.partial(tokens_kernel, z, first), "token_grads", (count,),
            [VMEM] * 5 + ([] if so_far is None else [pl.BlockSpec(memory_space=pl.ANY)]),
            pl.BlockSpec((rows, step), lambda i, *_: (0, first + i)),
            _shape((rows, width), bf16), [pltpu.VMEM((nb * rank, rows), bf16)],
            4 * rows * cols * step * count, 2 * rows * step * count,
            None if so_far is None else {6: 0},
        )(
            info, g_full, base_weight, back_part, back_other, block_down,
            *([] if so_far is None else [so_far]),
        )

    grads_1 = token_grads(_tie(info, up_sends[0]), 0, n_steps // 2)
    dense_u = dense(_tie(info, grads_1), got_u)
    far_u = to_far(dense_u)
    grad_tokens = token_grads(_tie(info, dense_u[1]), n_steps // 2, n_steps - n_steps // 2, grads_1)

    projected = _call(
        functools.partial(projected_kernel, z), "projected", (1,),
        [VMEM] * 5, _whole((rows, cols)), _shape((rows, cols), bf16),
        [pltpu.VMEM((nb * rank, rows), bf16)],
        2 * rows * cols * 128, 8 * rows * cols,
    )(_tie(info, grad_tokens), base_own, base_arrived, shrink_part, shrink_other, block_up)

    grad_up = final([far_u])
    grad_down = jnp.swapaxes(final([far_a, far_b]), 1, 2)
    return projected, grad_tokens, grad_down, grad_up


def solution(mesh):
    n_groups, n_dp = mesh.shape["groups"], mesh.shape["dp"]
    in_specs = (
        P(("groups", "dp"), "tensor"),
        P("tensor", None),
        P("dp", "tensor", None),
        P("dp", None, "tensor"),
        P(("groups", "dp"), "tensor"),
        P(("groups", "dp")),
        P(("groups", "dp")),
        P("groups"),
    )
    out_specs = (
        P(("groups", "dp"), "tensor"),
        P(("groups", "dp"), "tensor"),
        P(("groups", "dp"), "tensor", None),
        P(("groups", "dp"), None, "tensor"),
    )

    def run(*args):
        return on_device(n_groups, n_dp, *args)

    return jax.shard_map(
        run, mesh=mesh, in_specs=in_specs, out_specs=out_specs, check_vma=False
    )
```

```python
import functools

import jax
import jax.numpy as jnp
from jax import lax
from jax.experimental import pallas as pl
from jax.experimental.pallas import tpu as pltpu
from jax.sharding import PartitionSpec as P

TENANT_BLOCK = 128
CAP = 2
NEAR = 4
VMEM_LIMIT = 16 * 1024 * 1024
LANES = 128

adapter_scale = 2.0
f32 = jnp.float32
bf16 = jnp.bfloat16
i32 = jnp.int32

NT = (((1,), (1,)), ((), ()))
TN = (((0,), (0,)), ((), ()))
NN = (((1,), (0,)), ((), ()))


def _dot(a, b, dims):
    return lax.dot_general(a, b, dims, preferred_element_type=f32)


def _swap(x, axis):
    return lax.ppermute(x, axis, [(0, 1), (1, 0)])


def _xor(x, n, k):
    return lax.ppermute(x, "dp", [(i, i ^ k) for i in range(n)])


def _tie(x, *after):
    return lax.optimization_barrier((x,) + after)[0]


def _div(a, n):
    return a >> (n.bit_length() - 1) if n & (n - 1) == 0 else lax.div(a, jnp.int32(n))


def _rem(a, n):
    return a & (n - 1) if n & (n - 1) == 0 else lax.rem(a, jnp.int32(n))


VMEM = pl.BlockSpec(memory_space=pltpu.VMEM)


def _shape(shape, dtype):
    return jax.ShapeDtypeStruct(shape, dtype)


def _call(body, name, grid, in_specs, out_specs, out_shape, scratch, aliases=None):
    return pl.pallas_call(
        body,
        name=name,
        grid_spec=pltpu.PrefetchScalarGridSpec(
            num_scalar_prefetch=1,
            grid=grid,
            in_specs=in_specs,
            out_specs=out_specs,
            scratch_shapes=scratch,
        ),
        out_shape=out_shape,
        input_output_aliases=aliases or {},
        compiler_params=pltpu.CompilerParams(vmem_limit_bytes=VMEM_LIMIT),
        cost_estimate=pl.CostEstimate(flops=1, bytes_accessed=1, transcendentals=0),
    )


def _whole(shape):
    return pl.BlockSpec(shape, lambda *_: (0,) * len(shape))


class Sizes:
    def __init__(self, n_dp, nb, ten_dev, rank, cols, width):
        self.n_dp, self.nb, self.ten_dev = n_dp, nb, ten_dev
        self.rank, self.cols, self.width = rank, cols, width
        self.n_far = n_dp // NEAR
        self.rows = nb * TENANT_BLOCK
        self.me, self.core, self.quarter = (6, 0), (6, 1), (6, 2)

    def block(self, b):
        return slice(b * TENANT_BLOCK, (b + 1) * TENANT_BLOCK)

    def ranks(self, b):
        return slice(b * self.rank, (b + 1) * self.rank)

    def slot(self, info, which, b):
        return info[which, b]

    def valid(self, info, b):
        return info[7, b]

    def owner_and_order(self, info, which):
        owners = [_div(self.slot(info, which, b), self.ten_dev) for b in range(self.nb)]
        orders = []
        for b in range(self.nb):
            n = jnp.int32(0)
            for c in range(b):
                n = n + jnp.where(owners[c] == owners[b], 1, 0)
            orders.append(n)
        return owners, orders

    def places(self, info):
        owners, orders = self.owner_and_order(info, 0)
        out = []
        for o, r in zip(owners, orders):
            rel = o ^ info[self.me]
            place = (_rem(rel, NEAR) * self.n_far + _div(rel, NEAR)) * CAP + r
            out.append(pl.ds(pl.multiple_of(place * self.rank, self.rank), self.rank))
        return out


def _masked(x, valid):
    row = lax.broadcasted_iota(i32, x.shape, 0)
    return jnp.where(row < valid, x, jnp.zeros((), x.dtype))


def other_kernel(z, place, x_ref, w_ref, out_ref):
    far = pl.ds(pl.multiple_of((1 - place[z.core[1]]) * z.cols, z.cols), z.cols)
    out_ref[...] = _dot(x_ref[...], w_ref[:, far], NN).astype(bf16)


def own_kernel(z, info, x_ref, w_ref, far_ref, g_ref, h_ref, out_ref, full_ref):
    own = pl.ds(pl.multiple_of(info[z.core] * z.cols, z.cols), z.cols)
    far = pl.ds(pl.multiple_of((1 - info[z.core]) * z.cols, z.cols), z.cols)
    out_ref[...] = _dot(x_ref[...], w_ref[:, own], NN) + far_ref[...].astype(f32)
    for b in range(z.nb):
        cut = z.block(b)
        full_ref[cut, own] = _masked(g_ref[cut, :], z.valid(info, b))
        full_ref[cut, far] = _masked(h_ref[cut, :], z.valid(info, b))


def back_kernel(z, info, g_ref, *refs):
    packets, (up_ref, part_ref) = refs[:NEAR], refs[NEAR:]
    for b in range(z.nb):
        s = z.slot(info, 0, b)
        rel = _div(s, z.ten_dev) ^ info[z.me]
        at = _div(rel, NEAR) * z.ten_dev + _rem(s, z.ten_dev)
        at = pl.ds(pl.multiple_of(at * z.rank, z.rank), z.rank)
        near = _rem(rel, NEAR)
        u = packets[0][at, :]
        for k in range(1, NEAR):
            u = jnp.where(near == k, packets[k][at, :], u)
        up_ref[z.ranks(b), :] = u
        g = _masked(g_ref[z.block(b), :], z.valid(info, b))
        part_ref[:, z.block(b)] = _dot(u, g, NT)


def pack_kernel(z, n_out, start, info, mine_ref, other_ref, x_ref, *refs):
    outs, packed = refs[:n_out], refs[n_out]
    packed[...] = jnp.zeros_like(packed)
    for b, place in enumerate(z.places(info)):
        cut = z.block(b)
        v = (mine_ref[:, cut] + other_ref[:, cut]) * adapter_scale
        packed[place, cut] = v.astype(bf16)
    wide = outs[0].shape[1]
    res = _dot(packed[...], x_ref[:, start : start + wide], NN).astype(bf16)
    each = res.shape[0] // n_out
    for k in range(n_out):
        outs[k][...] = res[k * each : (k + 1) * each]


def pack_up_kernel(z, n_out, info, mine_ref, other_ref, g_ref, *refs):
    outs, packed = refs[:n_out], refs[n_out]
    own = pl.ds(pl.multiple_of(info[z.core] * z.cols, z.cols), z.cols)
    packed[...] = jnp.zeros_like(packed)
    for b, place in enumerate(z.places(info)):
        cut = z.block(b)
        packed[place, cut] = (mine_ref[:, cut] + other_ref[:, cut]).astype(bf16)
    res = (adapter_scale * _dot(packed[...], g_ref[:, own], NN)).astype(bf16)
    each = res.shape[0] // n_out
    for k in range(n_out):
        outs[k][...] = res[k * each : (k + 1) * each]


def dense_kernel(z, info, *refs):
    got, near_ref, far_refs = refs[:NEAR], refs[NEAR], refs[NEAR + 1 :]
    n = CAP * z.rank
    shape = (z.ten_dev * z.rank, n)
    row = lax.broadcasted_iota(i32, shape, 0)
    col = lax.broadcasted_iota(i32, shape, 1)
    same = _rem(row, z.rank) == _rem(col, z.rank)
    row_slot = _div(row, z.rank)
    tables = [z.owner_and_order(info, k) for k in range(NEAR)]
    for j in range(z.n_far):
        holder = info[z.me] ^ (NEAR * j)
        total = None
        for k in range(NEAR):
            owners, orders = tables[k]
            local = []
            for r in range(CAP):
                found = jnp.int32(0)
                for b in range(z.nb):
                    hit = (owners[b] == holder) & (orders[b] == r)
                    found = jnp.where(hit, _rem(z.slot(info, k, b), z.ten_dev), found)
                local.append(found)
            wanted = jnp.where(col < z.rank, local[0], local[1])
            one_hot = jnp.where(same & (row_slot == wanted), 1.0, 0.0).astype(bf16)
            term = _dot(one_hot, got[k][j * n : (j + 1) * n, :], NN)
            total = term if total is None else total + term
        if j == 0:
            near_ref[...] = total
        else:
            far_refs[j - 1][...] = total.astype(bf16)


def final_kernel(n_parts, n_far, info, *refs):
    out = refs[-1]
    at = 0
    for p in range(n_parts):
        near, far = refs[p * n_far], refs[p * n_far + 1 : (p + 1) * n_far]
        total = near[...]
        for r in far:
            total = total + r[...].astype(f32)
        out[:, at : at + total.shape[1]] = total
        at += total.shape[1]


def choose_kernel(z, info, own_ref, near_ref, far_ref, farther_ref, *outs):
    sources = (own_ref, near_ref, far_ref, farther_ref)
    for which, out in zip((0, 1, 4, 5), outs):
        for b in range(z.nb):
            s = z.slot(info, which, b)
            rel = _div(s, z.ten_dev) ^ info[z.me]
            at = _rem(rel, 2) * z.ten_dev + _rem(s, z.ten_dev)
            line = _div(rel, 2)
            v = sources[0][at]
            for k in range(1, 4):
                v = jnp.where(line == k, sources[k][at], v)
            out[z.ranks(b), :] = v


def shrink_kernel(z, n_parts, info, x_ref, *refs):
    parts, (full_ref, out_ref) = refs[:n_parts], refs[n_parts:]
    wide = z.width // n_parts
    total = None
    for j in range(n_parts):
        if n_parts == 1:
            cut = slice(0, wide)
        else:
            cut = pl.ds(pl.multiple_of((info[z.quarter] ^ j) * wide, wide), wide)
        full_ref[:, cut] = parts[j][...]
        term = _dot(x_ref[:, cut], parts[j][...], NT)
        total = term if total is None else total + term
    for b in range(z.nb):
        out_ref[:, z.block(b)] = total[z.block(b), :].T[z.ranks(b), :]


def projected_kernel(z, info, base_ref, mine_ref, other_ref, up_ref, out_ref, spread):
    spread[...] = jnp.zeros_like(spread)
    for b in range(z.nb):
        cut = z.block(b)
        spread[z.ranks(b), cut] = (mine_ref[:, cut] + other_ref[:, cut]).astype(bf16)
    wide = _dot(spread[...], up_ref[...], TN)
    for b in range(z.nb):
        cut = z.block(b)
        full = base_ref[cut, :] + adapter_scale * wide[cut]
        out_ref[cut, :] = _masked(full, z.valid(info, b)).astype(bf16)


def tokens_kernel(z, first, info, g_ref, w_ref, mine_ref, other_ref, d_ref, *refs):
    out_ref, spread = refs[-2:]
    step = pl.program_id(0)

    @pl.when(step == 0)
    def _():
        spread[...] = jnp.zeros_like(spread)
        for b in range(z.nb):
            cut = z.block(b)
            v = (mine_ref[:, cut] + other_ref[:, cut]) * adapter_scale
            spread[z.ranks(b), cut] = v.astype(bf16)

    wide = out_ref.shape[1]
    cut = pl.ds(pl.multiple_of((first + step) * wide, wide), wide)
    through = _dot(g_ref[...], w_ref[cut, :], NT)
    out_ref[...] = (through + _dot(spread[...], d_ref[:, cut], TN)).astype(bf16)


def on_device(
    n_groups,
    n_dp,
    tokens,
    base_weight,
    adapter_down,
    adapter_up,
    out_cotangent,
    block_tenant,
    block_valid,
    tenant_slot,
):
    nb = block_tenant.shape[0]
    rows, width = tokens.shape
    cols = out_cotangent.shape[1]
    tenants = tenant_slot.shape[0]
    ten_dev, _, rank = adapter_down.shape
    z = Sizes(n_dp, nb, ten_dev, rank, cols, width)
    n_far = z.n_far
    me = lax.axis_index("dp")
    core = lax.axis_index("tensor")
    group = lax.axis_index("groups")
    shared = n_groups == 2 and n_dp == 8
    n_parts = 4 if shared else 1
    mine_q = group * 2 + me % 2 if shared else jnp.int32(0)
    quarter = width // n_parts

    down_t = jnp.swapaxes(adapter_down, 1, 2)
    if shared:
        to_y = lax.dynamic_slice_in_dim(down_t, (mine_q ^ 1) * quarter, quarter, axis=2)
        from_y = _xor(to_y, n_dp, 1)
    far_up = [_xor(adapter_up, n_dp, NEAR * j) for j in range(1, n_far)]
    lanes = jnp.pad(block_tenant, (0, LANES - nb))
    tenant_match = lanes[:, None] == jnp.arange(tenants, dtype=i32)[None, :]
    slots = jnp.sum(jnp.where(tenant_match, tenant_slot[None, :], 0), axis=1).astype(i32)
    lane = jnp.arange(LANES, dtype=i32)
    place = jnp.where(lane == 0, me, jnp.where(lane == 1, core, mine_q))
    slots = _tie(slots, place)
    slots_x = _swap(slots, "groups") if shared else slots

    line = lax.broadcasted_iota(i32, (16, LANES), 0)
    tag = jnp.where(line == 0, slots[None, :], slots_x[None, :]).astype(bf16)
    tag = jnp.pad(tag, ((0, 0), (0, cols - LANES)))
    ups = [u.reshape(ten_dev * rank, cols) for u in [adapter_up] + far_up]
    packet = jnp.concatenate(ups + [tag], axis=0)
    packets = [packet] + [_xor(packet, n_dp, k) for k in range(1, NEAR)]

    if shared:
        own = lax.dynamic_slice_in_dim(down_t, mine_q * quarter, quarter, axis=2)
        shard = jnp.concatenate([own, from_y], axis=0)
        shard_far = _xor(shard, n_dp, 4)
        shard_near = _xor(shard, n_dp, 2)

    base_other = _call(
        functools.partial(other_kernel, z), "base_other", (1,),
        [VMEM, VMEM], _whole((rows, cols)), _shape((rows, cols), bf16), [],
    )(_tie(place, shard if shared else packet), tokens, base_weight)
    base_arrived = _swap(base_other, "tensor")
    packets = [_tie(p, base_other) for p in packets]

    line = lax.broadcasted_iota(i32, (8, LANES), 0)
    info = jnp.where(line == 6, place[None, :], jnp.pad(block_valid, (0, LANES - nb))[None, :])
    for k in range(NEAR):
        info = jnp.where(line == k, packets[k][-16, :LANES].astype(i32)[None, :], info)
    for k in range(2):
        info = jnp.where(line == 4 + k, packets[k][-15, :LANES].astype(i32)[None, :], info)

    if shared:
        info = _tie(info, shard_far, shard_near)
        farther = _xor(shard_far, n_dp, 2)

    part = (rank, rows)
    block_up, back_part = _call(
        functools.partial(back_kernel, z), "back", (1,),
        [VMEM] * (1 + NEAR), [VMEM, _whole(part)],
        [_shape((nb * rank, cols), bf16), _shape(part, f32)], [],
    )(info, out_cotangent, *packets)
    back_other = _swap(back_part, "tensor")
    cotangent_other = _swap(_tie(out_cotangent, back_part), "tensor")

    packed_rows = n_dp * CAP * rank
    near_rows = packed_rows // NEAR

    def pack(info, start, wide):
        return _call(
            functools.partial(pack_kernel, z, NEAR, start), "pack_down", (1,),
            [VMEM] * 3, [_whole((near_rows, wide))] * NEAR,
            [_shape((near_rows, wide), bf16)] * NEAR,
            [pltpu.VMEM((packed_rows, rows), bf16)],
        )(info, back_part, back_other, tokens)

    def to_near(sends):
        return [sends[0]] + [_xor(sends[k], n_dp, k) for k in range(1, NEAR)]

    def dense(info, got):
        wide = got[0].shape[1]
        out = (ten_dev * rank, wide)
        return _call(
            functools.partial(dense_kernel, z), "dense", (1,),
            [VMEM] * NEAR, [VMEM] + [_whole(out)] * (n_far - 1),
            [_shape(out, f32)] + [_shape(out, bf16)] * (n_far - 1), [],
        )(info, *got)

    def to_far(parts):
        return [parts[0]] + [_xor(parts[j], n_dp, NEAR * j) for j in range(1, n_far)]

    def final(groups):
        wide = sum(g[0].shape[1] for g in groups)
        out = (ten_dev * rank, wide)
        total = _call(
            functools.partial(final_kernel, len(groups), n_far), "final", (1,),
            [VMEM] * (len(groups) * n_far), _whole(out), _shape(out, f32), [],
        )(info, *[a for g in groups for a in g])
        return total.reshape(ten_dev, rank, wide)

    half = width // 2
    sends_a = pack(_tie(info, cotangent_other, base_arrived), 0, half)
    got_a = to_near(sends_a)

    if shared:
        block = (nb * rank, quarter)
        chosen = _call(
            functools.partial(choose_kernel, z), "choose", (1,),
            [VMEM] * 4, [_whole(block)] * 4, [_shape(block, bf16)] * 4, [],
        )(_tie(info, sends_a[0]), shard, shard_near, shard_far, farther)
        got_x = _swap(chosen[2], "groups")
        got_d = lax.ppermute(
            chosen[3],
            ("groups", "dp"),
            [(g * n_dp + d, (1 - g) * n_dp + (d ^ 1)) for g in range(2) for d in range(n_dp)],
        )
        after_choose = chosen[0]
    else:
        every = lax.all_gather(down_t, "dp", axis=0, tiled=True)
        got_down = [jnp.take(every, slots[:nb], axis=0).reshape(nb * rank, width)]
        after_choose = sends_a[0]

    sends_b = pack(_tie(info, after_choose), half, half)
    got_b = to_near(sends_b)

    base_own, g_full = _call(
        functools.partial(own_kernel, z), "base_own", (1,),
        [VMEM] * 5, [VMEM, VMEM],
        [_shape((rows, cols), f32), _shape((rows, 2 * cols), bf16)], [],
    )(_tie(info, sends_b[0]), tokens, base_weight, base_arrived, out_cotangent, cotangent_other)

    if shared:
        got_y = _xor(_tie(chosen[1], base_own), n_dp, 1)
        got_down = [chosen[0], got_y, got_x, got_d]
    dense_a = dense(_tie(info, base_own), got_a)
    far_a = to_far(dense_a)

    block_down, shrink_part = _call(
        functools.partial(shrink_kernel, z, n_parts), "shrink", (1,),
        [VMEM] * (1 + n_parts), [VMEM, _whole(part)],
        [_shape((nb * rank, width), bf16), _shape(part, f32)], [],
    )(_tie(info, dense_a[1]), tokens, *got_down)
    shrink_other = _swap(shrink_part, "tensor")

    step = min(512, width // 8)
    n_calls = 4
    per_call = width // step // n_calls

    def token_grads(info, call, so_far):
        first = call * per_call
        return _call(
            functools.partial(tokens_kernel, z, first), "token_grads", (per_call,),
            [VMEM] * 5 + ([] if so_far is None else [pl.BlockSpec(memory_space=pl.ANY)]),
            pl.BlockSpec((rows, step), lambda i, *_: (0, first + i)),
            _shape((rows, width), bf16), [pltpu.VMEM((nb * rank, rows), bf16)],
            None if so_far is None else {6: 0},
        )(
            info, g_full, base_weight, back_part, back_other, block_down,
            *([] if so_far is None else [so_far]),
        )

    grad_tokens = token_grads(_tie(info, shrink_part), 0, None)

    up_sends = _call(
        functools.partial(pack_up_kernel, z, NEAR), "pack_up", (1,),
        [VMEM] * 3, [_whole((near_rows, cols))] * NEAR,
        [_shape((near_rows, cols), bf16)] * NEAR,
        [pltpu.VMEM((packed_rows, rows), bf16)],
    )(_tie(info, grad_tokens), shrink_part, shrink_other, g_full)
    got_u = to_near(up_sends)

    dense_b = dense(_tie(info, up_sends[0]), got_b)
    far_b = to_far(dense_b)

    grad_tokens = token_grads(_tie(info, dense_b[1]), 1, grad_tokens)
    dense_u = dense(_tie(info, grad_tokens), got_u)
    far_u = to_far(dense_u)
    grad_tokens = token_grads(_tie(info, dense_u[1]), 2, grad_tokens)
    grad_tokens = token_grads(info, 3, grad_tokens)

    projected = _call(
        functools.partial(projected_kernel, z), "projected", (1,),
        [VMEM] * 4, _whole((rows, cols)), _shape((rows, cols), bf16),
        [pltpu.VMEM((nb * rank, rows), bf16)],
    )(_tie(info, grad_tokens), base_own, shrink_part, shrink_other, block_up)

    grad_up = final([far_u])
    grad_down = jnp.swapaxes(final([far_a, far_b]), 1, 2)
    return projected, grad_tokens, grad_down, grad_up


def solution(mesh):
    n_groups, n_dp = mesh.shape["groups"], mesh.shape["dp"]
    in_specs = (
        P(("groups", "dp"), "tensor"),
        P("tensor", None),
        P("dp", "tensor", None),
        P("dp", None, "tensor"),
        P(("groups", "dp"), "tensor"),
        P(("groups", "dp")),
        P(("groups", "dp")),
        P("groups"),
    )
    out_specs = (
        P(("groups", "dp"), "tensor"),
        P(("groups", "dp"), "tensor"),
        P(("groups", "dp"), "tensor", None),
        P(("groups", "dp"), None, "tensor"),
    )

    def run(*args):
        return on_device(n_groups, n_dp, *args)

    return jax.shard_map(
        run, mesh=mesh, in_specs=in_specs, out_specs=out_specs, check_vma=False
    )
```

```python
import functools

import jax
import jax.numpy as jnp
from jax import lax
from jax.experimental import pallas as pl
from jax.experimental.pallas import tpu as pltpu
from jax.sharding import PartitionSpec as P

TENANT_BLOCK = 128
CAP = 2
NEAR = 4
VMEM_LIMIT = 16 * 1024 * 1024
BIG_VMEM = 52 * 1024 * 1024
LANES = 128

adapter_scale = 2.0
f32 = jnp.float32
bf16 = jnp.bfloat16
i32 = jnp.int32

NT = (((1,), (1,)), ((), ()))
TN = (((0,), (0,)), ((), ()))
NN = (((1,), (0,)), ((), ()))


def _dot(a, b, dims):
    return lax.dot_general(a, b, dims, preferred_element_type=f32)


def _swap(x, axis):
    return lax.ppermute(x, axis, [(0, 1), (1, 0)])


def _xor(x, n, k):
    return lax.ppermute(x, "dp", [(i, i ^ k) for i in range(n)])


def _tie(x, *after):
    return lax.optimization_barrier((x,) + after)[0]


def _div(a, n):
    return a >> (n.bit_length() - 1) if n & (n - 1) == 0 else lax.div(a, jnp.int32(n))


def _rem(a, n):
    return a & (n - 1) if n & (n - 1) == 0 else lax.rem(a, jnp.int32(n))


VMEM = pl.BlockSpec(memory_space=pltpu.VMEM)


def _shape(shape, dtype):
    return jax.ShapeDtypeStruct(shape, dtype)


def _call(
    body, name, grid, in_specs, out_specs, out_shape, scratch, aliases=None, vmem=VMEM_LIMIT
):
    return pl.pallas_call(
        body,
        name=name,
        grid_spec=pltpu.PrefetchScalarGridSpec(
            num_scalar_prefetch=1,
            grid=grid,
            in_specs=in_specs,
            out_specs=out_specs,
            scratch_shapes=scratch,
        ),
        out_shape=out_shape,
        input_output_aliases=aliases or {},
        compiler_params=pltpu.CompilerParams(vmem_limit_bytes=vmem),
        cost_estimate=pl.CostEstimate(flops=1, bytes_accessed=1, transcendentals=0),
    )


def _whole(shape):
    return pl.BlockSpec(shape, lambda *_: (0,) * len(shape))


class Sizes:
    def __init__(self, n_dp, nb, ten_dev, rank, cols, width):
        self.n_dp, self.nb, self.ten_dev = n_dp, nb, ten_dev
        self.rank, self.cols, self.width = rank, cols, width
        self.n_far = n_dp // NEAR
        self.rows = nb * TENANT_BLOCK
        self.me, self.core, self.quarter = (6, 0), (6, 1), (6, 2)

    def block(self, b):
        return slice(b * TENANT_BLOCK, (b + 1) * TENANT_BLOCK)

    def ranks(self, b):
        return slice(b * self.rank, (b + 1) * self.rank)

    def slot(self, info, which, b):
        return info[which, b]

    def valid(self, info, b):
        return info[7, b]

    def owner_and_order(self, info, which):
        owners = [_div(self.slot(info, which, b), self.ten_dev) for b in range(self.nb)]
        orders = []
        for b in range(self.nb):
            n = jnp.int32(0)
            for c in range(b):
                n = n + jnp.where(owners[c] == owners[b], 1, 0)
            orders.append(n)
        return owners, orders

    def places(self, info):
        owners, orders = self.owner_and_order(info, 0)
        out = []
        for o, r in zip(owners, orders):
            rel = o ^ info[self.me]
            place = (_rem(rel, NEAR) * self.n_far + _div(rel, NEAR)) * CAP + r
            out.append(pl.ds(pl.multiple_of(place * self.rank, self.rank), self.rank))
        return out


def _masked(x, valid):
    row = lax.broadcasted_iota(i32, x.shape, 0)
    return jnp.where(row < valid, x, jnp.zeros((), x.dtype))


def other_kernel(z, place, x_hbm, w_hbm, out_ref, x_buf, w_buf, x_sem, w_sem):
    far = pl.ds(pl.multiple_of((1 - place[z.core[1]]) * z.cols, z.cols), z.cols)
    unit = z.width // 8
    copies = []
    for i, (first, last) in enumerate(((0, 1), (1, 2), (2, 4), (4, 6), (6, 8))):
        cut = pl.ds(first * unit, (last - first) * unit)
        x = pltpu.make_async_copy(x_hbm.at[:, cut], x_buf.at[:, cut], x_sem.at[i])
        w = pltpu.make_async_copy(w_hbm.at[cut, far], w_buf.at[cut], w_sem.at[i])
        x.start()
        w.start()
        copies.append((x, w, cut))
    total = None
    for x, w, cut in copies:
        x.wait()
        w.wait()
        term = _dot(x_buf[:, cut], w_buf[cut, :], NN)
        total = term if total is None else total + term
    out_ref[...] = total.astype(bf16)


def own_kernel(z, info, x_ref, w_ref, far_ref, g_ref, h_ref, out_ref, full_ref):
    own = pl.ds(pl.multiple_of(info[z.core] * z.cols, z.cols), z.cols)
    far = pl.ds(pl.multiple_of((1 - info[z.core]) * z.cols, z.cols), z.cols)
    out_ref[...] = _dot(x_ref[...], w_ref[:, own], NN) + far_ref[...].astype(f32)
    for b in range(z.nb):
        cut = z.block(b)
        full_ref[cut, own] = _masked(g_ref[cut, :], z.valid(info, b))
        full_ref[cut, far] = _masked(h_ref[cut, :], z.valid(info, b))


def back_kernel(z, info, g_ref, *refs):
    packets, (up_ref, part_ref) = refs[:NEAR], refs[NEAR:]
    for b in range(z.nb):
        s = z.slot(info, 0, b)
        rel = _div(s, z.ten_dev) ^ info[z.me]
        at = _div(rel, NEAR) * z.ten_dev + _rem(s, z.ten_dev)
        at = pl.ds(pl.multiple_of(at * z.rank, z.rank), z.rank)
        near = _rem(rel, NEAR)
        u = packets[0][at, :]
        for k in range(1, NEAR):
            u = jnp.where(near == k, packets[k][at, :], u)
        up_ref[z.ranks(b), :] = u
        g = _masked(g_ref[z.block(b), :], z.valid(info, b))
        part_ref[:, z.block(b)] = _dot(u, g, NT)


def pack_kernel(z, n_out, start, info, mine_ref, other_ref, x_ref, *refs):
    outs, packed = refs[:n_out], refs[n_out]
    packed[...] = jnp.zeros_like(packed)
    for b, place in enumerate(z.places(info)):
        cut = z.block(b)
        v = (mine_ref[:, cut] + other_ref[:, cut]) * adapter_scale
        packed[place, cut] = v.astype(bf16)
    wide = outs[0].shape[1]
    res = _dot(packed[...], x_ref[:, start : start + wide], NN).astype(bf16)
    each = res.shape[0] // n_out
    for k in range(n_out):
        outs[k][...] = res[k * each : (k + 1) * each]


def pack_up_kernel(z, n_out, info, mine_ref, other_ref, g_ref, *refs):
    outs, packed = refs[:n_out], refs[n_out]
    own = pl.ds(pl.multiple_of(info[z.core] * z.cols, z.cols), z.cols)
    packed[...] = jnp.zeros_like(packed)
    for b, place in enumerate(z.places(info)):
        cut = z.block(b)
        packed[place, cut] = (mine_ref[:, cut] + other_ref[:, cut]).astype(bf16)
    res = (adapter_scale * _dot(packed[...], g_ref[:, own], NN)).astype(bf16)
    each = res.shape[0] // n_out
    for k in range(n_out):
        outs[k][...] = res[k * each : (k + 1) * each]


def dense_kernel(z, info, *refs):
    got, near_ref, far_refs = refs[:NEAR], refs[NEAR], refs[NEAR + 1 :]
    n = CAP * z.rank
    shape = (z.ten_dev * z.rank, n)
    row = lax.broadcasted_iota(i32, shape, 0)
    col = lax.broadcasted_iota(i32, shape, 1)
    same = _rem(row, z.rank) == _rem(col, z.rank)
    row_slot = _div(row, z.rank)
    tables = [z.owner_and_order(info, k) for k in range(NEAR)]
    for j in range(z.n_far):
        holder = info[z.me] ^ (NEAR * j)
        total = None
        for k in range(NEAR):
            owners, orders = tables[k]
            local = []
            for r in range(CAP):
                found = jnp.int32(0)
                for b in range(z.nb):
                    hit = (owners[b] == holder) & (orders[b] == r)
                    found = jnp.where(hit, _rem(z.slot(info, k, b), z.ten_dev), found)
                local.append(found)
            wanted = jnp.where(col < z.rank, local[0], local[1])
            one_hot = jnp.where(same & (row_slot == wanted), 1.0, 0.0).astype(bf16)
            term = _dot(one_hot, got[k][j * n : (j + 1) * n, :], NN)
            total = term if total is None else total + term
        if j == 0:
            near_ref[...] = total
        else:
            far_refs[j - 1][...] = total.astype(bf16)


def final_kernel(n_parts, n_far, info, *refs):
    out = refs[-1]
    at = 0
    for p in range(n_parts):
        near, far = refs[p * n_far], refs[p * n_far + 1 : (p + 1) * n_far]
        total = near[...]
        for r in far:
            total = total + r[...].astype(f32)
        out[:, at : at + total.shape[1]] = total
        at += total.shape[1]


def choose_kernel(z, info, own_ref, near_ref, far_ref, farther_ref, *outs):
    sources = (own_ref, near_ref, far_ref, farther_ref)
    for which, out in zip((0, 1, 4, 5), outs):
        for b in range(z.nb):
            s = z.slot(info, which, b)
            rel = _div(s, z.ten_dev) ^ info[z.me]
            at = _rem(rel, 2) * z.ten_dev + _rem(s, z.ten_dev)
            line = _div(rel, 2)
            v = sources[0][at]
            for k in range(1, 4):
                v = jnp.where(line == k, sources[k][at], v)
            out[z.ranks(b), :] = v


def shrink_kernel(z, n_parts, info, x_ref, *refs):
    parts, (full_ref, out_ref) = refs[:n_parts], refs[n_parts:]
    wide = z.width // n_parts
    total = None
    for j in range(n_parts):
        if n_parts == 1:
            cut = slice(0, wide)
        else:
            cut = pl.ds(pl.multiple_of((info[z.quarter] ^ j) * wide, wide), wide)
        full_ref[:, cut] = parts[j][...]
        term = _dot(x_ref[:, cut], parts[j][...], NT)
        total = term if total is None else total + term
    for b in range(z.nb):
        out_ref[:, z.block(b)] = total[z.block(b), :].T[z.ranks(b), :]


def projected_kernel(z, info, base_ref, mine_ref, other_ref, up_ref, out_ref, spread):
    spread[...] = jnp.zeros_like(spread)
    for b in range(z.nb):
        cut = z.block(b)
        spread[z.ranks(b), cut] = (mine_ref[:, cut] + other_ref[:, cut]).astype(bf16)
    wide = _dot(spread[...], up_ref[...], TN)
    for b in range(z.nb):
        cut = z.block(b)
        full = base_ref[cut, :] + adapter_scale * wide[cut]
        out_ref[cut, :] = _masked(full, z.valid(info, b)).astype(bf16)


def tokens_kernel(z, first, info, g_ref, w_ref, mine_ref, other_ref, d_ref, *refs):
    out_ref, spread = refs[-2:]
    step = pl.program_id(0)

    @pl.when(step == 0)
    def _():
        spread[...] = jnp.zeros_like(spread)
        for b in range(z.nb):
            cut = z.block(b)
            v = (mine_ref[:, cut] + other_ref[:, cut]) * adapter_scale
            spread[z.ranks(b), cut] = v.astype(bf16)

    wide = out_ref.shape[1]
    cut = pl.ds(pl.multiple_of((first + step) * wide, wide), wide)
    through = _dot(g_ref[...], w_ref[cut, :], NT)
    out_ref[...] = (through + _dot(spread[...], d_ref[:, cut], TN)).astype(bf16)


def on_device(
    n_groups,
    n_dp,
    tokens,
    base_weight,
    adapter_down,
    adapter_up,
    out_cotangent,
    block_tenant,
    block_valid,
    tenant_slot,
):
    nb = block_tenant.shape[0]
    rows, width = tokens.shape
    cols = out_cotangent.shape[1]
    tenants = tenant_slot.shape[0]
    ten_dev, _, rank = adapter_down.shape
    z = Sizes(n_dp, nb, ten_dev, rank, cols, width)
    n_far = z.n_far
    me = lax.axis_index("dp")
    core = lax.axis_index("tensor")
    group = lax.axis_index("groups")
    shared = n_groups == 2 and n_dp == 8
    n_parts = 4 if shared else 1
    mine_q = group * 2 + me % 2 if shared else jnp.int32(0)
    quarter = width // n_parts

    down_t = jnp.swapaxes(adapter_down, 1, 2)
    if shared:
        to_y = lax.dynamic_slice_in_dim(down_t, (mine_q ^ 1) * quarter, quarter, axis=2)
        from_y = _xor(to_y, n_dp, 1)
    far_up = [_xor(adapter_up, n_dp, NEAR * j) for j in range(1, n_far)]
    lanes = jnp.pad(block_tenant, (0, LANES - nb))
    tenant_match = lanes[:, None] == jnp.arange(tenants, dtype=i32)[None, :]
    slots = jnp.sum(jnp.where(tenant_match, tenant_slot[None, :], 0), axis=1).astype(i32)
    lane = jnp.arange(LANES, dtype=i32)
    place = jnp.where(lane == 0, me, jnp.where(lane == 1, core, mine_q))
    slots = _tie(slots, place)
    slots_x = _swap(slots, "groups") if shared else slots

    line = lax.broadcasted_iota(i32, (16, LANES), 0)
    tag = jnp.where(line == 0, slots[None, :], slots_x[None, :]).astype(bf16)
    tag = jnp.pad(tag, ((0, 0), (0, cols - LANES)))
    ups = [u.reshape(ten_dev * rank, cols) for u in [adapter_up] + far_up]
    packet = jnp.concatenate(ups + [tag], axis=0)
    packets = [packet] + [_xor(packet, n_dp, k) for k in range(1, NEAR)]

    if shared:
        own = lax.dynamic_slice_in_dim(down_t, mine_q * quarter, quarter, axis=2)
        shard = jnp.concatenate([own, from_y], axis=0)
        shard_far = _xor(shard, n_dp, 4)
        shard_near = _xor(shard, n_dp, 2)

    base_other = _call(
        functools.partial(other_kernel, z), "base_other", (1,),
        [pl.BlockSpec(memory_space=pl.ANY)] * 2,
        _whole((rows, cols)), _shape((rows, cols), bf16),
        [
            pltpu.VMEM((rows, width), bf16), pltpu.VMEM((width, cols), bf16),
            pltpu.SemaphoreType.DMA((5,)), pltpu.SemaphoreType.DMA((5,)),
        ],
        vmem=BIG_VMEM,
    )(_tie(place, shard if shared else packet), tokens, base_weight)
    base_arrived = _swap(base_other, "tensor")
    packets = [_tie(p, base_other) for p in packets]

    line = lax.broadcasted_iota(i32, (8, LANES), 0)
    info = jnp.where(line == 6, place[None, :], jnp.pad(block_valid, (0, LANES - nb))[None, :])
    for k in range(NEAR):
        info = jnp.where(line == k, packets[k][-16, :LANES].astype(i32)[None, :], info)
    for k in range(2):
        info = jnp.where(line == 4 + k, packets[k][-15, :LANES].astype(i32)[None, :], info)

    if shared:
        info = _tie(info, shard_far, shard_near)
        farther = _xor(shard_far, n_dp, 2)

    part = (rank, rows)
    block_up, back_part = _call(
        functools.partial(back_kernel, z), "back", (1,),
        [VMEM] * (1 + NEAR), [VMEM, _whole(part)],
        [_shape((nb * rank, cols), bf16), _shape(part, f32)], [],
    )(info, out_cotangent, *packets)
    back_other = _swap(back_part, "tensor")
    cotangent_other = _swap(_tie(out_cotangent, back_part), "tensor")

    packed_rows = n_dp * CAP * rank
    near_rows = packed_rows // NEAR

    def pack(info, start, wide):
        return _call(
            functools.partial(pack_kernel, z, NEAR, start), "pack_down", (1,),
            [VMEM] * 3, [_whole((near_rows, wide))] * NEAR,
            [_shape((near_rows, wide), bf16)] * NEAR,
            [pltpu.VMEM((packed_rows, rows), bf16)],
        )(info, back_part, back_other, tokens)

    def to_near(sends):
        return [sends[0]] + [_xor(sends[k], n_dp, k) for k in range(1, NEAR)]

    def dense(info, got):
        wide = got[0].shape[1]
        out = (ten_dev * rank, wide)
        return _call(
            functools.partial(dense_kernel, z), "dense", (1,),
            [VMEM] * NEAR, [VMEM] + [_whole(out)] * (n_far - 1),
            [_shape(out, f32)] + [_shape(out, bf16)] * (n_far - 1), [],
        )(info, *got)

    def to_far(parts):
        return [parts[0]] + [_xor(parts[j], n_dp, NEAR * j) for j in range(1, n_far)]

    def final(groups):
        wide = sum(g[0].shape[1] for g in groups)
        out = (ten_dev * rank, wide)
        total = _call(
            functools.partial(final_kernel, len(groups), n_far), "final", (1,),
            [VMEM] * (len(groups) * n_far), _whole(out), _shape(out, f32), [],
        )(info, *[a for g in groups for a in g])
        return total.reshape(ten_dev, rank, wide)

    half = width // 2
    sends_a = pack(_tie(info, cotangent_other, base_arrived), 0, half)

    base_own, g_full = _call(
        functools.partial(own_kernel, z), "base_own", (1,),
        [VMEM] * 5, [VMEM, VMEM],
        [_shape((rows, cols), f32), _shape((rows, 2 * cols), bf16)], [],
    )(_tie(info, sends_a[0]), tokens, base_weight, base_arrived, out_cotangent, cotangent_other)

    if shared:
        block = (nb * rank, quarter)
        chosen = _call(
            functools.partial(choose_kernel, z), "choose", (1,),
            [VMEM] * 4, [_whole(block)] * 4, [_shape(block, bf16)] * 4, [],
        )(_tie(info, base_own), shard, shard_near, shard_far, farther)
        got_y = _xor(chosen[1], n_dp, 1)
        got_x = _swap(chosen[2], "groups")
        got_d = lax.ppermute(
            chosen[3],
            ("groups", "dp"),
            [(g * n_dp + d, (1 - g) * n_dp + (d ^ 1)) for g in range(2) for d in range(n_dp)],
        )
        after_choose = chosen[0]
    else:
        every = lax.all_gather(down_t, "dp", axis=0, tiled=True)
        got_down = [jnp.take(every, slots[:nb], axis=0).reshape(nb * rank, width)]
        after_choose = base_own

    sends_b = pack(_tie(info, after_choose), half, half)

    gate = [sends_b[0]] + ([got_x] if shared else [])
    got_a = to_near([sends_a[0], _tie(sends_a[1], *gate), *sends_a[2:]])
    got_b = to_near(sends_b)
    if shared:
        got_down = [chosen[0], got_y, got_x, got_d]
    block_down, shrink_part = _call(
        functools.partial(shrink_kernel, z, n_parts), "shrink", (1,),
        [VMEM] * (1 + n_parts), [VMEM, _whole(part)],
        [_shape((nb * rank, width), bf16), _shape(part, f32)], [],
    )(_tie(info, sends_b[0]), tokens, *got_down)
    shrink_other = _swap(shrink_part, "tensor")

    dense_a = dense(_tie(info, shrink_part), got_a)
    far_a = to_far(dense_a)

    step = min(1024, width // 4)
    n_calls = 2
    per_call = width // step // n_calls

    def token_grads(info, call, so_far):
        first = call * per_call
        return _call(
            functools.partial(tokens_kernel, z, first), "token_grads", (per_call,),
            [VMEM] * 5 + ([] if so_far is None else [pl.BlockSpec(memory_space=pl.ANY)]),
            pl.BlockSpec((rows, step), lambda i, *_: (0, first + i)),
            _shape((rows, width), bf16), [pltpu.VMEM((nb * rank, rows), bf16)],
            None if so_far is None else {6: 0},
        )(
            info, g_full, base_weight, back_part, back_other, block_down,
            *([] if so_far is None else [so_far]),
        )

    grad_tokens = token_grads(_tie(info, dense_a[1]), 0, None)

    up_sends = _call(
        functools.partial(pack_up_kernel, z, NEAR), "pack_up", (1,),
        [VMEM] * 3, [_whole((near_rows, cols))] * NEAR,
        [_shape((near_rows, cols), bf16)] * NEAR,
        [pltpu.VMEM((packed_rows, rows), bf16)],
    )(_tie(info, grad_tokens), shrink_part, shrink_other, g_full)
    got_u = to_near(up_sends)

    dense_b = dense(_tie(info, up_sends[0]), got_b)
    far_b = to_far(dense_b)

    grad_tokens = token_grads(_tie(info, dense_b[1]), 1, grad_tokens)
    dense_u = dense(_tie(info, grad_tokens), got_u)
    far_u = to_far(dense_u)

    projected = _call(
        functools.partial(projected_kernel, z), "projected", (1,),
        [VMEM] * 4, _whole((rows, cols)), _shape((rows, cols), bf16),
        [pltpu.VMEM((nb * rank, rows), bf16)],
    )(_tie(info, dense_u[1]), base_own, shrink_part, shrink_other, block_up)

    grad_down = jnp.swapaxes(final([far_a, far_b]), 1, 2)
    grad_up = final([far_u])
    return projected, grad_tokens, grad_down, grad_up


def solution(mesh):
    n_groups, n_dp = mesh.shape["groups"], mesh.shape["dp"]
    in_specs = (
        P(("groups", "dp"), "tensor"),
        P("tensor", None),
        P("dp", "tensor", None),
        P("dp", None, "tensor"),
        P(("groups", "dp"), "tensor"),
        P(("groups", "dp")),
        P(("groups", "dp")),
        P("groups"),
    )
    out_specs = (
        P(("groups", "dp"), "tensor"),
        P(("groups", "dp"), "tensor"),
        P(("groups", "dp"), "tensor", None),
        P(("groups", "dp"), None, "tensor"),
    )

    def run(*args):
        return on_device(n_groups, n_dp, *args)

    return jax.shard_map(
        run, mesh=mesh, in_specs=in_specs, out_specs=out_specs, check_vma=False
    )
```

```python
import functools

import jax
import jax.numpy as jnp
from jax import lax
from jax.experimental import pallas as pl
from jax.experimental.pallas import tpu as pltpu
from jax.sharding import PartitionSpec as P

TENANT_BLOCK = 128
CAP = 2
NEAR = 4
VMEM_LIMIT = 16 * 1024 * 1024
BIG_VMEM = 52 * 1024 * 1024
LANES = 128

adapter_scale = 2.0
f32 = jnp.float32
bf16 = jnp.bfloat16
i32 = jnp.int32

NT = (((1,), (1,)), ((), ()))
TN = (((0,), (0,)), ((), ()))
NN = (((1,), (0,)), ((), ()))


def _dot(a, b, dims):
    return lax.dot_general(a, b, dims, preferred_element_type=f32)


def _swap(x, axis):
    return lax.ppermute(x, axis, [(0, 1), (1, 0)])


def _xor(x, n, k):
    return lax.ppermute(x, "dp", [(i, i ^ k) for i in range(n)])


def _tie(x, *after):
    return lax.optimization_barrier((x,) + after)[0]


def _div(a, n):
    return a >> (n.bit_length() - 1) if n & (n - 1) == 0 else lax.div(a, jnp.int32(n))


def _rem(a, n):
    return a & (n - 1) if n & (n - 1) == 0 else lax.rem(a, jnp.int32(n))


VMEM = pl.BlockSpec(memory_space=pltpu.VMEM)


def _shape(shape, dtype):
    return jax.ShapeDtypeStruct(shape, dtype)


def _call(
    body, name, grid, in_specs, out_specs, out_shape, scratch, aliases=None, vmem=VMEM_LIMIT,
    n_scalars=1,
):
    return pl.pallas_call(
        body,
        name=name,
        grid_spec=pltpu.PrefetchScalarGridSpec(
            num_scalar_prefetch=n_scalars,
            grid=grid,
            in_specs=in_specs,
            out_specs=out_specs,
            scratch_shapes=scratch,
        ),
        out_shape=out_shape,
        input_output_aliases=aliases or {},
        compiler_params=pltpu.CompilerParams(vmem_limit_bytes=vmem),
        cost_estimate=pl.CostEstimate(flops=1, bytes_accessed=1, transcendentals=0),
    )


def _whole(shape):
    return pl.BlockSpec(shape, lambda *_: (0,) * len(shape))


class Sizes:
    def __init__(self, n_dp, nb, ten_dev, rank, cols, width):
        self.n_dp, self.nb, self.ten_dev = n_dp, nb, ten_dev
        self.rank, self.cols, self.width = rank, cols, width
        self.n_far = n_dp // NEAR
        self.rows = nb * TENANT_BLOCK
        self.me, self.core, self.quarter = (8, 0), (8, 1), (8, 2)

    def block(self, b):
        return slice(b * TENANT_BLOCK, (b + 1) * TENANT_BLOCK)

    def ranks(self, b):
        return slice(b * self.rank, (b + 1) * self.rank)

    def slot(self, info, which, b):
        return info[6, info[which, b]]

    def valid(self, info, b):
        return info[9, b]

    def owner_and_order(self, info, which):
        owners = [_div(self.slot(info, which, b), self.ten_dev) for b in range(self.nb)]
        orders = []
        for b in range(self.nb):
            n = jnp.int32(0)
            for c in range(b):
                n = n + jnp.where(owners[c] == owners[b], 1, 0)
            orders.append(n)
        return owners, orders

    def places(self, info):
        owners, orders = self.owner_and_order(info, 0)
        out = []
        for o, r in zip(owners, orders):
            rel = o ^ info[self.me]
            place = (_rem(rel, NEAR) * self.n_far + _div(rel, NEAR)) * CAP + r
            out.append(pl.ds(pl.multiple_of(place * self.rank, self.rank), self.rank))
        return out


def _masked(x, valid):
    row = lax.broadcasted_iota(i32, x.shape, 0)
    return jnp.where(row < valid, x, jnp.zeros((), x.dtype))


def other_kernel(z, place, x_hbm, w_hbm, out_ref, x_buf, w_buf, x_sem, w_sem):
    far = pl.ds(pl.multiple_of((1 - place[z.core]) * z.cols, z.cols), z.cols)
    unit = z.width // 8
    copies = []
    for i, (first, last) in enumerate(((0, 1), (1, 2), (2, 4), (4, 6), (6, 8))):
        cut = pl.ds(first * unit, (last - first) * unit)
        x = pltpu.make_async_copy(x_hbm.at[:, cut], x_buf.at[:, cut], x_sem.at[i])
        w = pltpu.make_async_copy(w_hbm.at[cut, far], w_buf.at[cut], w_sem.at[i])
        x.start()
        w.start()
        copies.append((x, w, cut))
    total = None
    for x, w, cut in copies:
        x.wait()
        w.wait()
        term = _dot(x_buf[:, cut], w_buf[cut, :], NN)
        total = term if total is None else total + term
    out_ref[...] = total.astype(bf16)


def own_kernel(z, info, x_ref, w_ref, far_ref, g_ref, h_ref, out_ref, full_ref):
    own = pl.ds(pl.multiple_of(info[z.core] * z.cols, z.cols), z.cols)
    far = pl.ds(pl.multiple_of((1 - info[z.core]) * z.cols, z.cols), z.cols)
    out_ref[...] = _dot(x_ref[...], w_ref[:, own], NN) + far_ref[...].astype(f32)
    for b in range(z.nb):
        cut = z.block(b)
        full_ref[cut, own] = _masked(g_ref[cut, :], z.valid(info, b))
        full_ref[cut, far] = _masked(h_ref[cut, :], z.valid(info, b))


def back_kernel(z, info, g_ref, *refs):
    packets, (up_ref, part_ref) = refs[:NEAR], refs[NEAR:]
    for b in range(z.nb):
        s = z.slot(info, 0, b)
        rel = _div(s, z.ten_dev) ^ info[z.me]
        at = _div(rel, NEAR) * z.ten_dev + _rem(s, z.ten_dev)
        at = pl.ds(pl.multiple_of(at * z.rank, z.rank), z.rank)
        near = _rem(rel, NEAR)
        u = packets[0][at, :]
        for k in range(1, NEAR):
            u = jnp.where(near == k, packets[k][at, :], u)
        up_ref[z.ranks(b), :] = u
        g = _masked(g_ref[z.block(b), :], z.valid(info, b))
        part_ref[:, z.block(b)] = _dot(u, g, NT)


def pack_kernel(z, n_out, start, info, mine_ref, other_ref, x_ref, *refs):
    outs, packed = refs[:n_out], refs[n_out]
    packed[...] = jnp.zeros_like(packed)
    for b, place in enumerate(z.places(info)):
        cut = z.block(b)
        v = (mine_ref[:, cut] + other_ref[:, cut]) * adapter_scale
        packed[place, cut] = v.astype(bf16)
    wide = outs[0].shape[1]
    res = _dot(packed[...], x_ref[:, start : start + wide], NN).astype(bf16)
    each = res.shape[0] // n_out
    for k in range(n_out):
        outs[k][...] = res[k * each : (k + 1) * each]


def pack_up_kernel(z, n_out, info, mine_ref, other_ref, g_ref, *refs):
    outs, packed = refs[:n_out], refs[n_out]
    own = pl.ds(pl.multiple_of(info[z.core] * z.cols, z.cols), z.cols)
    packed[...] = jnp.zeros_like(packed)
    for b, place in enumerate(z.places(info)):
        cut = z.block(b)
        packed[place, cut] = (mine_ref[:, cut] + other_ref[:, cut]).astype(bf16)
    res = (adapter_scale * _dot(packed[...], g_ref[:, own], NN)).astype(bf16)
    each = res.shape[0] // n_out
    for k in range(n_out):
        outs[k][...] = res[k * each : (k + 1) * each]


def dense_kernel(z, info, *refs):
    got, near_ref, far_refs = refs[:NEAR], refs[NEAR], refs[NEAR + 1 :]
    n = CAP * z.rank
    shape = (z.ten_dev * z.rank, n)
    row = lax.broadcasted_iota(i32, shape, 0)
    col = lax.broadcasted_iota(i32, shape, 1)
    same = _rem(row, z.rank) == _rem(col, z.rank)
    row_slot = _div(row, z.rank)
    tables = [z.owner_and_order(info, k) for k in range(NEAR)]
    for j in range(z.n_far):
        holder = info[z.me] ^ (NEAR * j)
        total = None
        for k in range(NEAR):
            owners, orders = tables[k]
            local = []
            for r in range(CAP):
                found = jnp.int32(0)
                for b in range(z.nb):
                    hit = (owners[b] == holder) & (orders[b] == r)
                    found = jnp.where(hit, _rem(z.slot(info, k, b), z.ten_dev), found)
                local.append(found)
            wanted = jnp.where(col < z.rank, local[0], local[1])
            one_hot = jnp.where(same & (row_slot == wanted), 1.0, 0.0).astype(bf16)
            term = _dot(one_hot, got[k][j * n : (j + 1) * n, :], NN)
            total = term if total is None else total + term
        if j == 0:
            near_ref[...] = total
        else:
            far_refs[j - 1][...] = total.astype(bf16)


def final_kernel(n_parts, n_far, info, *refs):
    out = refs[-1]
    at = 0
    for p in range(n_parts):
        near, far = refs[p * n_far], refs[p * n_far + 1 : (p + 1) * n_far]
        total = near[...]
        for r in far:
            total = total + r[...].astype(f32)
        out[:, at : at + total.shape[1]] = total
        at += total.shape[1]


def choose_kernel(z, info, info_x, own_ref, near_ref, far_ref, farther_ref, *outs):
    sources = (own_ref, near_ref, far_ref, farther_ref)
    wanted = ((info, 0), (info, 1), (info_x, 0), (info_x, 1))
    for (table, which), out in zip(wanted, outs):
        for b in range(z.nb):
            s = z.slot(table, which, b)
            rel = _div(s, z.ten_dev) ^ info[z.me]
            at = _rem(rel, 2) * z.ten_dev + _rem(s, z.ten_dev)
            line = _div(rel, 2)
            v = sources[0][at]
            for k in range(1, 4):
                v = jnp.where(line == k, sources[k][at], v)
            out[z.ranks(b), :] = v


def shrink_kernel(z, n_parts, info, x_ref, *refs):
    parts, (full_ref, out_ref) = refs[:n_parts], refs[n_parts:]
    wide = z.width // n_parts
    total = None
    for j in range(n_parts):
        if n_parts == 1:
            cut = slice(0, wide)
        else:
            cut = pl.ds(pl.multiple_of((info[z.quarter] ^ j) * wide, wide), wide)
        full_ref[:, cut] = parts[j][...]
        term = _dot(x_ref[:, cut], parts[j][...], NT)
        total = term if total is None else total + term
    for b in range(z.nb):
        out_ref[:, z.block(b)] = total[z.block(b), :].T[z.ranks(b), :]


def projected_kernel(z, info, base_ref, mine_ref, other_ref, up_ref, out_ref, spread):
    spread[...] = jnp.zeros_like(spread)
    for b in range(z.nb):
        cut = z.block(b)
        spread[z.ranks(b), cut] = (mine_ref[:, cut] + other_ref[:, cut]).astype(bf16)
    wide = _dot(spread[...], up_ref[...], TN)
    for b in range(z.nb):
        cut = z.block(b)
        full = base_ref[cut, :] + adapter_scale * wide[cut]
        out_ref[cut, :] = _masked(full, z.valid(info, b)).astype(bf16)


def through_kernel(info, g_ref, w_ref, out_ref):
    half = out_ref.shape[1] // 2
    for h in range(2):
        cut = slice(h * half, (h + 1) * half)
        out_ref[:, cut] = _dot(g_ref[...], w_ref[cut, :], NT)


def tokens_kernel(z, first, ready, info, g_ref, w_ref, mine_ref, other_ref, d_ref, *refs):
    out_ref, spread = refs[-2:]
    step = pl.program_id(0)

    @pl.when(step == 0)
    def _():
        spread[...] = jnp.zeros_like(spread)
        for b in range(z.nb):
            cut = z.block(b)
            v = (mine_ref[:, cut] + other_ref[:, cut]) * adapter_scale
            spread[z.ranks(b), cut] = v.astype(bf16)

    wide = out_ref.shape[1]
    cut = pl.ds(pl.multiple_of((first + step) * wide, wide), wide)
    through = g_ref[:, cut] if ready else _dot(g_ref[...], w_ref[cut, :], NT)
    out_ref[...] = (through + _dot(spread[...], d_ref[:, cut], TN)).astype(bf16)


def on_device(
    n_groups,
    n_dp,
    tokens,
    base_weight,
    adapter_down,
    adapter_up,
    out_cotangent,
    block_tenant,
    block_valid,
    tenant_slot,
):
    nb = block_tenant.shape[0]
    rows, width = tokens.shape
    cols = out_cotangent.shape[1]
    tenants = tenant_slot.shape[0]
    ten_dev, _, rank = adapter_down.shape
    z = Sizes(n_dp, nb, ten_dev, rank, cols, width)
    n_far = z.n_far
    me = lax.axis_index("dp")
    core = lax.axis_index("tensor")
    group = lax.axis_index("groups")
    shared = n_groups == 2 and n_dp == 8
    n_parts = 4 if shared else 1
    mine_q = group * 2 + me % 2 if shared else jnp.int32(0)
    quarter = width // n_parts

    down_t = jnp.swapaxes(adapter_down, 1, 2)
    if shared:
        to_y = lax.dynamic_slice_in_dim(down_t, (mine_q ^ 1) * quarter, quarter, axis=2)
        from_y = _xor(to_y, n_dp, 1)
    far_up = [_xor(adapter_up, n_dp, NEAR * j) for j in range(1, n_far)]
    lane = jnp.arange(LANES, dtype=i32)

    def spread_out(x):
        hit = lane[:, None] == jnp.arange(x.shape[0], dtype=i32)[None, :]
        return jnp.sum(jnp.where(hit, x[None, :], 0), axis=1).astype(i32)

    own_tenants = spread_out(block_tenant)
    tag = jnp.broadcast_to(own_tenants[None, :], (16, LANES)).astype(bf16)
    tag = jnp.pad(tag, ((0, 0), (0, cols - LANES)))
    ups = [u.reshape(ten_dev * rank, cols) for u in [adapter_up] + far_up]
    packet = jnp.concatenate(ups + [tag], axis=0)
    packets = [packet] + [_xor(packet, n_dp, k) for k in range(1, NEAR)]

    if shared:
        own = lax.dynamic_slice_in_dim(down_t, mine_q * quarter, quarter, axis=2)
        shard = jnp.concatenate([own, from_y], axis=0)
        shard_far = _xor(shard, n_dp, 4)
        shard_near = _xor(shard, n_dp, 2)

    line = lax.broadcasted_iota(i32, (16, LANES), 0)
    place = jnp.where(lane == 0, me, jnp.where(lane == 1, core, mine_q))
    info = jnp.where(line == 8, place[None, :], spread_out(block_valid)[None, :])
    info = jnp.where(line == 6, spread_out(tenant_slot)[None, :], info)
    info = jnp.where(line == 0, own_tenants[None, :], info)

    base_other = _call(
        functools.partial(other_kernel, z), "base_other", (1,),
        [pl.BlockSpec(memory_space=pl.ANY)] * 2,
        _whole((rows, cols)), _shape((rows, cols), bf16),
        [
            pltpu.VMEM((rows, width), bf16), pltpu.VMEM((width, cols), bf16),
            pltpu.SemaphoreType.DMA((5,)), pltpu.SemaphoreType.DMA((5,)),
        ],
        vmem=BIG_VMEM,
    )(_tie(info, shard if shared else packet), tokens, base_weight)
    base_arrived = _swap(base_other, "tensor")
    packets = [_tie(p, base_other) for p in packets]

    for k in range(1, NEAR):
        info = jnp.where(line == k, packets[k][-16, :LANES].astype(i32)[None, :], info)

    if shared:
        info = _tie(info, shard_far, shard_near)
        farther = _xor(shard_far, n_dp, 2)
        info_x = _swap(info, "groups")

    part = (rank, rows)
    block_up, back_part = _call(
        functools.partial(back_kernel, z), "back", (1,),
        [VMEM] * (1 + NEAR), [VMEM, _whole(part)],
        [_shape((nb * rank, cols), bf16), _shape(part, f32)], [],
    )(info, out_cotangent, *packets)
    back_other = _swap(back_part, "tensor")
    cotangent_other = _swap(_tie(out_cotangent, back_part), "tensor")

    packed_rows = n_dp * CAP * rank
    near_rows = packed_rows // NEAR

    def pack(info, start, wide):
        return _call(
            functools.partial(pack_kernel, z, NEAR, start), "pack_down", (1,),
            [VMEM] * 3, [_whole((near_rows, wide))] * NEAR,
            [_shape((near_rows, wide), bf16)] * NEAR,
            [pltpu.VMEM((packed_rows, rows), bf16)],
        )(info, back_part, back_other, tokens)

    def to_near(sends):
        return [sends[0]] + [_xor(sends[k], n_dp, k) for k in range(1, NEAR)]

    def dense(info, got):
        wide = got[0].shape[1]
        out = (ten_dev * rank, wide)
        return _call(
            functools.partial(dense_kernel, z), "dense", (1,),
            [VMEM] * NEAR, [VMEM] + [_whole(out)] * (n_far - 1),
            [_shape(out, f32)] + [_shape(out, bf16)] * (n_far - 1), [],
        )(info, *got)

    def to_far(parts):
        return [parts[0]] + [_xor(parts[j], n_dp, NEAR * j) for j in range(1, n_far)]

    def final(groups):
        wide = sum(g[0].shape[1] for g in groups)
        out = (ten_dev * rank, wide)
        total = _call(
            functools.partial(final_kernel, len(groups), n_far), "final", (1,),
            [VMEM] * (len(groups) * n_far), _whole(out), _shape(out, f32), [],
        )(info, *[a for g in groups for a in g])
        return total.reshape(ten_dev, rank, wide)

    half = width // 2
    sends_a = pack(_tie(info, cotangent_other, base_arrived, *([info_x] if shared else [])), 0, half)

    if shared:
        block = (nb * rank, quarter)
        chosen = _call(
            functools.partial(choose_kernel, z), "choose", (1,),
            [VMEM] * 4, [_whole(block)] * 4, [_shape(block, bf16)] * 4, [],
            n_scalars=2,
        )(_tie(info, sends_a[0]), info_x, shard, shard_near, shard_far, farther)
        got_y = _xor(chosen[1], n_dp, 1)
        got_x = _swap(chosen[2], "groups")
        got_d = lax.ppermute(
            chosen[3],
            ("groups", "dp"),
            [(g * n_dp + d, (1 - g) * n_dp + (d ^ 1)) for g in range(2) for d in range(n_dp)],
        )
        after_choose = chosen[0]
    else:
        every = lax.all_gather(down_t, "dp", axis=0, tiled=True)
        slots = jnp.take(tenant_slot, block_tenant, axis=0)
        got_down = [jnp.take(every, slots, axis=0).reshape(nb * rank, width)]
        after_choose = sends_a[0]

    sends_b = pack(_tie(info, after_choose), half, half)

    base_own, g_full = _call(
        functools.partial(own_kernel, z), "base_own", (1,),
        [VMEM] * 5, [VMEM, VMEM],
        [_shape((rows, cols), f32), _shape((rows, 2 * cols), bf16)], [],
    )(_tie(info, sends_b[0]), tokens, base_weight, base_arrived, out_cotangent, cotangent_other)

    through = _call(
        through_kernel, "through", (1,), [VMEM] * 2, VMEM, _shape((rows, half), f32), [],
    )(_tie(info, base_own), g_full, base_weight)

    gate = [through]
    got_a = to_near([sends_a[0], _tie(sends_a[1], *gate), *sends_a[2:]])
    got_b = to_near(sends_b)
    if shared:
        got_down = [chosen[0], got_y, got_x, got_d]
    block_down, shrink_part = _call(
        functools.partial(shrink_kernel, z, n_parts), "shrink", (1,),
        [VMEM] * (1 + n_parts), [VMEM, _whole(part)],
        [_shape((nb * rank, width), bf16), _shape(part, f32)], [],
    )(_tie(info, through), tokens, *got_down)
    shrink_other = _swap(shrink_part, "tensor")

    dense_a = dense(_tie(info, shrink_part), got_a)
    far_a = to_far(dense_a)

    step = min(1024, width // 4)
    n_calls = 2
    per_call = width // step // n_calls

    def token_grads(info, call, g, so_far):
        first = call * per_call
        return _call(
            functools.partial(tokens_kernel, z, first, so_far is None), "token_grads", (per_call,),
            [VMEM] * 5 + ([] if so_far is None else [pl.BlockSpec(memory_space=pl.ANY)]),
            pl.BlockSpec((rows, step), lambda i, *_: (0, first + i)),
            _shape((rows, width), bf16), [pltpu.VMEM((nb * rank, rows), bf16)],
            None if so_far is None else {6: 0},
        )(
            info, g, g if so_far is None else base_weight, back_part, back_other, block_down,
            *([] if so_far is None else [so_far]),
        )

    grad_tokens = token_grads(_tie(info, dense_a[1]), 0, through, None)

    up_sends = _call(
        functools.partial(pack_up_kernel, z, NEAR), "pack_up", (1,),
        [VMEM] * 3, [_whole((near_rows, cols))] * NEAR,
        [_shape((near_rows, cols), bf16)] * NEAR,
        [pltpu.VMEM((packed_rows, rows), bf16)],
    )(_tie(info, grad_tokens), shrink_part, shrink_other, g_full)
    got_u = to_near(up_sends)

    dense_b = dense(_tie(info, up_sends[0]), got_b)
    far_b = to_far(dense_b)

    grad_tokens = token_grads(_tie(info, dense_b[1]), 1, g_full, grad_tokens)
    dense_u = dense(_tie(info, grad_tokens), got_u)
    far_u = to_far(dense_u)

    projected = _call(
        functools.partial(projected_kernel, z), "projected", (1,),
        [VMEM] * 4, _whole((rows, cols)), _shape((rows, cols), bf16),
        [pltpu.VMEM((nb * rank, rows), bf16)],
    )(_tie(info, dense_u[1]), base_own, shrink_part, shrink_other, block_up)

    grad_down = jnp.swapaxes(final([far_a, far_b]), 1, 2)
    grad_up = final([far_u])
    return projected, grad_tokens, grad_down, grad_up


def solution(mesh):
    n_groups, n_dp = mesh.shape["groups"], mesh.shape["dp"]
    in_specs = (
        P(("groups", "dp"), "tensor"),
        P("tensor", None),
        P("dp", "tensor", None),
        P("dp", None, "tensor"),
        P(("groups", "dp"), "tensor"),
        P(("groups", "dp")),
        P(("groups", "dp")),
        P("groups"),
    )
    out_specs = (
        P(("groups", "dp"), "tensor"),
        P(("groups", "dp"), "tensor"),
        P(("groups", "dp"), "tensor", None),
        P(("groups", "dp"), None, "tensor"),
    )

    def run(*args):
        return on_device(n_groups, n_dp, *args)

    return jax.shard_map(
        run, mesh=mesh, in_specs=in_specs, out_specs=out_specs, check_vma=False
    )
```

```python
import functools

import jax
import jax.numpy as jnp
from jax import lax
from jax.experimental import pallas as pl
from jax.experimental.pallas import tpu as pltpu
from jax.sharding import PartitionSpec as P

TENANT_BLOCK = 128
CAP = 2
NEAR = 4
VMEM_LIMIT = 16 * 1024 * 1024
BIG_VMEM = 52 * 1024 * 1024
LANES = 128

adapter_scale = 2.0
f32 = jnp.float32
bf16 = jnp.bfloat16
i32 = jnp.int32

NT = (((1,), (1,)), ((), ()))
TN = (((0,), (0,)), ((), ()))
NN = (((1,), (0,)), ((), ()))


def _dot(a, b, dims):
    return lax.dot_general(a, b, dims, preferred_element_type=f32)


def _swap(x, axis):
    return lax.ppermute(x, axis, [(0, 1), (1, 0)])


def _xor(x, n, k):
    return lax.ppermute(x, "dp", [(i, i ^ k) for i in range(n)])


def _tie(x, *after):
    return lax.optimization_barrier((x,) + after)[0]


def _div(a, n):
    return a >> (n.bit_length() - 1) if n & (n - 1) == 0 else lax.div(a, jnp.int32(n))


def _rem(a, n):
    return a & (n - 1) if n & (n - 1) == 0 else lax.rem(a, jnp.int32(n))


VMEM = pl.BlockSpec(memory_space=pltpu.VMEM)


def _shape(shape, dtype):
    return jax.ShapeDtypeStruct(shape, dtype)


def _call(
    body, name, grid, in_specs, out_specs, out_shape, scratch, aliases=None, vmem=VMEM_LIMIT,
    n_scalars=1,
):
    return pl.pallas_call(
        body,
        name=name,
        grid_spec=pltpu.PrefetchScalarGridSpec(
            num_scalar_prefetch=n_scalars,
            grid=grid,
            in_specs=in_specs,
            out_specs=out_specs,
            scratch_shapes=scratch,
        ),
        out_shape=out_shape,
        input_output_aliases=aliases or {},
        compiler_params=pltpu.CompilerParams(vmem_limit_bytes=vmem),
        cost_estimate=pl.CostEstimate(flops=1, bytes_accessed=1, transcendentals=0),
    )


def _whole(shape):
    return pl.BlockSpec(shape, lambda *_: (0,) * len(shape))


class Sizes:
    def __init__(self, n_dp, nb, ten_dev, rank, cols, width):
        self.n_dp, self.nb, self.ten_dev = n_dp, nb, ten_dev
        self.rank, self.cols, self.width = rank, cols, width
        self.n_far = n_dp // NEAR
        self.rows = nb * TENANT_BLOCK
        self.me, self.core, self.quarter = (8, 0), (8, 1), (8, 2)

    def block(self, b):
        return slice(b * TENANT_BLOCK, (b + 1) * TENANT_BLOCK)

    def ranks(self, b):
        return slice(b * self.rank, (b + 1) * self.rank)

    def slot(self, info, which, b):
        return info[6, info[which, b]]

    def valid(self, info, b):
        return info[9, b]

    def owner_and_order(self, info, which):
        owners = [_div(self.slot(info, which, b), self.ten_dev) for b in range(self.nb)]
        orders = []
        for b in range(self.nb):
            n = jnp.int32(0)
            for c in range(b):
                n = n + jnp.where(owners[c] == owners[b], 1, 0)
            orders.append(n)
        return owners, orders

    def places(self, info):
        owners, orders = self.owner_and_order(info, 0)
        out = []
        for o, r in zip(owners, orders):
            rel = o ^ info[self.me]
            place = (_rem(rel, NEAR) * self.n_far + _div(rel, NEAR)) * CAP + r
            out.append(pl.ds(pl.multiple_of(place * self.rank, self.rank), self.rank))
        return out


def _masked(x, valid):
    row = lax.broadcasted_iota(i32, x.shape, 0)
    return jnp.where(row < valid, x, jnp.zeros((), x.dtype))


def other_kernel(z, place, x_hbm, w_hbm, out_ref, x_buf, w_buf, x_sem, w_sem):
    far = pl.ds(pl.multiple_of((1 - place[z.core]) * z.cols, z.cols), z.cols)
    unit = z.width // 8
    copies = []
    for i, (first, last) in enumerate(((0, 1), (1, 2), (2, 4), (4, 6), (6, 8))):
        cut = pl.ds(first * unit, (last - first) * unit)
        x = pltpu.make_async_copy(x_hbm.at[:, cut], x_buf.at[:, cut], x_sem.at[i])
        w = pltpu.make_async_copy(w_hbm.at[cut, far], w_buf.at[cut], w_sem.at[i])
        x.start()
        w.start()
        copies.append((x, w, cut))
    total = None
    for x, w, cut in copies:
        x.wait()
        w.wait()
        term = _dot(x_buf[:, cut], w_buf[cut, :], NN)
        total = term if total is None else total + term
    out_ref[...] = total.astype(bf16)


def own_kernel(z, info, x_ref, w_ref, far_ref, g_ref, h_ref, out_ref, full_ref):
    own = pl.ds(pl.multiple_of(info[z.core] * z.cols, z.cols), z.cols)
    far = pl.ds(pl.multiple_of((1 - info[z.core]) * z.cols, z.cols), z.cols)
    out_ref[...] = _dot(x_ref[...], w_ref[:, own], NN) + far_ref[...].astype(f32)
    for b in range(z.nb):
        cut = z.block(b)
        full_ref[cut, own] = _masked(g_ref[cut, :], z.valid(info, b))
        full_ref[cut, far] = _masked(h_ref[cut, :], z.valid(info, b))


def back_kernel(z, info, g_ref, *refs):
    packets, (up_ref, part_ref) = refs[:NEAR], refs[NEAR:]
    for b in range(z.nb):
        s = z.slot(info, 0, b)
        rel = _div(s, z.ten_dev) ^ info[z.me]
        at = _div(rel, NEAR) * z.ten_dev + _rem(s, z.ten_dev)
        at = pl.ds(pl.multiple_of(at * z.rank, z.rank), z.rank)
        near = _rem(rel, NEAR)
        u = packets[0][at, :]
        for k in range(1, NEAR):
            u = jnp.where(near == k, packets[k][at, :], u)
        up_ref[z.ranks(b), :] = u
        g = _masked(g_ref[z.block(b), :], z.valid(info, b))
        part_ref[:, z.block(b)] = _dot(u, g, NT)


def pack_kernel(z, n_out, start, info, mine_ref, other_ref, x_ref, *refs):
    outs, packed = refs[:n_out], refs[n_out]
    packed[...] = jnp.zeros_like(packed)
    for b, place in enumerate(z.places(info)):
        cut = z.block(b)
        v = (mine_ref[:, cut] + other_ref[:, cut]) * adapter_scale
        packed[place, cut] = v.astype(bf16)
    wide = outs[0].shape[1]
    res = _dot(packed[...], x_ref[:, start : start + wide], NN).astype(bf16)
    each = res.shape[0] // n_out
    for k in range(n_out):
        outs[k][...] = res[k * each : (k + 1) * each]


def pack_up_kernel(z, n_out, info, mine_ref, other_ref, g_ref, *refs):
    outs, packed = refs[:n_out], refs[n_out]
    own = pl.ds(pl.multiple_of(info[z.core] * z.cols, z.cols), z.cols)
    packed[...] = jnp.zeros_like(packed)
    for b, place in enumerate(z.places(info)):
        cut = z.block(b)
        packed[place, cut] = (mine_ref[:, cut] + other_ref[:, cut]).astype(bf16)
    res = (adapter_scale * _dot(packed[...], g_ref[:, own], NN)).astype(bf16)
    each = res.shape[0] // n_out
    for k in range(n_out):
        outs[k][...] = res[k * each : (k + 1) * each]


def dense_kernel(z, info, *refs):
    got, near_ref, far_refs = refs[:NEAR], refs[NEAR], refs[NEAR + 1 :]
    n = CAP * z.rank
    shape = (z.ten_dev * z.rank, n)
    row = lax.broadcasted_iota(i32, shape, 0)
    col = lax.broadcasted_iota(i32, shape, 1)
    same = _rem(row, z.rank) == _rem(col, z.rank)
    row_slot = _div(row, z.rank)
    tables = [z.owner_and_order(info, k) for k in range(NEAR)]
    for j in range(z.n_far):
        holder = info[z.me] ^ (NEAR * j)
        total = None
        for k in range(NEAR):
            owners, orders = tables[k]
            local = []
            for r in range(CAP):
                found = jnp.int32(0)
                for b in range(z.nb):
                    hit = (owners[b] == holder) & (orders[b] == r)
                    found = jnp.where(hit, _rem(z.slot(info, k, b), z.ten_dev), found)
                local.append(found)
            wanted = jnp.where(col < z.rank, local[0], local[1])
            one_hot = jnp.where(same & (row_slot == wanted), 1.0, 0.0).astype(bf16)
            term = _dot(one_hot, got[k][j * n : (j + 1) * n, :], NN)
            total = term if total is None else total + term
        if j == 0:
            near_ref[...] = total
        else:
            far_refs[j - 1][...] = total.astype(bf16)


def final_kernel(n_parts, n_far, info, *refs):
    out = refs[-1]
    at = 0
    for p in range(n_parts):
        near, far = refs[p * n_far], refs[p * n_far + 1 : (p + 1) * n_far]
        total = near[...]
        for r in far:
            total = total + r[...].astype(f32)
        out[:, at : at + total.shape[1]] = total
        at += total.shape[1]


def choose_kernel(z, info, info_x, own_ref, near_ref, far_ref, farther_ref, *outs):
    sources = (own_ref, near_ref, far_ref, farther_ref)
    wanted = ((info, 0), (info, 1), (info_x, 0), (info_x, 1))
    for (table, which), out in zip(wanted, outs):
        for b in range(z.nb):
            s = z.slot(table, which, b)
            rel = _div(s, z.ten_dev) ^ info[z.me]
            at = _rem(rel, 2) * z.ten_dev + _rem(s, z.ten_dev)
            line = _div(rel, 2)
            v = sources[0][at]
            for k in range(1, 4):
                v = jnp.where(line == k, sources[k][at], v)
            out[z.ranks(b), :] = v


def shrink_kernel(z, n_parts, info, x_ref, *refs):
    parts, (full_ref, out_ref) = refs[:n_parts], refs[n_parts:]
    wide = z.width // n_parts
    total = None
    for j in range(n_parts):
        if n_parts == 1:
            cut = slice(0, wide)
        else:
            cut = pl.ds(pl.multiple_of((info[z.quarter] ^ j) * wide, wide), wide)
        full_ref[:, cut] = parts[j][...]
        term = _dot(x_ref[:, cut], parts[j][...], NT)
        total = term if total is None else total + term
    for b in range(z.nb):
        out_ref[:, z.block(b)] = total[z.block(b), :].T[z.ranks(b), :]


def projected_kernel(z, info, base_ref, mine_ref, other_ref, up_ref, out_ref, spread):
    spread[...] = jnp.zeros_like(spread)
    for b in range(z.nb):
        cut = z.block(b)
        spread[z.ranks(b), cut] = (mine_ref[:, cut] + other_ref[:, cut]).astype(bf16)
    wide = _dot(spread[...], up_ref[...], TN)
    for b in range(z.nb):
        cut = z.block(b)
        full = base_ref[cut, :] + adapter_scale * wide[cut]
        out_ref[cut, :] = _masked(full, z.valid(info, b)).astype(bf16)


def through_kernel(info, g_ref, w_ref, out_ref):
    half = out_ref.shape[1] // 2
    for h in range(2):
        cut = slice(h * half, (h + 1) * half)
        out_ref[:, cut] = _dot(g_ref[...], w_ref[cut, :], NT)


def tokens_kernel(z, first, ready, info, g_ref, w_ref, mine_ref, other_ref, d_ref, *refs):
    out_ref, spread = refs[-2:]
    step = pl.program_id(0)

    @pl.when(step == 0)
    def _():
        spread[...] = jnp.zeros_like(spread)
        for b in range(z.nb):
            cut = z.block(b)
            v = (mine_ref[:, cut] + other_ref[:, cut]) * adapter_scale
            spread[z.ranks(b), cut] = v.astype(bf16)

    wide = out_ref.shape[1]
    cut = pl.ds(pl.multiple_of((first + step) * wide, wide), wide)
    through = g_ref[:, cut] if ready else _dot(g_ref[...], w_ref[cut, :], NT)
    out_ref[...] = (through + _dot(spread[...], d_ref[:, cut], TN)).astype(bf16)


def on_device(
    n_groups,
    n_dp,
    tokens,
    base_weight,
    adapter_down,
    adapter_up,
    out_cotangent,
    block_tenant,
    block_valid,
    tenant_slot,
):
    nb = block_tenant.shape[0]
    rows, width = tokens.shape
    cols = out_cotangent.shape[1]
    tenants = tenant_slot.shape[0]
    ten_dev, _, rank = adapter_down.shape
    z = Sizes(n_dp, nb, ten_dev, rank, cols, width)
    n_far = z.n_far
    me = lax.axis_index("dp")
    core = lax.axis_index("tensor")
    group = lax.axis_index("groups")
    shared = n_groups == 2 and n_dp == 8
    n_parts = 4 if shared else 1
    mine_q = group * 2 + me % 2 if shared else jnp.int32(0)
    quarter = width // n_parts

    down_t = jnp.swapaxes(adapter_down, 1, 2)
    if shared:
        to_y = lax.dynamic_slice_in_dim(down_t, (mine_q ^ 1) * quarter, quarter, axis=2)
        from_y = _xor(to_y, n_dp, 1)
    far_up = [_xor(adapter_up, n_dp, NEAR * j) for j in range(1, n_far)]
    lane = jnp.arange(LANES, dtype=i32)

    def spread_out(x):
        hit = lane[:, None] == jnp.arange(x.shape[0], dtype=i32)[None, :]
        return jnp.sum(jnp.where(hit, x[None, :], 0), axis=1).astype(i32)

    own_tenants = spread_out(block_tenant)
    tag = jnp.broadcast_to(own_tenants[None, :], (16, LANES)).astype(bf16)
    tag = jnp.pad(tag, ((0, 0), (0, cols - LANES)))
    ups = [u.reshape(ten_dev * rank, cols) for u in [adapter_up] + far_up]
    packet = jnp.concatenate(ups + [tag], axis=0)
    packets = [packet] + [_xor(packet, n_dp, k) for k in range(1, NEAR)]

    if shared:
        own = lax.dynamic_slice_in_dim(down_t, mine_q * quarter, quarter, axis=2)
        shard = jnp.concatenate([own, from_y], axis=0)
        shard_far = _xor(shard, n_dp, 4)

    line = lax.broadcasted_iota(i32, (16, LANES), 0)
    place = jnp.where(lane == 0, me, jnp.where(lane == 1, core, mine_q))
    info = jnp.where(line == 8, place[None, :], spread_out(block_valid)[None, :])
    info = jnp.where(line == 6, spread_out(tenant_slot)[None, :], info)
    info = jnp.where(line == 0, own_tenants[None, :], info)

    base_other = _call(
        functools.partial(other_kernel, z), "base_other", (1,),
        [pl.BlockSpec(memory_space=pl.ANY)] * 2,
        _whole((rows, cols)), _shape((rows, cols), bf16),
        [
            pltpu.VMEM((rows, width), bf16), pltpu.VMEM((width, cols), bf16),
            pltpu.SemaphoreType.DMA((5,)), pltpu.SemaphoreType.DMA((5,)),
        ],
        vmem=BIG_VMEM,
    )(_tie(info, shard if shared else packet), tokens, base_weight)
    base_arrived = _swap(base_other, "tensor")
    packets = [_tie(p, base_other) for p in packets]

    for k in range(1, NEAR):
        info = jnp.where(line == k, packets[k][-16, :LANES].astype(i32)[None, :], info)

    if shared:
        info = _tie(info, shard_far)
        farther = _xor(shard_far, n_dp, 2)

    part = (rank, rows)
    block_up, back_part = _call(
        functools.partial(back_kernel, z), "back", (1,),
        [VMEM] * (1 + NEAR), [VMEM, _whole(part)],
        [_shape((nb * rank, cols), bf16), _shape(part, f32)], [],
    )(info, out_cotangent, *packets)
    back_other = _swap(back_part, "tensor")
    cotangent_other = _swap(_tie(out_cotangent, back_part), "tensor")
    ready = [cotangent_other, base_arrived]
    if shared:
        shard_near = _xor(_tie(shard, base_other), n_dp, 2)
        info_x = _swap(info, "groups")

    packed_rows = n_dp * CAP * rank
    near_rows = packed_rows // NEAR

    def pack(info, start, wide):
        return _call(
            functools.partial(pack_kernel, z, NEAR, start), "pack_down", (1,),
            [VMEM] * 3, [_whole((near_rows, wide))] * NEAR,
            [_shape((near_rows, wide), bf16)] * NEAR,
            [pltpu.VMEM((packed_rows, rows), bf16)],
        )(info, back_part, back_other, tokens)

    def to_near(sends):
        return [sends[0]] + [_xor(sends[k], n_dp, k) for k in range(1, NEAR)]

    def dense(info, got):
        wide = got[0].shape[1]
        out = (ten_dev * rank, wide)
        return _call(
            functools.partial(dense_kernel, z), "dense", (1,),
            [VMEM] * NEAR, [VMEM] + [_whole(out)] * (n_far - 1),
            [_shape(out, f32)] + [_shape(out, bf16)] * (n_far - 1), [],
        )(info, *got)

    def to_far(parts):
        return [parts[0]] + [_xor(parts[j], n_dp, NEAR * j) for j in range(1, n_far)]

    def final(groups):
        wide = sum(g[0].shape[1] for g in groups)
        out = (ten_dev * rank, wide)
        total = _call(
            functools.partial(final_kernel, len(groups), n_far), "final", (1,),
            [VMEM] * (len(groups) * n_far), _whole(out), _shape(out, f32), [],
        )(_tie(info, grad_tokens), *[a for g in groups for a in g])
        return total.reshape(ten_dev, rank, wide)

    half = width // 2
    sends_a = pack(_tie(info, *ready), 0, half)
    got_a = to_near(sends_a)

    if shared:
        block = (nb * rank, quarter)
        chosen = _call(
            functools.partial(choose_kernel, z), "choose", (1,),
            [VMEM] * 4, [_whole(block)] * 4, [_shape(block, bf16)] * 4, [],
            n_scalars=2,
        )(_tie(info, sends_a[0]), info_x, shard, shard_near, shard_far, farther)
        got_y = _xor(_tie(chosen[1], got_a[2]), n_dp, 1)
        got_x = _swap(chosen[2], "groups")
        got_d = lax.ppermute(
            chosen[3],
            ("groups", "dp"),
            [(g * n_dp + d, (1 - g) * n_dp + (d ^ 1)) for g in range(2) for d in range(n_dp)],
        )
        after_choose = chosen[0]
    else:
        every = lax.all_gather(down_t, "dp", axis=0, tiled=True)
        slots = jnp.take(tenant_slot, block_tenant, axis=0)
        got_down = [jnp.take(every, slots, axis=0).reshape(nb * rank, width)]
        after_choose = sends_a[0]

    sends_b = pack(_tie(info, after_choose), half, half)

    base_own, g_full = _call(
        functools.partial(own_kernel, z), "base_own", (1,),
        [VMEM] * 5, [VMEM, VMEM],
        [_shape((rows, cols), f32), _shape((rows, 2 * cols), bf16)], [],
    )(_tie(info, sends_b[0]), tokens, base_weight, base_arrived, out_cotangent, cotangent_other)

    dense_a = dense(_tie(info, base_own), got_a)
    far_a = to_far(dense_a)

    gate = [dense_a[1]] + ([got_y] if shared else [])
    got_b = to_near(
        [_tie(b, *gate) if k in (1, 3) else _tie(b, dense_a[1]) for k, b in enumerate(sends_b)]
    )

    through = _call(
        through_kernel, "through", (1,), [VMEM] * 2, VMEM, _shape((rows, half), f32), [],
    )(_tie(info, dense_a[1]), g_full, base_weight)

    if shared:
        got_down = [chosen[0], got_y, got_x, got_d]
    block_down, shrink_part = _call(
        functools.partial(shrink_kernel, z, n_parts), "shrink", (1,),
        [VMEM] * (1 + n_parts), [VMEM, _whole(part)],
        [_shape((nb * rank, width), bf16), _shape(part, f32)], [],
    )(_tie(info, through), tokens, *got_down)
    shrink_other = _swap(shrink_part, "tensor")

    def token_grads(info, start, wide, step, g, so_far):
        first = start // step
        return _call(
            functools.partial(tokens_kernel, z, first, so_far is None), "token_grads", (wide // step,),
            [VMEM] * 5 + ([] if so_far is None else [pl.BlockSpec(memory_space=pl.ANY)]),
            pl.BlockSpec((rows, step), lambda i, *_: (0, first + i)),
            _shape((rows, width), bf16), [pltpu.VMEM((nb * rank, rows), bf16)],
            None if so_far is None else {6: 0},
        )(
            info, g, g if so_far is None else base_weight, back_part, back_other, block_down,
            *([] if so_far is None else [so_far]),
        )

    grad_tokens = token_grads(_tie(info, shrink_part), 0, half, half // 2, through, None)

    up_sends = _call(
        functools.partial(pack_up_kernel, z, NEAR), "pack_up", (1,),
        [VMEM] * 3, [_whole((near_rows, cols))] * NEAR,
        [_shape((near_rows, cols), bf16)] * NEAR,
        [pltpu.VMEM((packed_rows, rows), bf16)],
    )(_tie(info, grad_tokens), shrink_part, shrink_other, g_full)
    got_u = to_near(up_sends)

    dense_b = dense(_tie(info, up_sends[0]), got_b)
    far_b = to_far(dense_b)

    rest = (width - half) // 2
    grad_tokens = token_grads(
        _tie(info, dense_b[1]), half, rest, rest // 2, g_full, grad_tokens
    )
    projected = _call(
        functools.partial(projected_kernel, z), "projected", (1,),
        [VMEM] * 4, _whole((rows, cols)), _shape((rows, cols), bf16),
        [pltpu.VMEM((nb * rank, rows), bf16)],
    )(_tie(info, grad_tokens), base_own, shrink_part, shrink_other, block_up)
    dense_u = dense(_tie(info, projected), got_u)
    far_u = to_far(dense_u)
    grad_tokens = token_grads(
        _tie(info, dense_u[1]), half + rest, rest, rest // 2, g_full, grad_tokens
    )


    grad_down = jnp.swapaxes(final([far_a, far_b]), 1, 2)
    grad_up = final([far_u])
    return projected, grad_tokens, grad_down, grad_up


def solution(mesh):
    n_groups, n_dp = mesh.shape["groups"], mesh.shape["dp"]
    in_specs = (
        P(("groups", "dp"), "tensor"),
        P("tensor", None),
        P("dp", "tensor", None),
        P("dp", None, "tensor"),
        P(("groups", "dp"), "tensor"),
        P(("groups", "dp")),
        P(("groups", "dp")),
        P("groups"),
    )
    out_specs = (
        P(("groups", "dp"), "tensor"),
        P(("groups", "dp"), "tensor"),
        P(("groups", "dp"), "tensor", None),
        P(("groups", "dp"), None, "tensor"),
    )

    def run(*args):
        return on_device(n_groups, n_dp, *args)

    return jax.shard_map(
        run, mesh=mesh, in_specs=in_specs, out_specs=out_specs, check_vma=False
    )
```

```python
import functools

import jax
import jax.numpy as jnp
from jax import lax
from jax.experimental import pallas as pl
from jax.experimental.pallas import tpu as pltpu
from jax.sharding import PartitionSpec as P

TENANT_BLOCK = 128
CAP = 2
NEAR = 4
VMEM_LIMIT = 9 * 1024 * 1024
BIG_VMEM = 36 * 1024 * 1024
LANES = 128

adapter_scale = 2.0
f32 = jnp.float32
bf16 = jnp.bfloat16
i32 = jnp.int32

NT = (((1,), (1,)), ((), ()))
TN = (((0,), (0,)), ((), ()))
NN = (((1,), (0,)), ((), ()))


def _dot(a, b, dims):
    return lax.dot_general(a, b, dims, preferred_element_type=f32)


def _swap(x, axis):
    return lax.ppermute(x, axis, [(0, 1), (1, 0)])


def _xor(x, n, k):
    return lax.ppermute(x, "dp", [(i, i ^ k) for i in range(n)])


def _tie(x, *after):
    return lax.optimization_barrier((x,) + after)[0]


def _div(a, n):
    return a >> (n.bit_length() - 1) if n & (n - 1) == 0 else lax.div(a, jnp.int32(n))


def _rem(a, n):
    return a & (n - 1) if n & (n - 1) == 0 else lax.rem(a, jnp.int32(n))


VMEM = pl.BlockSpec(memory_space=pltpu.VMEM)


def _shape(shape, dtype):
    return jax.ShapeDtypeStruct(shape, dtype)


def _call(
    body, name, grid, in_specs, out_specs, out_shape, scratch, aliases=None, vmem=VMEM_LIMIT,
    n_scalars=1,
):
    return pl.pallas_call(
        body,
        name=name,
        grid_spec=pltpu.PrefetchScalarGridSpec(
            num_scalar_prefetch=n_scalars,
            grid=grid,
            in_specs=in_specs,
            out_specs=out_specs,
            scratch_shapes=scratch,
        ),
        out_shape=out_shape,
        input_output_aliases=aliases or {},
        compiler_params=pltpu.CompilerParams(vmem_limit_bytes=vmem),
        cost_estimate=pl.CostEstimate(flops=1, bytes_accessed=1, transcendentals=0),
    )


def _whole(shape):
    return pl.BlockSpec(shape, lambda *_: (0,) * len(shape))


class Sizes:
    def __init__(self, n_dp, nb, ten_dev, rank, cols, width):
        self.n_dp, self.nb, self.ten_dev = n_dp, nb, ten_dev
        self.rank, self.cols, self.width = rank, cols, width
        self.n_far = n_dp // NEAR
        self.rows = nb * TENANT_BLOCK
        self.me, self.core, self.quarter = (8, 0), (8, 1), (8, 2)

    def block(self, b):
        return slice(b * TENANT_BLOCK, (b + 1) * TENANT_BLOCK)

    def ranks(self, b):
        return slice(b * self.rank, (b + 1) * self.rank)

    def slot(self, info, which, b):
        return info[6, info[which, b]]

    def valid(self, info, b):
        return info[9, b]

    def owner_and_order(self, info, which):
        owners = [_div(self.slot(info, which, b), self.ten_dev) for b in range(self.nb)]
        orders = []
        for b in range(self.nb):
            n = jnp.int32(0)
            for c in range(b):
                n = n + jnp.where(owners[c] == owners[b], 1, 0)
            orders.append(n)
        return owners, orders

    def places(self, info):
        owners, orders = self.owner_and_order(info, 0)
        out = []
        for o, r in zip(owners, orders):
            rel = o ^ info[self.me]
            place = (_rem(rel, NEAR) * self.n_far + _div(rel, NEAR)) * CAP + r
            out.append(pl.ds(pl.multiple_of(place * self.rank, self.rank), self.rank))
        return out


def _masked(x, valid):
    row = lax.broadcasted_iota(i32, x.shape, 0)
    return jnp.where(row < valid, x, jnp.zeros((), x.dtype))


def base_kernel(
    z, info, x_hbm, w_hbm, g_ref, h_ref, far_ref, own_ref, full_ref, x_ref, w_ref, x_sem, w_sem
):
    own = pl.ds(pl.multiple_of(info[z.core] * z.cols, z.cols), z.cols)
    far = pl.ds(pl.multiple_of((1 - info[z.core]) * z.cols, z.cols), z.cols)
    unit = z.width // 8
    copies = []
    for i, (first, last) in enumerate(((0, 1), (1, 2), (2, 4), (4, 6), (6, 8))):
        cut = pl.ds(first * unit, (last - first) * unit)
        x = pltpu.make_async_copy(x_hbm.at[:, cut], x_ref.at[:, cut], x_sem.at[i])
        w = pltpu.make_async_copy(w_hbm.at[cut], w_ref.at[cut], w_sem.at[i])
        x.start()
        w.start()
        copies.append((x, w, cut))
    for b in range(z.nb):
        cut = z.block(b)
        full_ref[cut, own] = _masked(g_ref[cut, :], z.valid(info, b))
        full_ref[cut, far] = _masked(h_ref[cut, :], z.valid(info, b))
    for x, w, cut in copies:
        x.wait()
        w.wait()
    far_ref[...] = _dot(x_ref[...], w_ref[:, far], NN).astype(bf16)
    own_ref[...] = _dot(x_ref[...], w_ref[:, own], NN)


def back_kernel(z, info, g_ref, *refs):
    packets, (up_ref, part_ref) = refs[:NEAR], refs[NEAR:]
    for b in range(z.nb):
        s = z.slot(info, 0, b)
        rel = _div(s, z.ten_dev) ^ info[z.me]
        at = _div(rel, NEAR) * z.ten_dev + _rem(s, z.ten_dev)
        at = pl.ds(pl.multiple_of(at * z.rank, z.rank), z.rank)
        near = _rem(rel, NEAR)
        u = packets[0][at, :]
        for k in range(1, NEAR):
            u = jnp.where(near == k, packets[k][at, :], u)
        up_ref[z.ranks(b), :] = u
        g = _masked(g_ref[z.block(b), :], z.valid(info, b))
        part_ref[:, z.block(b)] = _dot(u, g, NT)


def pack_kernel(z, n_out, start, info, mine_ref, other_ref, x_ref, *refs):
    outs, packed = refs[:n_out], refs[n_out]
    packed[...] = jnp.zeros_like(packed)
    for b, place in enumerate(z.places(info)):
        cut = z.block(b)
        v = (mine_ref[:, cut] + other_ref[:, cut]) * adapter_scale
        packed[place, cut] = v.astype(bf16)
    wide = outs[0].shape[1]
    res = _dot(packed[...], x_ref[:, start : start + wide], NN).astype(bf16)
    each = res.shape[0] // n_out
    for k in range(n_out):
        outs[k][...] = res[k * each : (k + 1) * each]


def pack_up_kernel(z, n_out, info, mine_ref, other_ref, g_ref, *refs):
    outs, packed = refs[:n_out], refs[n_out]
    own = pl.ds(pl.multiple_of(info[z.core] * z.cols, z.cols), z.cols)
    packed[...] = jnp.zeros_like(packed)
    for b, place in enumerate(z.places(info)):
        cut = z.block(b)
        packed[place, cut] = (mine_ref[:, cut] + other_ref[:, cut]).astype(bf16)
    res = (adapter_scale * _dot(packed[...], g_ref[:, own], NN)).astype(bf16)
    each = res.shape[0] // n_out
    for k in range(n_out):
        outs[k][...] = res[k * each : (k + 1) * each]


def one_hot_sums(z, info, sums_ref):
    n = CAP * z.rank
    shape = (z.ten_dev * z.rank, n)
    row = lax.broadcasted_iota(i32, shape, 0)
    col = lax.broadcasted_iota(i32, shape, 1)
    same = _rem(row, z.rank) == _rem(col, z.rank)
    row_slot = _div(row, z.rank)
    tables = [z.owner_and_order(info, k) for k in range(NEAR)]
    for j in range(z.n_far):
        holder = info[z.me] ^ (NEAR * j)
        parts = []
        for k in range(NEAR):
            owners, orders = tables[k]
            local = []
            for r in range(CAP):
                found = jnp.int32(0)
                for b in range(z.nb):
                    hit = (owners[b] == holder) & (orders[b] == r)
                    found = jnp.where(hit, _rem(z.slot(info, k, b), z.ten_dev), found)
                local.append(found)
            wanted = jnp.where(col < z.rank, local[0], local[1])
            parts.append(jnp.where(same & (row_slot == wanted), 1.0, 0.0))
        sums_ref[j] = jnp.concatenate(parts, axis=1).astype(bf16)


def dense_kernel(z, info, sums_ref, *refs):
    got, near_ref, far_refs = refs[:NEAR], refs[NEAR], refs[NEAR + 1 :]
    n = CAP * z.rank
    for j in range(z.n_far):
        stacked = jnp.concatenate([g[j * n : (j + 1) * n, :] for g in got], axis=0)
        total = _dot(sums_ref[j], stacked, NN)
        if j == 0:
            near_ref[...] = total
        else:
            far_refs[j - 1][...] = total.astype(bf16)


def final_kernel(parts, n_far, info, *refs):
    outs = refs[len(refs) - len(parts) :]
    i = 0
    for n, out in zip(parts, outs):
        at = 0
        for _ in range(n):
            total = refs[i][...]
            for r in refs[i + 1 : i + n_far]:
                total = total + r[...].astype(f32)
            out[:, at : at + total.shape[1]] = total
            at += total.shape[1]
            i += n_far


def choose_kernel(z, info, info_x, own_ref, far_ref, pair_ref, *outs):
    half = own_ref.shape[0]
    sources = (own_ref, pair_ref.at[:half], far_ref, pair_ref.at[half:])
    wanted = ((info, 0), (info, 1), (info_x, 0), (info_x, 1))
    for (table, which), out in zip(wanted, outs):
        for b in range(z.nb):
            s = z.slot(table, which, b)
            rel = _div(s, z.ten_dev) ^ info[z.me]
            at = _rem(rel, 2) * z.ten_dev + _rem(s, z.ten_dev)
            line = _div(rel, 2)
            v = sources[0][at]
            for k in range(1, 4):
                v = jnp.where(line == k, sources[k][at], v)
            out[z.ranks(b), :] = v


def shrink_kernel(z, n_parts, info, x_ref, *refs):
    parts, (full_ref, out_ref) = refs[:n_parts], refs[n_parts:]
    wide = z.width // n_parts
    total = None
    for j in range(n_parts):
        if n_parts == 1:
            cut = slice(0, wide)
        else:
            cut = pl.ds(pl.multiple_of((info[z.quarter] ^ j) * wide, wide), wide)
        full_ref[:, cut] = parts[j][...]
        term = _dot(x_ref[:, cut], parts[j][...], NT)
        total = term if total is None else total + term
    for b in range(z.nb):
        out_ref[:, z.block(b)] = total[z.block(b), :].T[z.ranks(b), :]


def projected_kernel(z, info, base_ref, far_ref, mine_ref, other_ref, up_ref, out_ref, spread):
    spread[...] = jnp.zeros_like(spread)
    for b in range(z.nb):
        cut = z.block(b)
        spread[z.ranks(b), cut] = (mine_ref[:, cut] + other_ref[:, cut]).astype(bf16)
    wide = _dot(spread[...], up_ref[...], TN)
    for b in range(z.nb):
        cut = z.block(b)
        full = base_ref[cut, :] + far_ref[cut, :].astype(f32) + adapter_scale * wide[cut]
        out_ref[cut, :] = _masked(full, z.valid(info, b)).astype(bf16)


def through_kernel(z, first, info, g_ref, w_ref, out_ref, *sums):
    step = out_ref.shape[1] // 4
    for h in range(4):
        cut = slice(h * step, (h + 1) * step)
        rows = slice(first + h * step, first + (h + 1) * step)
        out_ref[:, cut] = _dot(g_ref[...], w_ref[rows, :], NT)
    for s in sums:
        one_hot_sums(z, info, s)


def tokens_kernel(z, info, low_ref, high_ref, mine_ref, other_ref, d_ref, out_ref, spread):
    step = pl.program_id(0)
    wide = out_ref.shape[1]
    per_half = low_ref.shape[1] // wide

    @pl.when(step == 0)
    def _():
        spread[...] = jnp.zeros_like(spread)
        for b in range(z.nb):
            cut = z.block(b)
            v = (mine_ref[:, cut] + other_ref[:, cut]) * adapter_scale
            spread[z.ranks(b), cut] = v.astype(bf16)

    cut = pl.ds(pl.multiple_of(step * wide, wide), wide)
    added = _dot(spread[...], d_ref[:, cut], TN)
    for half, through in enumerate((low_ref, high_ref)):

        @pl.when(step // per_half == half)
        def _():
            here = pl.ds(pl.multiple_of((step - half * per_half) * wide, wide), wide)
            out_ref[...] = (through[:, here] + added).astype(bf16)


def on_device(
    n_groups,
    n_dp,
    tokens,
    base_weight,
    adapter_down,
    adapter_up,
    out_cotangent,
    block_tenant,
    block_valid,
    tenant_slot,
):
    nb = block_tenant.shape[0]
    rows, width = tokens.shape
    cols = out_cotangent.shape[1]
    tenants = tenant_slot.shape[0]
    ten_dev, _, rank = adapter_down.shape
    z = Sizes(n_dp, nb, ten_dev, rank, cols, width)
    n_far = z.n_far
    me = lax.axis_index("dp")
    core = lax.axis_index("tensor")
    group = lax.axis_index("groups")
    shared = n_groups == 2 and n_dp == 8
    n_parts = 4 if shared else 1
    mine_q = group * 2 + me % 2 if shared else jnp.int32(0)
    quarter = width // n_parts

    cotangent_other = _swap(out_cotangent, "tensor")

    down_t = jnp.swapaxes(adapter_down, 1, 2)
    if shared:
        to_y = lax.dynamic_slice_in_dim(down_t, (mine_q ^ 1) * quarter, quarter, axis=2)
        from_y = _xor(to_y, n_dp, 1)
    far_up = [_xor(adapter_up, n_dp, NEAR * j) for j in range(1, n_far)]
    lane = jnp.arange(LANES, dtype=i32)

    def spread_out(x):
        hit = lane[:, None] == jnp.arange(x.shape[0], dtype=i32)[None, :]
        return jnp.sum(jnp.where(hit, x[None, :], 0), axis=1).astype(i32)

    own_tenants = spread_out(block_tenant)
    tag = jnp.broadcast_to(own_tenants[None, :], (16, LANES)).astype(bf16)
    tag = jnp.pad(tag, ((0, 0), (0, cols - LANES)))
    ups = [u.reshape(ten_dev * rank, cols) for u in [adapter_up] + far_up]
    packet = jnp.concatenate(ups + [tag], axis=0)
    packets = [packet] + [_xor(packet, n_dp, k) for k in range(1, NEAR)]

    if shared:
        own = lax.dynamic_slice_in_dim(down_t, mine_q * quarter, quarter, axis=2)
        shard = jnp.concatenate([own, from_y], axis=0)
        shard_far = _xor(shard, n_dp, 4)

    line = lax.broadcasted_iota(i32, (16, LANES), 0)
    place = jnp.where(lane == 0, me, jnp.where(lane == 1, core, mine_q))
    info = jnp.where(line == 8, place[None, :], spread_out(block_valid)[None, :])
    info = jnp.where(line == 6, spread_out(tenant_slot)[None, :], info)
    info = jnp.where(line == 0, own_tenants[None, :], info)

    base_other, base_own, g_full, x_in, w_in = _call(
        functools.partial(base_kernel, z), "base", (1,),
        [pl.BlockSpec(memory_space=pl.ANY)] * 2 + [VMEM] * 2,
        [_whole((rows, cols))] + [VMEM] * 4,
        [
            _shape((rows, cols), bf16), _shape((rows, cols), f32),
            _shape((rows, 2 * cols), bf16), _shape(tokens.shape, bf16),
            _shape(base_weight.shape, bf16),
        ],
        [pltpu.SemaphoreType.DMA((5,)), pltpu.SemaphoreType.DMA((5,))],
        vmem=BIG_VMEM,
    )(
        _tie(info, shard if shared else packet),
        tokens, base_weight, out_cotangent, cotangent_other,
    )
    base_arrived = _swap(base_other, "tensor")
    packets = [_tie(p, base_other) for p in packets]

    for k in range(1, NEAR):
        info = jnp.where(line == k, packets[k][-16, :LANES].astype(i32)[None, :], info)

    if shared:
        shard_far = _tie(shard_far, base_other)
        info = _tie(info, shard_far)
        farther = _xor(jnp.concatenate([shard, shard_far], axis=0), n_dp, 2)

    part = (rank, rows)
    block_up, back_part = _call(
        functools.partial(back_kernel, z), "back", (1,),
        [VMEM] * (1 + NEAR), [VMEM, _whole(part)],
        [_shape((nb * rank, cols), bf16), _shape(part, f32)], [],
    )(info, out_cotangent, *packets)
    back_other = _swap(back_part, "tensor")
    ready = [base_arrived]
    if shared:
        info_x = _swap(info, "groups")
        ready.append(info_x)

    packed_rows = n_dp * CAP * rank
    near_rows = packed_rows // NEAR

    def pack(info, start, wide):
        return _call(
            functools.partial(pack_kernel, z, NEAR, start), "pack_down", (1,),
            [VMEM] * 3, [_whole((near_rows, wide))] * NEAR,
            [_shape((near_rows, wide), bf16)] * NEAR,
            [pltpu.VMEM((packed_rows, rows), bf16)],
        )(info, back_part, back_other, x_in)

    def to_near(sends):
        return [sends[0]] + [_xor(sends[k], n_dp, k) for k in range(1, NEAR)]

    def dense(info, got):
        wide = got[0].shape[1]
        out = (ten_dev * rank, wide)
        return _call(
            functools.partial(dense_kernel, z), "dense", (1,),
            [VMEM] * (1 + NEAR), [VMEM] + [_whole(out)] * (n_far - 1),
            [_shape(out, f32)] + [_shape(out, bf16)] * (n_far - 1), [],
        )(info, sums, *got)

    def to_far(parts):
        return [parts[0]] + [_xor(parts[j], n_dp, NEAR * j) for j in range(1, n_far)]

    def through(info, first, wide, with_sums):
        sums = _shape((n_far, ten_dev * rank, NEAR * CAP * rank), bf16)
        return _call(
            functools.partial(through_kernel, z, first), "through", (1,), [VMEM] * 2,
            [VMEM] * (1 + with_sums), [_shape((rows, wide), f32)] + [sums] * with_sums, [],
        )(info, g_full, w_in)

    half = width // 2
    wide_a = width * 5 // 8
    sends_a = pack(_tie(info, *ready), 0, wide_a)
    got_a = to_near(sends_a)

    low, sums = through(_tie(info, sends_a[0]), 0, half, 1)

    if shared:
        block = (nb * rank, quarter)
        chosen = _call(
            functools.partial(choose_kernel, z), "choose", (1,),
            [VMEM] * 3, [_whole(block)] * 4, [_shape(block, bf16)] * 4, [],
            n_scalars=2,
        )(_tie(info, low), info_x, shard, shard_far, farther)
        got_y = _xor(_tie(chosen[1], got_a[2]), n_dp, 1)
        got_x = _swap(chosen[2], "groups")
        got_d = lax.ppermute(
            chosen[3],
            ("groups", "dp"),
            [(g * n_dp + d, (1 - g) * n_dp + (d ^ 1)) for g in range(2) for d in range(n_dp)],
        )
        after_choose = chosen[0]
    else:
        every = lax.all_gather(down_t, "dp", axis=0, tiled=True)
        slots = jnp.take(tenant_slot, block_tenant, axis=0)
        got_down = [jnp.take(every, slots, axis=0).reshape(nb * rank, width)]
        after_choose = low

    sends_b = pack(_tie(info, after_choose), wide_a, width - wide_a)

    dense_a = dense(_tie(info, sends_b[0]), got_a)
    far_a = to_far(dense_a)

    gate = [dense_a[1]] + ([got_y] if shared else [])
    got_b = to_near(
        [_tie(b, *gate) if k in (1, 3) else _tie(b, dense_a[1]) for k, b in enumerate(sends_b)]
    )

    (high,) = through(_tie(info, dense_a[1]), half, width - half, 0)

    if shared:
        got_down = [chosen[0], got_y, got_x, got_d]
    block_down, shrink_part = _call(
        functools.partial(shrink_kernel, z, n_parts), "shrink", (1,),
        [VMEM] * (1 + n_parts), [VMEM, _whole(part)],
        [_shape((nb * rank, width), bf16), _shape(part, f32)], [],
    )(_tie(info, high), x_in, *got_down)
    shrink_other = _swap(shrink_part, "tensor")

    step = min(512, width // 8)
    grad_tokens = _call(
        functools.partial(tokens_kernel, z), "token_grads", (width // step,),
        [VMEM] * 5, pl.BlockSpec((rows, step), lambda i, *_: (0, i)),
        _shape((rows, width), bf16), [pltpu.VMEM((nb * rank, rows), bf16)],
    )(_tie(info, shrink_part), low, high, back_part, back_other, block_down)

    up_sends = _call(
        functools.partial(pack_up_kernel, z, NEAR), "pack_up", (1,),
        [VMEM] * 3, [_whole((near_rows, cols))] * NEAR,
        [_shape((near_rows, cols), bf16)] * NEAR,
        [pltpu.VMEM((packed_rows, rows), bf16)],
    )(_tie(info, grad_tokens), shrink_part, shrink_other, g_full)
    got_u = to_near(up_sends)

    dense_b = dense(_tie(info, up_sends[0]), got_b)
    far_b = to_far(dense_b)

    projected = _call(
        functools.partial(projected_kernel, z), "projected", (1,),
        [VMEM] * 5, _whole((rows, cols)), _shape((rows, cols), bf16),
        [pltpu.VMEM((nb * rank, rows), bf16)],
    )(
        _tie(info, dense_b[1]),
        base_own, base_arrived, shrink_part, shrink_other, block_up,
    )
    dense_u = dense(_tie(info, projected), got_u)
    far_u = to_far(dense_u)

    outs = [(ten_dev * rank, width), (ten_dev * rank, cols)]
    grad_down, grad_up = _call(
        functools.partial(final_kernel, (2, 1), n_far), "final", (1,),
        [VMEM] * (3 * n_far), [_whole(o) for o in outs], [_shape(o, f32) for o in outs], [],
    )(info, *far_a, *far_b, *far_u)
    grad_down = jnp.swapaxes(grad_down.reshape(ten_dev, rank, width), 1, 2)
    return projected, grad_tokens, grad_down, grad_up.reshape(ten_dev, rank, cols)


def solution(mesh):
    n_groups, n_dp = mesh.shape["groups"], mesh.shape["dp"]
    in_specs = (
        P(("groups", "dp"), "tensor"),
        P("tensor", None),
        P("dp", "tensor", None),
        P("dp", None, "tensor"),
        P(("groups", "dp"), "tensor"),
        P(("groups", "dp")),
        P(("groups", "dp")),
        P("groups"),
    )
    out_specs = (
        P(("groups", "dp"), "tensor"),
        P(("groups", "dp"), "tensor"),
        P(("groups", "dp"), "tensor", None),
        P(("groups", "dp"), None, "tensor"),
    )

    def run(*args):
        return on_device(n_groups, n_dp, *args)

    return jax.shard_map(
        run, mesh=mesh, in_specs=in_specs, out_specs=out_specs, check_vma=False
    )
```

```python
import functools

import jax
import jax.numpy as jnp
from jax import lax
from jax.experimental import pallas as pl
from jax.experimental.pallas import tpu as pltpu
from jax.sharding import PartitionSpec as P

TENANT_BLOCK = 128
CAP = 2
NEAR = 4
VMEM_LIMIT = 9 * 1024 * 1024
BIG_VMEM = 36 * 1024 * 1024
LANES = 128

adapter_scale = 2.0
f32 = jnp.float32
bf16 = jnp.bfloat16
i32 = jnp.int32

NT = (((1,), (1,)), ((), ()))
TN = (((0,), (0,)), ((), ()))
NN = (((1,), (0,)), ((), ()))


def _dot(a, b, dims):
    return lax.dot_general(a, b, dims, preferred_element_type=f32)


def _swap(x, axis):
    return lax.ppermute(x, axis, [(0, 1), (1, 0)])


def _xor(x, n, k):
    return lax.ppermute(x, "dp", [(i, i ^ k) for i in range(n)])


def _tie(x, *after):
    return lax.optimization_barrier((x,) + after)[0]


def _div(a, n):
    return a >> (n.bit_length() - 1) if n & (n - 1) == 0 else lax.div(a, jnp.int32(n))


def _rem(a, n):
    return a & (n - 1) if n & (n - 1) == 0 else lax.rem(a, jnp.int32(n))


VMEM = pl.BlockSpec(memory_space=pltpu.VMEM)


def _shape(shape, dtype):
    return jax.ShapeDtypeStruct(shape, dtype)


def _call(
    body, name, grid, in_specs, out_specs, out_shape, scratch, aliases=None, vmem=VMEM_LIMIT,
    n_scalars=1,
):
    return pl.pallas_call(
        body,
        name=name,
        grid_spec=pltpu.PrefetchScalarGridSpec(
            num_scalar_prefetch=n_scalars,
            grid=grid,
            in_specs=in_specs,
            out_specs=out_specs,
            scratch_shapes=scratch,
        ),
        out_shape=out_shape,
        input_output_aliases=aliases or {},
        compiler_params=pltpu.CompilerParams(vmem_limit_bytes=vmem),
        cost_estimate=pl.CostEstimate(flops=1, bytes_accessed=1, transcendentals=0),
    )


def _whole(shape):
    return pl.BlockSpec(shape, lambda *_: (0,) * len(shape))


class Sizes:
    def __init__(self, n_dp, nb, ten_dev, rank, cols, width):
        self.n_dp, self.nb, self.ten_dev = n_dp, nb, ten_dev
        self.rank, self.cols, self.width = rank, cols, width
        self.n_far = n_dp // NEAR
        self.rows = nb * TENANT_BLOCK
        self.me, self.core, self.quarter = (8, 0), (8, 1), (8, 2)

    def block(self, b):
        return slice(b * TENANT_BLOCK, (b + 1) * TENANT_BLOCK)

    def ranks(self, b):
        return slice(b * self.rank, (b + 1) * self.rank)

    def slot(self, info, which, b):
        return info[6, info[which, b]]

    def valid(self, info, b):
        return info[9, b]

    def owner_and_order(self, info, which):
        owners = [_div(self.slot(info, which, b), self.ten_dev) for b in range(self.nb)]
        orders = []
        for b in range(self.nb):
            n = jnp.int32(0)
            for c in range(b):
                n = n + jnp.where(owners[c] == owners[b], 1, 0)
            orders.append(n)
        return owners, orders

    def places(self, info):
        owners, orders = self.owner_and_order(info, 0)
        out = []
        for o, r in zip(owners, orders):
            rel = o ^ info[self.me]
            place = (_rem(rel, NEAR) * self.n_far + _div(rel, NEAR)) * CAP + r
            out.append(pl.ds(pl.multiple_of(place * self.rank, self.rank), self.rank))
        return out


def _masked(x, valid):
    row = lax.broadcasted_iota(i32, x.shape, 0)
    return jnp.where(row < valid, x, jnp.zeros((), x.dtype))


def base_kernel(
    z, info, x_hbm, w_hbm, g_ref, h_ref, far_ref, full_ref, x_ref, w_ref, x_sem, w_sem
):
    own = pl.ds(pl.multiple_of(info[z.core] * z.cols, z.cols), z.cols)
    far = pl.ds(pl.multiple_of((1 - info[z.core]) * z.cols, z.cols), z.cols)
    unit = z.width // 8
    copies = []
    for i, (first, last) in enumerate(((0, 1), (1, 3), (3, 5), (5, 7), (7, 8))):
        cut = pl.ds(first * unit, (last - first) * unit)
        x = pltpu.make_async_copy(x_hbm.at[:, cut], x_ref.at[:, cut], x_sem.at[i])
        w = pltpu.make_async_copy(w_hbm.at[cut], w_ref.at[cut], w_sem.at[i])
        x.start()
        w.start()
        copies.append((x, w, cut))
    for b in range(z.nb):
        cut = z.block(b)
        full_ref[cut, own] = _masked(g_ref[cut, :], z.valid(info, b))
        full_ref[cut, far] = _masked(h_ref[cut, :], z.valid(info, b))
    total = None
    for x, w, cut in copies:
        x.wait()
        w.wait()
        term = _dot(x_ref[:, cut], w_ref[cut, far], NN)
        total = term if total is None else total + term
    far_ref[...] = total.astype(bf16)


def own_kernel(z, info, x_ref, w_ref, far_ref, out_ref):
    own = pl.ds(pl.multiple_of(info[z.core] * z.cols, z.cols), z.cols)
    out_ref[...] = _dot(x_ref[...], w_ref[:, own], NN) + far_ref[...].astype(f32)


def back_kernel(z, info, g_ref, *refs):
    packets, (up_ref, part_ref) = refs[:NEAR], refs[NEAR:]
    for b in range(z.nb):
        s = z.slot(info, 0, b)
        rel = _div(s, z.ten_dev) ^ info[z.me]
        at = _div(rel, NEAR) * z.ten_dev + _rem(s, z.ten_dev)
        at = pl.ds(pl.multiple_of(at * z.rank, z.rank), z.rank)
        near = _rem(rel, NEAR)
        u = packets[0][at, :]
        for k in range(1, NEAR):
            u = jnp.where(near == k, packets[k][at, :], u)
        up_ref[z.ranks(b), :] = u
        g = _masked(g_ref[z.block(b), :], z.valid(info, b))
        part_ref[:, z.block(b)] = _dot(u, g, NT)


def pack_kernel(z, n_out, start, info, mine_ref, other_ref, x_ref, *refs):
    outs, packed = refs[:n_out], refs[n_out]
    packed[...] = jnp.zeros_like(packed)
    for b, place in enumerate(z.places(info)):
        cut = z.block(b)
        v = (mine_ref[:, cut] + other_ref[:, cut]) * adapter_scale
        packed[place, cut] = v.astype(bf16)
    wide = outs[0].shape[1]
    res = _dot(packed[...], x_ref[:, start : start + wide], NN).astype(bf16)
    each = res.shape[0] // n_out
    for k in range(n_out):
        outs[k][...] = res[k * each : (k + 1) * each]


def pack_up_kernel(z, n_out, info, mine_ref, other_ref, g_ref, *refs):
    outs, packed = refs[:n_out], refs[n_out]
    own = pl.ds(pl.multiple_of(info[z.core] * z.cols, z.cols), z.cols)
    packed[...] = jnp.zeros_like(packed)
    for b, place in enumerate(z.places(info)):
        cut = z.block(b)
        packed[place, cut] = (mine_ref[:, cut] + other_ref[:, cut]).astype(bf16)
    res = (adapter_scale * _dot(packed[...], g_ref[:, own], NN)).astype(bf16)
    each = res.shape[0] // n_out
    for k in range(n_out):
        outs[k][...] = res[k * each : (k + 1) * each]


def one_hot_sums(z, info, sums_ref):
    n = CAP * z.rank
    shape = (z.ten_dev * z.rank, n)
    row = lax.broadcasted_iota(i32, shape, 0)
    col = lax.broadcasted_iota(i32, shape, 1)
    same = _rem(row, z.rank) == _rem(col, z.rank)
    row_slot = _div(row, z.rank)
    tables = [z.owner_and_order(info, k) for k in range(NEAR)]
    for j in range(z.n_far):
        holder = info[z.me] ^ (NEAR * j)
        parts = []
        for k in range(NEAR):
            owners, orders = tables[k]
            local = []
            for r in range(CAP):
                found = jnp.int32(0)
                for b in range(z.nb):
                    hit = (owners[b] == holder) & (orders[b] == r)
                    found = jnp.where(hit, _rem(z.slot(info, k, b), z.ten_dev), found)
                local.append(found)
            wanted = jnp.where(col < z.rank, local[0], local[1])
            parts.append(jnp.where(same & (row_slot == wanted), 1.0, 0.0))
        sums_ref[j] = jnp.concatenate(parts, axis=1).astype(bf16)


def dense_kernel(z, info, sums_ref, *refs):
    got, near_ref, far_refs = refs[:NEAR], refs[NEAR], refs[NEAR + 1 :]
    n = CAP * z.rank
    for j in range(z.n_far):
        stacked = jnp.concatenate([g[j * n : (j + 1) * n, :] for g in got], axis=0)
        total = _dot(sums_ref[j], stacked, NN)
        if j == 0:
            near_ref[...] = total
        else:
            far_refs[j - 1][...] = total.astype(bf16)


def final_kernel(parts, n_far, info, *refs):
    outs = refs[len(refs) - len(parts) :]
    i = 0
    for n, out in zip(parts, outs):
        at = 0
        for _ in range(n):
            total = refs[i][...]
            for r in refs[i + 1 : i + n_far]:
                total = total + r[...].astype(f32)
            out[:, at : at + total.shape[1]] = total
            at += total.shape[1]
            i += n_far


def choose_kernel(z, info, info_x, own_ref, far_ref, pair_ref, *outs):
    half = own_ref.shape[0]
    sources = (own_ref, pair_ref.at[:half], far_ref, pair_ref.at[half:])
    wanted = ((info, 0), (info, 1), (info_x, 0), (info_x, 1))
    for (table, which), out in zip(wanted, outs):
        for b in range(z.nb):
            s = z.slot(table, which, b)
            rel = _div(s, z.ten_dev) ^ info[z.me]
            at = _rem(rel, 2) * z.ten_dev + _rem(s, z.ten_dev)
            line = _div(rel, 2)
            v = sources[0][at]
            for k in range(1, 4):
                v = jnp.where(line == k, sources[k][at], v)
            out[z.ranks(b), :] = v


def shrink_kernel(z, n_parts, info, x_ref, *refs):
    parts, (full_ref, out_ref) = refs[:n_parts], refs[n_parts:]
    wide = z.width // n_parts
    total = None
    for j in range(n_parts):
        if n_parts == 1:
            cut = slice(0, wide)
        else:
            cut = pl.ds(pl.multiple_of((info[z.quarter] ^ j) * wide, wide), wide)
        full_ref[:, cut] = parts[j][...]
        term = _dot(x_ref[:, cut], parts[j][...], NT)
        total = term if total is None else total + term
    for b in range(z.nb):
        out_ref[:, z.block(b)] = total[z.block(b), :].T[z.ranks(b), :]


def projected_kernel(z, info, base_ref, mine_ref, other_ref, up_ref, out_ref, spread):
    spread[...] = jnp.zeros_like(spread)
    for b in range(z.nb):
        cut = z.block(b)
        spread[z.ranks(b), cut] = (mine_ref[:, cut] + other_ref[:, cut]).astype(bf16)
    wide = _dot(spread[...], up_ref[...], TN)
    for b in range(z.nb):
        cut = z.block(b)
        full = base_ref[cut, :] + adapter_scale * wide[cut]
        out_ref[cut, :] = _masked(full, z.valid(info, b)).astype(bf16)


def through_kernel(z, first, info, g_ref, w_ref, out_ref, *sums):
    step = out_ref.shape[1] // 4
    for h in range(4):
        cut = slice(h * step, (h + 1) * step)
        rows = slice(first + h * step, first + (h + 1) * step)
        out_ref[:, cut] = _dot(g_ref[...], w_ref[rows, :], NT)
    for s in sums:
        one_hot_sums(z, info, s)


def tokens_kernel(z, info, low_ref, high_ref, mine_ref, other_ref, d_ref, out_ref, spread):
    step = pl.program_id(0)
    wide = out_ref.shape[1]
    per_half = low_ref.shape[1] // wide

    @pl.when(step == 0)
    def _():
        spread[...] = jnp.zeros_like(spread)
        for b in range(z.nb):
            cut = z.block(b)
            v = (mine_ref[:, cut] + other_ref[:, cut]) * adapter_scale
            spread[z.ranks(b), cut] = v.astype(bf16)

    cut = pl.ds(pl.multiple_of(step * wide, wide), wide)
    added = _dot(spread[...], d_ref[:, cut], TN)
    for half, through in enumerate((low_ref, high_ref)):

        @pl.when(step // per_half == half)
        def _():
            here = pl.ds(pl.multiple_of((step - half * per_half) * wide, wide), wide)
            out_ref[...] = (through[:, here] + added).astype(bf16)


def on_device(
    n_groups,
    n_dp,
    tokens,
    base_weight,
    adapter_down,
    adapter_up,
    out_cotangent,
    block_tenant,
    block_valid,
    tenant_slot,
):
    nb = block_tenant.shape[0]
    rows, width = tokens.shape
    cols = out_cotangent.shape[1]
    tenants = tenant_slot.shape[0]
    ten_dev, _, rank = adapter_down.shape
    z = Sizes(n_dp, nb, ten_dev, rank, cols, width)
    n_far = z.n_far
    me = lax.axis_index("dp")
    core = lax.axis_index("tensor")
    group = lax.axis_index("groups")
    shared = n_groups == 2 and n_dp == 8
    n_parts = 4 if shared else 1
    mine_q = group * 2 + me % 2 if shared else jnp.int32(0)
    quarter = width // n_parts

    cotangent_other = _swap(out_cotangent, "tensor")

    down_t = jnp.swapaxes(adapter_down, 1, 2)
    if shared:
        to_y = lax.dynamic_slice_in_dim(down_t, (mine_q ^ 1) * quarter, quarter, axis=2)
        from_y = _xor(to_y, n_dp, 1)
    far_up = [_xor(adapter_up, n_dp, NEAR * j) for j in range(1, n_far)]
    lane = jnp.arange(LANES, dtype=i32)

    def spread_out(x):
        hit = lane[:, None] == jnp.arange(x.shape[0], dtype=i32)[None, :]
        return jnp.sum(jnp.where(hit, x[None, :], 0), axis=1).astype(i32)

    own_tenants = spread_out(block_tenant)
    tag = jnp.broadcast_to(own_tenants[None, :], (16, LANES)).astype(bf16)
    tag = jnp.pad(tag, ((0, 0), (0, cols - LANES)))
    ups = [u.reshape(ten_dev * rank, cols) for u in [adapter_up] + far_up]
    packet = jnp.concatenate(ups + [tag], axis=0)
    packets = [packet] + [_xor(packet, n_dp, k) for k in range(1, NEAR)]

    if shared:
        own = lax.dynamic_slice_in_dim(down_t, mine_q * quarter, quarter, axis=2)
        shard = jnp.concatenate([own, from_y], axis=0)
        shard_far = _xor(shard, n_dp, 4)

    line = lax.broadcasted_iota(i32, (16, LANES), 0)
    place = jnp.where(lane == 0, me, jnp.where(lane == 1, core, mine_q))
    info = jnp.where(line == 8, place[None, :], spread_out(block_valid)[None, :])
    info = jnp.where(line == 6, spread_out(tenant_slot)[None, :], info)
    info = jnp.where(line == 0, own_tenants[None, :], info)

    base_other, g_full, x_in, w_in = _call(
        functools.partial(base_kernel, z), "base", (1,),
        [pl.BlockSpec(memory_space=pl.ANY)] * 2 + [VMEM] * 2,
        [_whole((rows, cols))] + [VMEM] * 3,
        [
            _shape((rows, cols), bf16), _shape((rows, 2 * cols), bf16), _shape(tokens.shape, bf16),
            _shape(base_weight.shape, bf16),
        ],
        [pltpu.SemaphoreType.DMA((5,)), pltpu.SemaphoreType.DMA((5,))],
        vmem=BIG_VMEM,
    )(
        _tie(info, shard if shared else packet),
        tokens, base_weight, out_cotangent, cotangent_other,
    )
    base_arrived = _swap(base_other, "tensor")
    packets = [_tie(p, base_other) for p in packets]

    for k in range(1, NEAR):
        info = jnp.where(line == k, packets[k][-16, :LANES].astype(i32)[None, :], info)

    if shared:
        shard_far = _tie(shard_far, base_other)
        info = _tie(info, shard_far)
        farther = _xor(jnp.concatenate([shard, shard_far], axis=0), n_dp, 2)

    part = (rank, rows)
    block_up, back_part = _call(
        functools.partial(back_kernel, z), "back", (1,),
        [VMEM] * (1 + NEAR), [VMEM, _whole(part)],
        [_shape((nb * rank, cols), bf16), _shape(part, f32)], [],
    )(info, out_cotangent, *packets)
    back_other = _swap(back_part, "tensor")
    ready = [base_arrived]
    if shared:
        info_x = _swap(info, "groups")

    packed_rows = n_dp * CAP * rank
    near_rows = packed_rows // NEAR

    def pack(info, start, wide):
        return _call(
            functools.partial(pack_kernel, z, NEAR, start), "pack_down", (1,),
            [VMEM] * 3, [_whole((near_rows, wide))] * NEAR,
            [_shape((near_rows, wide), bf16)] * NEAR,
            [pltpu.VMEM((packed_rows, rows), bf16)],
        )(info, back_part, back_other, x_in)

    def to_near(sends):
        return [sends[0]] + [_xor(sends[k], n_dp, k) for k in range(1, NEAR)]

    def dense(info, got):
        wide = got[0].shape[1]
        out = (ten_dev * rank, wide)
        return _call(
            functools.partial(dense_kernel, z), "dense", (1,),
            [VMEM] * (1 + NEAR), [VMEM] + [_whole(out)] * (n_far - 1),
            [_shape(out, f32)] + [_shape(out, bf16)] * (n_far - 1), [],
        )(info, sums, *got)

    def to_far(parts):
        return [parts[0]] + [_xor(parts[j], n_dp, NEAR * j) for j in range(1, n_far)]

    def through(info, first, wide, with_sums):
        sums = _shape((n_far, ten_dev * rank, NEAR * CAP * rank), bf16)
        return _call(
            functools.partial(through_kernel, z, first), "through", (1,), [VMEM] * 2,
            [VMEM] * (1 + with_sums), [_shape((rows, wide), f32)] + [sums] * with_sums, [],
        )(info, g_full, w_in)

    half = width // 2
    wide_a = half
    sends_a = pack(_tie(info, *ready), 0, wide_a)
    low, sums = through(_tie(info, sends_a[0]), 0, half, 1)

    if shared:
        block = (nb * rank, quarter)
        chosen = _call(
            functools.partial(choose_kernel, z), "choose", (1,),
            [VMEM] * 3, [_whole(block)] * 4, [_shape(block, bf16)] * 4, [],
            n_scalars=2,
        )(_tie(info, low), info_x, shard, shard_far, farther)
        got_y = _xor(chosen[1], n_dp, 1)
        got_x = _swap(chosen[2], "groups")
        got_d = lax.ppermute(
            chosen[3],
            ("groups", "dp"),
            [(g * n_dp + d, (1 - g) * n_dp + (d ^ 1)) for g in range(2) for d in range(n_dp)],
        )
        after_choose = chosen[0]
    else:
        every = lax.all_gather(down_t, "dp", axis=0, tiled=True)
        slots = jnp.take(tenant_slot, block_tenant, axis=0)
        got_down = [jnp.take(every, slots, axis=0).reshape(nb * rank, width)]
        after_choose = low

    sends_b = pack(_tie(info, after_choose), wide_a, width - wide_a)

    got_a = [sends_a[0], None] + [_xor(sends_a[k], n_dp, k) for k in range(2, NEAR)]
    got_a[1] = _xor(_tie(sends_a[1], sends_b[0], got_a[2]), n_dp, 1)

    base_own = _call(
        functools.partial(own_kernel, z), "base_own", (1,),
        [VMEM] * 3, VMEM, _shape((rows, cols), f32), [],
    )(_tie(info, sends_b[0]), x_in, w_in, base_arrived)
    (high,) = through(_tie(info, base_own), half, width - half, 0)

    if shared:
        got_down = [chosen[0], got_y, got_x, got_d]
    block_down, shrink_part = _call(
        functools.partial(shrink_kernel, z, n_parts), "shrink", (1,),
        [VMEM] * (1 + n_parts), [VMEM, _whole(part)],
        [_shape((nb * rank, width), bf16), _shape(part, f32)], [],
    )(_tie(info, high), x_in, *got_down)
    shrink_other = _swap(shrink_part, "tensor")

    dense_a = dense(_tie(info, shrink_part), got_a)
    far_a = to_far(dense_a)
    got_b = to_near([_tie(b, shrink_part) for b in sends_b])

    step = min(512, width // 8)
    grad_tokens = _call(
        functools.partial(tokens_kernel, z), "token_grads", (width // step,),
        [VMEM] * 5, pl.BlockSpec((rows, step), lambda i, *_: (0, i)),
        _shape((rows, width), bf16), [pltpu.VMEM((nb * rank, rows), bf16)],
    )(_tie(info, dense_a[1]), low, high, back_part, back_other, block_down)

    up_sends = _call(
        functools.partial(pack_up_kernel, z, NEAR), "pack_up", (1,),
        [VMEM] * 3, [_whole((near_rows, cols))] * NEAR,
        [_shape((near_rows, cols), bf16)] * NEAR,
        [pltpu.VMEM((packed_rows, rows), bf16)],
    )(_tie(info, grad_tokens), shrink_part, shrink_other, g_full)
    got_u = to_near(up_sends)

    dense_b = dense(_tie(info, up_sends[0]), got_b)
    far_b = to_far(dense_b)

    projected = _call(
        functools.partial(projected_kernel, z), "projected", (1,),
        [VMEM] * 4, _whole((rows, cols)), _shape((rows, cols), bf16),
        [pltpu.VMEM((nb * rank, rows), bf16)],
    )(
        _tie(info, dense_b[1]),
        base_own, shrink_part, shrink_other, block_up,
    )
    dense_u = dense(_tie(info, projected), got_u)
    far_u = to_far(dense_u)

    outs = [(ten_dev * rank, width), (ten_dev * rank, cols)]
    grad_down, grad_up = _call(
        functools.partial(final_kernel, (2, 1), n_far), "final", (1,),
        [VMEM] * (3 * n_far), [_whole(o) for o in outs], [_shape(o, f32) for o in outs], [],
    )(info, *far_a, *far_b, *far_u)
    grad_down = jnp.swapaxes(grad_down.reshape(ten_dev, rank, width), 1, 2)
    return projected, grad_tokens, grad_down, grad_up.reshape(ten_dev, rank, cols)


def solution(mesh):
    n_groups, n_dp = mesh.shape["groups"], mesh.shape["dp"]
    in_specs = (
        P(("groups", "dp"), "tensor"),
        P("tensor", None),
        P("dp", "tensor", None),
        P("dp", None, "tensor"),
        P(("groups", "dp"), "tensor"),
        P(("groups", "dp")),
        P(("groups", "dp")),
        P("groups"),
    )
    out_specs = (
        P(("groups", "dp"), "tensor"),
        P(("groups", "dp"), "tensor"),
        P(("groups", "dp"), "tensor", None),
        P(("groups", "dp"), None, "tensor"),
    )

    def run(*args):
        return on_device(n_groups, n_dp, *args)

    return jax.shard_map(
        run, mesh=mesh, in_specs=in_specs, out_specs=out_specs, check_vma=False
    )
```

```python
import functools

import jax
import jax.numpy as jnp
from jax import lax
from jax.experimental import pallas as pl
from jax.experimental.pallas import tpu as pltpu
from jax.sharding import PartitionSpec as P

TENANT_BLOCK = 128
CAP = 2
NEAR = 4
VMEM_LIMIT = 9 * 1024 * 1024
BIG_VMEM = 36 * 1024 * 1024
LANES = 128

adapter_scale = 2.0
f32 = jnp.float32
bf16 = jnp.bfloat16
i32 = jnp.int32

NT = (((1,), (1,)), ((), ()))
TN = (((0,), (0,)), ((), ()))
NN = (((1,), (0,)), ((), ()))


def _dot(a, b, dims):
    return lax.dot_general(a, b, dims, preferred_element_type=f32)


def _swap(x, axis):
    return lax.ppermute(x, axis, [(0, 1), (1, 0)])


def _xor(x, n, k):
    return lax.ppermute(x, "dp", [(i, i ^ k) for i in range(n)])


def _tie(x, *after):
    return lax.optimization_barrier((x,) + after)[0]


def _div(a, n):
    return a >> (n.bit_length() - 1) if n & (n - 1) == 0 else lax.div(a, jnp.int32(n))


def _rem(a, n):
    return a & (n - 1) if n & (n - 1) == 0 else lax.rem(a, jnp.int32(n))


VMEM = pl.BlockSpec(memory_space=pltpu.VMEM)


def _shape(shape, dtype):
    return jax.ShapeDtypeStruct(shape, dtype)


def _call(
    body, name, grid, in_specs, out_specs, out_shape, scratch, aliases=None, vmem=VMEM_LIMIT,
    n_scalars=1,
):
    return pl.pallas_call(
        body,
        name=name,
        grid_spec=pltpu.PrefetchScalarGridSpec(
            num_scalar_prefetch=n_scalars,
            grid=grid,
            in_specs=in_specs,
            out_specs=out_specs,
            scratch_shapes=scratch,
        ),
        out_shape=out_shape,
        input_output_aliases=aliases or {},
        compiler_params=pltpu.CompilerParams(vmem_limit_bytes=vmem),
        cost_estimate=pl.CostEstimate(flops=1, bytes_accessed=1, transcendentals=0),
    )


def _whole(shape):
    return pl.BlockSpec(shape, lambda *_: (0,) * len(shape))


class Sizes:
    def __init__(self, n_dp, nb, ten_dev, rank, cols, width):
        self.n_dp, self.nb, self.ten_dev = n_dp, nb, ten_dev
        self.rank, self.cols, self.width = rank, cols, width
        self.n_far = n_dp // NEAR
        self.rows = nb * TENANT_BLOCK
        self.me, self.core, self.quarter = (8, 0), (8, 1), (8, 2)

    def block(self, b):
        return slice(b * TENANT_BLOCK, (b + 1) * TENANT_BLOCK)

    def ranks(self, b):
        return slice(b * self.rank, (b + 1) * self.rank)

    def slot(self, info, which, b):
        return info[6, info[which, b]]

    def valid(self, info, b):
        return info[9, b]

    def owner_and_order(self, info, which):
        owners = [_div(self.slot(info, which, b), self.ten_dev) for b in range(self.nb)]
        orders = []
        for b in range(self.nb):
            n = jnp.int32(0)
            for c in range(b):
                n = n + jnp.where(owners[c] == owners[b], 1, 0)
            orders.append(n)
        return owners, orders

    def places(self, info):
        owners, orders = self.owner_and_order(info, 0)
        out = []
        for o, r in zip(owners, orders):
            rel = o ^ info[self.me]
            place = (_rem(rel, NEAR) * self.n_far + _div(rel, NEAR)) * CAP + r
            out.append(pl.ds(pl.multiple_of(place * self.rank, self.rank), self.rank))
        return out


def _masked(x, valid):
    row = lax.broadcasted_iota(i32, x.shape, 0)
    return jnp.where(row < valid, x, jnp.zeros((), x.dtype))


def base_kernel(
    z, info, x_hbm, w_hbm, g_ref, h_ref, far_ref, full_ref, x_ref, w_ref, x_sem, w_sem
):
    own = pl.ds(pl.multiple_of(info[z.core] * z.cols, z.cols), z.cols)
    far = pl.ds(pl.multiple_of((1 - info[z.core]) * z.cols, z.cols), z.cols)
    unit = z.width // 8
    copies = []
    for i, (first, last) in enumerate(((0, 1), (1, 3), (3, 5), (5, 7), (7, 8))):
        cut = pl.ds(first * unit, (last - first) * unit)
        x = pltpu.make_async_copy(x_hbm.at[:, cut], x_ref.at[:, cut], x_sem.at[i])
        w = pltpu.make_async_copy(w_hbm.at[cut, far], w_ref.at[cut], w_sem.at[i])
        x.start()
        w.start()
        copies.append((x, w, cut))
    for b in range(z.nb):
        cut = z.block(b)
        full_ref[cut, own] = _masked(g_ref[cut, :], z.valid(info, b))
        full_ref[cut, far] = _masked(h_ref[cut, :], z.valid(info, b))
    total = None
    for x, w, cut in copies:
        x.wait()
        w.wait()
        term = _dot(x_ref[:, cut], w_ref[cut, :], NN)
        total = term if total is None else total + term
    far_ref[...] = total.astype(bf16)


def own_kernel(z, info, x_ref, w_ref, far_ref, out_ref):
    own = pl.ds(pl.multiple_of(info[z.core] * z.cols, z.cols), z.cols)
    out_ref[...] = _dot(x_ref[...], w_ref[:, own], NN) + far_ref[...].astype(f32)


def back_kernel(z, info, g_ref, *refs):
    packets, (up_ref, part_ref) = refs[:NEAR], refs[NEAR:]
    for b in range(z.nb):
        s = z.slot(info, 0, b)
        rel = _div(s, z.ten_dev) ^ info[z.me]
        at = _div(rel, NEAR) * z.ten_dev + _rem(s, z.ten_dev)
        at = pl.ds(pl.multiple_of(at * z.rank, z.rank), z.rank)
        near = _rem(rel, NEAR)
        u = packets[0][at, :]
        for k in range(1, NEAR):
            u = jnp.where(near == k, packets[k][at, :], u)
        up_ref[z.ranks(b), :] = u
        g = _masked(g_ref[z.block(b), :], z.valid(info, b))
        part_ref[:, z.block(b)] = _dot(u, g, NT)


def pack_kernel(z, n_out, start, info, mine_ref, other_ref, x_ref, *refs):
    outs, packed = refs[:n_out], refs[n_out]
    packed[...] = jnp.zeros_like(packed)
    for b, place in enumerate(z.places(info)):
        cut = z.block(b)
        v = (mine_ref[:, cut] + other_ref[:, cut]) * adapter_scale
        packed[place, cut] = v.astype(bf16)
    wide = outs[0].shape[1]
    res = _dot(packed[...], x_ref[:, start : start + wide], NN).astype(bf16)
    each = res.shape[0] // n_out
    for k in range(n_out):
        outs[k][...] = res[k * each : (k + 1) * each]


def pack_up_kernel(z, n_out, info, mine_ref, other_ref, g_ref, *refs):
    outs, packed = refs[:n_out], refs[n_out]
    own = pl.ds(pl.multiple_of(info[z.core] * z.cols, z.cols), z.cols)
    packed[...] = jnp.zeros_like(packed)
    for b, place in enumerate(z.places(info)):
        cut = z.block(b)
        packed[place, cut] = (mine_ref[:, cut] + other_ref[:, cut]).astype(bf16)
    res = (adapter_scale * _dot(packed[...], g_ref[:, own], NN)).astype(bf16)
    each = res.shape[0] // n_out
    for k in range(n_out):
        outs[k][...] = res[k * each : (k + 1) * each]


def one_hot_sums(z, info, sums_ref):
    n = CAP * z.rank
    shape = (z.ten_dev * z.rank, n)
    row = lax.broadcasted_iota(i32, shape, 0)
    col = lax.broadcasted_iota(i32, shape, 1)
    same = _rem(row, z.rank) == _rem(col, z.rank)
    row_slot = _div(row, z.rank)
    tables = [z.owner_and_order(info, k) for k in range(NEAR)]
    for j in range(z.n_far):
        holder = info[z.me] ^ (NEAR * j)
        parts = []
        for k in range(NEAR):
            owners, orders = tables[k]
            local = []
            for r in range(CAP):
                found = jnp.int32(0)
                for b in range(z.nb):
                    hit = (owners[b] == holder) & (orders[b] == r)
                    found = jnp.where(hit, _rem(z.slot(info, k, b), z.ten_dev), found)
                local.append(found)
            wanted = jnp.where(col < z.rank, local[0], local[1])
            parts.append(jnp.where(same & (row_slot == wanted), 1.0, 0.0))
        sums_ref[j] = jnp.concatenate(parts, axis=1).astype(bf16)


def dense_kernel(z, info, sums_ref, *refs):
    got, near_ref, far_refs = refs[:NEAR], refs[NEAR], refs[NEAR + 1 :]
    n = CAP * z.rank
    for j in range(z.n_far):
        stacked = jnp.concatenate([g[j * n : (j + 1) * n, :] for g in got], axis=0)
        total = _dot(sums_ref[j], stacked, NN)
        if j == 0:
            near_ref[...] = total
        else:
            far_refs[j - 1][...] = total.astype(bf16)


def final_kernel(parts, n_far, info, *refs):
    outs = refs[len(refs) - len(parts) :]
    i = 0
    for n, out in zip(parts, outs):
        at = 0
        for _ in range(n):
            total = refs[i][...]
            for r in refs[i + 1 : i + n_far]:
                total = total + r[...].astype(f32)
            out[:, at : at + total.shape[1]] = total
            at += total.shape[1]
            i += n_far


def choose_kernel(z, info, info_x, own_ref, far_ref, pair_ref, *outs):
    half = own_ref.shape[0]
    sources = (own_ref, pair_ref.at[:half], far_ref, pair_ref.at[half:])
    wanted = ((info, 0), (info, 1), (info_x, 0), (info_x, 1))
    for (table, which), out in zip(wanted, outs):
        for b in range(z.nb):
            s = z.slot(table, which, b)
            rel = _div(s, z.ten_dev) ^ info[z.me]
            at = _rem(rel, 2) * z.ten_dev + _rem(s, z.ten_dev)
            line = _div(rel, 2)
            v = sources[0][at]
            for k in range(1, 4):
                v = jnp.where(line == k, sources[k][at], v)
            out[z.ranks(b), :] = v


def shrink_kernel(z, n_parts, info, x_ref, *refs):
    parts, (full_ref, out_ref) = refs[:n_parts], refs[n_parts:]
    wide = z.width // n_parts
    total = None
    for j in range(n_parts):
        if n_parts == 1:
            cut = slice(0, wide)
        else:
            cut = pl.ds(pl.multiple_of((info[z.quarter] ^ j) * wide, wide), wide)
        full_ref[:, cut] = parts[j][...]
        term = _dot(x_ref[:, cut], parts[j][...], NT)
        total = term if total is None else total + term
    for b in range(z.nb):
        out_ref[:, z.block(b)] = total[z.block(b), :].T[z.ranks(b), :]


def projected_kernel(z, info, base_ref, mine_ref, other_ref, up_ref, out_ref, spread):
    spread[...] = jnp.zeros_like(spread)
    for b in range(z.nb):
        cut = z.block(b)
        spread[z.ranks(b), cut] = (mine_ref[:, cut] + other_ref[:, cut]).astype(bf16)
    wide = _dot(spread[...], up_ref[...], TN)
    for b in range(z.nb):
        cut = z.block(b)
        full = base_ref[cut, :] + adapter_scale * wide[cut]
        out_ref[cut, :] = _masked(full, z.valid(info, b)).astype(bf16)


def through_kernel(z, first, info, g_ref, w_ref, out_ref, *sums):
    step = out_ref.shape[1] // 4
    for h in range(4):
        cut = slice(h * step, (h + 1) * step)
        rows = slice(first + h * step, first + (h + 1) * step)
        out_ref[:, cut] = _dot(g_ref[...], w_ref[rows, :], NT)
    for s in sums:
        one_hot_sums(z, info, s)


def tokens_kernel(z, info, low_ref, high_ref, mine_ref, other_ref, d_ref, out_ref, spread):
    step = pl.program_id(0)
    wide = out_ref.shape[1]
    per_half = low_ref.shape[1] // wide

    @pl.when(step == 0)
    def _():
        spread[...] = jnp.zeros_like(spread)
        for b in range(z.nb):
            cut = z.block(b)
            v = (mine_ref[:, cut] + other_ref[:, cut]) * adapter_scale
            spread[z.ranks(b), cut] = v.astype(bf16)

    cut = pl.ds(pl.multiple_of(step * wide, wide), wide)
    added = _dot(spread[...], d_ref[:, cut], TN)
    for half, through in enumerate((low_ref, high_ref)):

        @pl.when(step // per_half == half)
        def _():
            here = pl.ds(pl.multiple_of((step - half * per_half) * wide, wide), wide)
            out_ref[...] = (through[:, here] + added).astype(bf16)


def on_device(
    n_groups,
    n_dp,
    tokens,
    base_weight,
    adapter_down,
    adapter_up,
    out_cotangent,
    block_tenant,
    block_valid,
    tenant_slot,
):
    nb = block_tenant.shape[0]
    rows, width = tokens.shape
    cols = out_cotangent.shape[1]
    tenants = tenant_slot.shape[0]
    ten_dev, _, rank = adapter_down.shape
    z = Sizes(n_dp, nb, ten_dev, rank, cols, width)
    n_far = z.n_far
    me = lax.axis_index("dp")
    core = lax.axis_index("tensor")
    group = lax.axis_index("groups")
    shared = n_groups == 2 and n_dp == 8
    n_parts = 4 if shared else 1
    mine_q = group * 2 + me % 2 if shared else jnp.int32(0)
    quarter = width // n_parts

    cotangent_other = _swap(out_cotangent, "tensor")

    down_t = jnp.swapaxes(adapter_down, 1, 2)
    if shared:
        to_y = lax.dynamic_slice_in_dim(down_t, (mine_q ^ 1) * quarter, quarter, axis=2)
        from_y = _xor(to_y, n_dp, 1)
    far_up = [_xor(adapter_up, n_dp, NEAR * j) for j in range(1, n_far)]
    lane = jnp.arange(LANES, dtype=i32)

    def spread_out(x):
        hit = lane[:, None] == jnp.arange(x.shape[0], dtype=i32)[None, :]
        return jnp.sum(jnp.where(hit, x[None, :], 0), axis=1).astype(i32)

    own_tenants = spread_out(block_tenant)
    tag = jnp.broadcast_to(own_tenants[None, :], (16, LANES)).astype(bf16)
    tag = jnp.pad(tag, ((0, 0), (0, cols - LANES)))
    ups = [u.reshape(ten_dev * rank, cols) for u in [adapter_up] + far_up]
    packet = jnp.concatenate(ups + [tag], axis=0)
    packets = [packet] + [_xor(packet, n_dp, k) for k in range(1, NEAR)]

    if shared:
        own = lax.dynamic_slice_in_dim(down_t, mine_q * quarter, quarter, axis=2)
        shard = jnp.concatenate([own, from_y], axis=0)
        shard_far = _xor(shard, n_dp, 4)

    line = lax.broadcasted_iota(i32, (16, LANES), 0)
    place = jnp.where(lane == 0, me, jnp.where(lane == 1, core, mine_q))
    info = jnp.where(line == 8, place[None, :], spread_out(block_valid)[None, :])
    info = jnp.where(line == 6, spread_out(tenant_slot)[None, :], info)
    info = jnp.where(line == 0, own_tenants[None, :], info)

    base_other, g_full, x_in = _call(
        functools.partial(base_kernel, z), "base", (1,),
        [pl.BlockSpec(memory_space=pl.ANY)] * 2 + [VMEM] * 2,
        [_whole((rows, cols))] + [VMEM] * 2,
        [
            _shape((rows, cols), bf16), _shape((rows, 2 * cols), bf16), _shape(tokens.shape, bf16),
        ],
        [
            pltpu.VMEM((width, cols), bf16),
            pltpu.SemaphoreType.DMA((5,)), pltpu.SemaphoreType.DMA((5,)),
        ],
        vmem=BIG_VMEM,
    )(
        _tie(info, shard if shared else packet),
        tokens, base_weight, out_cotangent, cotangent_other,
    )
    base_arrived = _swap(base_other, "tensor")
    packets = [_tie(p, base_other) for p in packets]

    for k in range(1, NEAR):
        info = jnp.where(line == k, packets[k][-16, :LANES].astype(i32)[None, :], info)

    if shared:
        shard_far = _tie(shard_far, base_other)
        info = _tie(info, shard_far)
        farther = _xor(jnp.concatenate([shard, shard_far], axis=0), n_dp, 2)

    part = (rank, rows)
    block_up, back_part = _call(
        functools.partial(back_kernel, z), "back", (1,),
        [VMEM] * (1 + NEAR), [VMEM, _whole(part)],
        [_shape((nb * rank, cols), bf16), _shape(part, f32)], [],
    )(info, out_cotangent, *packets)
    back_other = _swap(back_part, "tensor")
    ready = [base_arrived]
    if shared:
        info_x = _swap(info, "groups")

    packed_rows = n_dp * CAP * rank
    near_rows = packed_rows // NEAR

    def pack(info, start, wide):
        return _call(
            functools.partial(pack_kernel, z, NEAR, start), "pack_down", (1,),
            [VMEM] * 3, [_whole((near_rows, wide))] * NEAR,
            [_shape((near_rows, wide), bf16)] * NEAR,
            [pltpu.VMEM((packed_rows, rows), bf16)],
        )(info, back_part, back_other, x_in)

    def to_near(sends):
        return [sends[0]] + [_xor(sends[k], n_dp, k) for k in range(1, NEAR)]

    def dense(info, got):
        wide = got[0].shape[1]
        out = (ten_dev * rank, wide)
        return _call(
            functools.partial(dense_kernel, z), "dense", (1,),
            [VMEM] * (1 + NEAR), [VMEM] + [_whole(out)] * (n_far - 1),
            [_shape(out, f32)] + [_shape(out, bf16)] * (n_far - 1), [],
        )(info, sums, *got)

    def to_far(parts):
        return [parts[0]] + [_xor(parts[j], n_dp, NEAR * j) for j in range(1, n_far)]

    def through(info, first, wide, with_sums):
        sums = _shape((n_far, ten_dev * rank, NEAR * CAP * rank), bf16)
        return _call(
            functools.partial(through_kernel, z, first), "through", (1,), [VMEM] * 2,
            [VMEM] * (1 + with_sums), [_shape((rows, wide), f32)] + [sums] * with_sums, [],
        )(info, g_full, base_weight)

    half = width // 2
    wide_a = half
    sends_a = pack(_tie(info, *ready), 0, wide_a)
    got_a = to_near(sends_a)
    low, sums = through(_tie(info, sends_a[0]), 0, half, 1)

    if shared:
        block = (nb * rank, quarter)
        chosen = _call(
            functools.partial(choose_kernel, z), "choose", (1,),
            [VMEM] * 3, [_whole(block)] * 4, [_shape(block, bf16)] * 4, [],
            n_scalars=2,
        )(_tie(info, low), info_x, shard, shard_far, farther)
        got_y = _xor(_tie(chosen[1], got_a[2]), n_dp, 1)
        got_x = _swap(chosen[2], "groups")
        got_d = lax.ppermute(
            chosen[3],
            ("groups", "dp"),
            [(g * n_dp + d, (1 - g) * n_dp + (d ^ 1)) for g in range(2) for d in range(n_dp)],
        )
        after_choose = chosen[0]
    else:
        every = lax.all_gather(down_t, "dp", axis=0, tiled=True)
        slots = jnp.take(tenant_slot, block_tenant, axis=0)
        got_down = [jnp.take(every, slots, axis=0).reshape(nb * rank, width)]
        after_choose = low

    sends_b = pack(_tie(info, after_choose), wide_a, width - wide_a)

    base_own = _call(
        functools.partial(own_kernel, z), "base_own", (1,),
        [VMEM] * 3, VMEM, _shape((rows, cols), f32), [],
    )(_tie(info, sends_b[0]), x_in, base_weight, base_arrived)
    dense_a = dense(_tie(info, base_own), got_a)
    far_a = to_far(dense_a)

    gate = [dense_a[1]] + ([got_y] if shared else [])
    got_b = to_near(
        [_tie(b, *gate) if k in (1, 3) else _tie(b, dense_a[1]) for k, b in enumerate(sends_b)]
    )
    (high,) = through(_tie(info, dense_a[1]), half, width - half, 0)

    if shared:
        got_down = [chosen[0], got_y, got_x, got_d]
    block_down, shrink_part = _call(
        functools.partial(shrink_kernel, z, n_parts), "shrink", (1,),
        [VMEM] * (1 + n_parts), [VMEM, _whole(part)],
        [_shape((nb * rank, width), bf16), _shape(part, f32)], [],
    )(_tie(info, high), x_in, *got_down)
    shrink_other = _swap(shrink_part, "tensor")


    step = min(512, width // 8)
    grad_tokens = _call(
        functools.partial(tokens_kernel, z), "token_grads", (width // step,),
        [VMEM] * 5, pl.BlockSpec((rows, step), lambda i, *_: (0, i)),
        _shape((rows, width), bf16), [pltpu.VMEM((nb * rank, rows), bf16)],
    )(_tie(info, shrink_part), low, high, back_part, back_other, block_down)

    up_sends = _call(
        functools.partial(pack_up_kernel, z, NEAR), "pack_up", (1,),
        [VMEM] * 3, [_whole((near_rows, cols))] * NEAR,
        [_shape((near_rows, cols), bf16)] * NEAR,
        [pltpu.VMEM((packed_rows, rows), bf16)],
    )(_tie(info, grad_tokens), shrink_part, shrink_other, g_full)
    got_u = to_near(up_sends)

    dense_b = dense(_tie(info, up_sends[0]), got_b)
    far_b = to_far(dense_b)

    projected = _call(
        functools.partial(projected_kernel, z), "projected", (1,),
        [VMEM] * 4, _whole((rows, cols)), _shape((rows, cols), bf16),
        [pltpu.VMEM((nb * rank, rows), bf16)],
    )(
        _tie(info, dense_b[1]),
        base_own, shrink_part, shrink_other, block_up,
    )
    dense_u = dense(_tie(info, projected), got_u)
    far_u = to_far(dense_u)

    outs = [(ten_dev * rank, width), (ten_dev * rank, cols)]
    grad_down, grad_up = _call(
        functools.partial(final_kernel, (2, 1), n_far), "final", (1,),
        [VMEM] * (3 * n_far), [_whole(o) for o in outs], [_shape(o, f32) for o in outs], [],
    )(info, *far_a, *far_b, *far_u)
    grad_down = jnp.swapaxes(grad_down.reshape(ten_dev, rank, width), 1, 2)
    return projected, grad_tokens, grad_down, grad_up.reshape(ten_dev, rank, cols)


def solution(mesh):
    n_groups, n_dp = mesh.shape["groups"], mesh.shape["dp"]
    in_specs = (
        P(("groups", "dp"), "tensor"),
        P("tensor", None),
        P("dp", "tensor", None),
        P("dp", None, "tensor"),
        P(("groups", "dp"), "tensor"),
        P(("groups", "dp")),
        P(("groups", "dp")),
        P("groups"),
    )
    out_specs = (
        P(("groups", "dp"), "tensor"),
        P(("groups", "dp"), "tensor"),
        P(("groups", "dp"), "tensor", None),
        P(("groups", "dp"), None, "tensor"),
    )

    def run(*args):
        return on_device(n_groups, n_dp, *args)

    return jax.shard_map(
        run, mesh=mesh, in_specs=in_specs, out_specs=out_specs, check_vma=False
    )
```

```python
import functools

import jax
import jax.numpy as jnp
from jax import lax
from jax.experimental import pallas as pl
from jax.experimental.pallas import tpu as pltpu
from jax.sharding import PartitionSpec as P

TENANT_BLOCK = 128
CAP = 2
NEAR = 4
VMEM_LIMIT = 9 * 1024 * 1024
BIG_VMEM = 36 * 1024 * 1024
LANES = 128

adapter_scale = 2.0
f32 = jnp.float32
bf16 = jnp.bfloat16
i32 = jnp.int32

NT = (((1,), (1,)), ((), ()))
TN = (((0,), (0,)), ((), ()))
NN = (((1,), (0,)), ((), ()))


def _dot(a, b, dims):
    return lax.dot_general(a, b, dims, preferred_element_type=f32)


def _swap(x, axis):
    return lax.ppermute(x, axis, [(0, 1), (1, 0)])


def _xor(x, n, k):
    return lax.ppermute(x, "dp", [(i, i ^ k) for i in range(n)])


def _tie(x, *after):
    return lax.optimization_barrier((x,) + after)[0]


def _div(a, n):
    return a >> (n.bit_length() - 1) if n & (n - 1) == 0 else lax.div(a, jnp.int32(n))


def _rem(a, n):
    return a & (n - 1) if n & (n - 1) == 0 else lax.rem(a, jnp.int32(n))


VMEM = pl.BlockSpec(memory_space=pltpu.VMEM)


def _shape(shape, dtype):
    return jax.ShapeDtypeStruct(shape, dtype)


def _call(
    body, name, grid, in_specs, out_specs, out_shape, scratch, aliases=None, vmem=VMEM_LIMIT,
    n_scalars=1,
):
    return pl.pallas_call(
        body,
        name=name,
        grid_spec=pltpu.PrefetchScalarGridSpec(
            num_scalar_prefetch=n_scalars,
            grid=grid,
            in_specs=in_specs,
            out_specs=out_specs,
            scratch_shapes=scratch,
        ),
        out_shape=out_shape,
        input_output_aliases=aliases or {},
        compiler_params=pltpu.CompilerParams(vmem_limit_bytes=vmem),
        cost_estimate=pl.CostEstimate(flops=1, bytes_accessed=1, transcendentals=0),
    )


def _whole(shape):
    return pl.BlockSpec(shape, lambda *_: (0,) * len(shape))


class Sizes:
    def __init__(self, n_dp, nb, ten_dev, rank, cols, width):
        self.n_dp, self.nb, self.ten_dev = n_dp, nb, ten_dev
        self.rank, self.cols, self.width = rank, cols, width
        self.n_far = n_dp // NEAR
        self.rows = nb * TENANT_BLOCK
        self.me, self.core, self.quarter = (8, 0), (8, 1), (8, 2)

    def block(self, b):
        return slice(b * TENANT_BLOCK, (b + 1) * TENANT_BLOCK)

    def ranks(self, b):
        return slice(b * self.rank, (b + 1) * self.rank)

    def slot(self, info, which, b):
        return info[6, info[which, b]]

    def valid(self, info, b):
        return info[9, b]

    def owner_and_order(self, info, which):
        owners = [_div(self.slot(info, which, b), self.ten_dev) for b in range(self.nb)]
        orders = []
        for b in range(self.nb):
            n = jnp.int32(0)
            for c in range(b):
                n = n + jnp.where(owners[c] == owners[b], 1, 0)
            orders.append(n)
        return owners, orders

    def places(self, info):
        owners, orders = self.owner_and_order(info, 0)
        out = []
        for o, r in zip(owners, orders):
            rel = o ^ info[self.me]
            place = (_rem(rel, NEAR) * self.n_far + _div(rel, NEAR)) * CAP + r
            out.append(pl.ds(pl.multiple_of(place * self.rank, self.rank), self.rank))
        return out


def _masked(x, valid):
    row = lax.broadcasted_iota(i32, x.shape, 0)
    return jnp.where(row < valid, x, jnp.zeros((), x.dtype))


def base_kernel(
    z, info, x_hbm, w_hbm, g_hbm, h_ref, far_ref, full_ref, x_ref, w_ref, g_ref, x_sem, w_sem, g_sem
):
    own = pl.ds(pl.multiple_of(info[z.core] * z.cols, z.cols), z.cols)
    far = pl.ds(pl.multiple_of((1 - info[z.core]) * z.cols, z.cols), z.cols)
    unit = z.width // 8
    g = pltpu.make_async_copy(g_hbm, g_ref, g_sem)
    g.start()
    copies = []
    for i, (first, last) in enumerate(((0, 1), (1, 3), (3, 5), (5, 7), (7, 8))):
        cut = pl.ds(first * unit, (last - first) * unit)
        x = pltpu.make_async_copy(x_hbm.at[:, cut], x_ref.at[:, cut], x_sem.at[i])
        w = pltpu.make_async_copy(w_hbm.at[cut, far], w_ref.at[cut], w_sem.at[i])
        x.start()
        w.start()
        copies.append((x, w, cut))
    g.wait()
    for b in range(z.nb):
        cut = z.block(b)
        full_ref[cut, own] = _masked(g_ref[cut, :], z.valid(info, b))
        full_ref[cut, far] = _masked(h_ref[cut, :], z.valid(info, b))
    total = None
    for x, w, cut in copies:
        x.wait()
        w.wait()
        term = _dot(x_ref[:, cut], w_ref[cut, :], NN)
        total = term if total is None else total + term
    far_ref[...] = total.astype(bf16)


def own_kernel(z, info, x_ref, w_ref, far_ref, out_ref):
    own = pl.ds(pl.multiple_of(info[z.core] * z.cols, z.cols), z.cols)
    out_ref[...] = _dot(x_ref[...], w_ref[:, own], NN) + far_ref[...].astype(f32)


def back_kernel(z, info, g_ref, *refs):
    packets, (up_ref, part_ref) = refs[:NEAR], refs[NEAR:]
    own = pl.ds(pl.multiple_of(info[z.core] * z.cols, z.cols), z.cols)
    for b in range(z.nb):
        s = z.slot(info, 0, b)
        rel = _div(s, z.ten_dev) ^ info[z.me]
        at = _div(rel, NEAR) * z.ten_dev + _rem(s, z.ten_dev)
        at = pl.ds(pl.multiple_of(at * z.rank, z.rank), z.rank)
        near = _rem(rel, NEAR)
        u = packets[0][at, :]
        for k in range(1, NEAR):
            u = jnp.where(near == k, packets[k][at, :], u)
        up_ref[z.ranks(b), :] = u
        part_ref[:, z.block(b)] = _dot(u, g_ref[z.block(b), own], NT)


def pack_kernel(z, n_out, start, info, mine_ref, other_ref, x_ref, *refs):
    outs, packed = refs[:n_out], refs[n_out]
    packed[...] = jnp.zeros_like(packed)
    for b, place in enumerate(z.places(info)):
        cut = z.block(b)
        v = (mine_ref[:, cut] + other_ref[:, cut]) * adapter_scale
        packed[place, cut] = v.astype(bf16)
    wide = outs[0].shape[1]
    res = _dot(packed[...], x_ref[:, start : start + wide], NN).astype(bf16)
    each = res.shape[0] // n_out
    for k in range(n_out):
        outs[k][...] = res[k * each : (k + 1) * each]


def pack_up_kernel(z, n_out, info, mine_ref, other_ref, g_ref, *refs):
    outs, packed = refs[:n_out], refs[n_out]
    own = pl.ds(pl.multiple_of(info[z.core] * z.cols, z.cols), z.cols)
    packed[...] = jnp.zeros_like(packed)
    for b, place in enumerate(z.places(info)):
        cut = z.block(b)
        packed[place, cut] = (mine_ref[:, cut] + other_ref[:, cut]).astype(bf16)
    res = (adapter_scale * _dot(packed[...], g_ref[:, own], NN)).astype(bf16)
    each = res.shape[0] // n_out
    for k in range(n_out):
        outs[k][...] = res[k * each : (k + 1) * each]


def one_hot_sums(z, info, sums_ref):
    n = CAP * z.rank
    shape = (z.ten_dev * z.rank, n)
    row = lax.broadcasted_iota(i32, shape, 0)
    col = lax.broadcasted_iota(i32, shape, 1)
    same = _rem(row, z.rank) == _rem(col, z.rank)
    row_slot = _div(row, z.rank)
    tables = [z.owner_and_order(info, k) for k in range(NEAR)]
    for j in range(z.n_far):
        holder = info[z.me] ^ (NEAR * j)
        parts = []
        for k in range(NEAR):
            owners, orders = tables[k]
            local = []
            for r in range(CAP):
                found = jnp.int32(0)
                for b in range(z.nb):
                    hit = (owners[b] == holder) & (orders[b] == r)
                    found = jnp.where(hit, _rem(z.slot(info, k, b), z.ten_dev), found)
                local.append(found)
            wanted = jnp.where(col < z.rank, local[0], local[1])
            parts.append(jnp.where(same & (row_slot == wanted), 1.0, 0.0))
        sums_ref[j] = jnp.concatenate(parts, axis=1).astype(bf16)


def dense_kernel(z, info, sums_ref, *refs):
    got, near_ref, far_refs = refs[:NEAR], refs[NEAR], refs[NEAR + 1 :]
    n = CAP * z.rank
    for j in range(z.n_far):
        stacked = jnp.concatenate([g[j * n : (j + 1) * n, :] for g in got], axis=0)
        total = _dot(sums_ref[j], stacked, NN)
        if j == 0:
            near_ref[...] = total
        else:
            far_refs[j - 1][...] = total.astype(bf16)


def final_kernel(parts, n_far, info, *refs):
    outs = refs[len(refs) - len(parts) :]
    i = 0
    for n, out in zip(parts, outs):
        at = 0
        for _ in range(n):
            total = refs[i][...]
            for r in refs[i + 1 : i + n_far]:
                total = total + r[...].astype(f32)
            out[:, at : at + total.shape[1]] = total
            at += total.shape[1]
            i += n_far


def choose_kernel(z, info, info_x, own_ref, far_ref, pair_ref, *outs):
    half = own_ref.shape[0]
    sources = (own_ref, pair_ref.at[:half], far_ref, pair_ref.at[half:])
    wanted = ((info, 0), (info, 1), (info_x, 0), (info_x, 1))
    for (table, which), out in zip(wanted, outs):
        for b in range(z.nb):
            s = z.slot(table, which, b)
            rel = _div(s, z.ten_dev) ^ info[z.me]
            at = _rem(rel, 2) * z.ten_dev + _rem(s, z.ten_dev)
            line = _div(rel, 2)
            v = sources[0][at]
            for k in range(1, 4):
                v = jnp.where(line == k, sources[k][at], v)
            out[z.ranks(b), :] = v


def shrink_kernel(z, n_parts, info, x_ref, *refs):
    parts, (full_ref, out_ref) = refs[:n_parts], refs[n_parts:]
    wide = z.width // n_parts
    total = None
    for j in range(n_parts):
        if n_parts == 1:
            cut = slice(0, wide)
        else:
            cut = pl.ds(pl.multiple_of((info[z.quarter] ^ j) * wide, wide), wide)
        full_ref[:, cut] = parts[j][...]
        term = _dot(x_ref[:, cut], parts[j][...], NT)
        total = term if total is None else total + term
    for b in range(z.nb):
        out_ref[:, z.block(b)] = total[z.block(b), :].T[z.ranks(b), :]


def projected_kernel(z, info, base_ref, mine_ref, other_ref, up_ref, out_ref, spread):
    spread[...] = jnp.zeros_like(spread)
    for b in range(z.nb):
        cut = z.block(b)
        spread[z.ranks(b), cut] = (mine_ref[:, cut] + other_ref[:, cut]).astype(bf16)
    wide = _dot(spread[...], up_ref[...], TN)
    for b in range(z.nb):
        cut = z.block(b)
        full = base_ref[cut, :] + adapter_scale * wide[cut]
        out_ref[cut, :] = _masked(full, z.valid(info, b)).astype(bf16)


def through_kernel(z, first, info, g_ref, w_ref, out_ref, *sums):
    step = out_ref.shape[1] // 4
    for h in range(4):
        cut = slice(h * step, (h + 1) * step)
        rows = slice(first + h * step, first + (h + 1) * step)
        out_ref[:, cut] = _dot(g_ref[...], w_ref[rows, :], NT)
    for s in sums:
        one_hot_sums(z, info, s)


def tokens_kernel(z, first, info, through_ref, mine_ref, other_ref, d_ref, *refs):
    out_ref, spread = refs[-2:]
    step = pl.program_id(0)
    wide = out_ref.shape[1]

    @pl.when(step == 0)
    def _():
        spread[...] = jnp.zeros_like(spread)
        for b in range(z.nb):
            cut = z.block(b)
            v = (mine_ref[:, cut] + other_ref[:, cut]) * adapter_scale
            spread[z.ranks(b), cut] = v.astype(bf16)

    here = pl.ds(pl.multiple_of(step * wide, wide), wide)
    cut = pl.ds(pl.multiple_of((first + step) * wide, wide), wide)
    added = _dot(spread[...], d_ref[:, cut], TN)
    out_ref[...] = (through_ref[:, here] + added).astype(bf16)


def on_device(
    n_groups,
    n_dp,
    tokens,
    base_weight,
    adapter_down,
    adapter_up,
    out_cotangent,
    block_tenant,
    block_valid,
    tenant_slot,
):
    nb = block_tenant.shape[0]
    rows, width = tokens.shape
    cols = out_cotangent.shape[1]
    tenants = tenant_slot.shape[0]
    ten_dev, _, rank = adapter_down.shape
    z = Sizes(n_dp, nb, ten_dev, rank, cols, width)
    n_far = z.n_far
    me = lax.axis_index("dp")
    core = lax.axis_index("tensor")
    group = lax.axis_index("groups")
    shared = n_groups == 2 and n_dp == 8
    n_parts = 4 if shared else 1
    mine_q = group * 2 + me % 2 if shared else jnp.int32(0)
    quarter = width // n_parts

    cotangent_other = _swap(out_cotangent, "tensor")

    down_t = jnp.swapaxes(adapter_down, 1, 2)
    if shared:
        to_y = lax.dynamic_slice_in_dim(down_t, (mine_q ^ 1) * quarter, quarter, axis=2)
        from_y = _xor(to_y, n_dp, 1)
    far_up = [_xor(adapter_up, n_dp, NEAR * j) for j in range(1, n_far)]
    lane = jnp.arange(LANES, dtype=i32)

    def spread_out(x):
        hit = lane[:, None] == jnp.arange(x.shape[0], dtype=i32)[None, :]
        return jnp.sum(jnp.where(hit, x[None, :], 0), axis=1).astype(i32)

    own_tenants = spread_out(block_tenant)
    tag = jnp.broadcast_to(own_tenants[None, :], (16, LANES)).astype(bf16)
    tag = jnp.pad(tag, ((0, 0), (0, cols - LANES)))
    ups = [u.reshape(ten_dev * rank, cols) for u in [adapter_up] + far_up]
    packet = jnp.concatenate(ups + [tag], axis=0)
    packets = [packet] + [_xor(packet, n_dp, k) for k in range(1, NEAR)]

    if shared:
        own = lax.dynamic_slice_in_dim(down_t, mine_q * quarter, quarter, axis=2)
        shard = jnp.concatenate([own, from_y], axis=0)
        shard_far = _xor(shard, n_dp, 4)

    line = lax.broadcasted_iota(i32, (16, LANES), 0)
    place = jnp.where(lane == 0, me, jnp.where(lane == 1, core, mine_q))
    info = jnp.where(line == 8, place[None, :], spread_out(block_valid)[None, :])
    info = jnp.where(line == 6, spread_out(tenant_slot)[None, :], info)
    info = jnp.where(line == 0, own_tenants[None, :], info)

    base_other, g_full, x_in = _call(
        functools.partial(base_kernel, z), "base", (1,),
        [pl.BlockSpec(memory_space=pl.ANY)] * 3 + [VMEM],
        [_whole((rows, cols))] + [VMEM] * 2,
        [
            _shape((rows, cols), bf16), _shape((rows, 2 * cols), bf16), _shape(tokens.shape, bf16),
        ],
        [
            pltpu.VMEM((width, cols), bf16), pltpu.VMEM((rows, cols), bf16),
            pltpu.SemaphoreType.DMA((5,)), pltpu.SemaphoreType.DMA((5,)),
            pltpu.SemaphoreType.DMA,
        ],
        vmem=BIG_VMEM,
    )(
        _tie(info, shard if shared else packet),
        tokens, base_weight, out_cotangent, cotangent_other,
    )
    base_arrived = _swap(base_other, "tensor")
    packets = [_tie(p, base_other) for p in packets]

    for k in range(1, NEAR):
        info = jnp.where(line == k, packets[k][-16, :LANES].astype(i32)[None, :], info)

    if shared:
        shard_far = _tie(shard_far, base_other)
        info = _tie(info, shard_far)
        farther = _xor(jnp.concatenate([shard, shard_far], axis=0), n_dp, 2)

    part = (rank, rows)
    block_up, back_part = _call(
        functools.partial(back_kernel, z), "back", (1,),
        [VMEM] * (1 + NEAR), [VMEM, _whole(part)],
        [_shape((nb * rank, cols), bf16), _shape(part, f32)], [],
    )(info, g_full, *packets)
    back_other = _swap(back_part, "tensor")
    ready = [base_arrived]
    if shared:
        info_x = _swap(info, "groups")

    packed_rows = n_dp * CAP * rank
    near_rows = packed_rows // NEAR

    def pack(info, start, wide):
        return _call(
            functools.partial(pack_kernel, z, NEAR, start), "pack_down", (1,),
            [VMEM] * 3, [_whole((near_rows, wide))] * NEAR,
            [_shape((near_rows, wide), bf16)] * NEAR,
            [pltpu.VMEM((packed_rows, rows), bf16)],
        )(info, back_part, back_other, x_in)

    def to_near(sends):
        return [sends[0]] + [_xor(sends[k], n_dp, k) for k in range(1, NEAR)]

    def dense(info, got):
        wide = got[0].shape[1]
        out = (ten_dev * rank, wide)
        return _call(
            functools.partial(dense_kernel, z), "dense", (1,),
            [VMEM] * (1 + NEAR), [VMEM] + [_whole(out)] * (n_far - 1),
            [_shape(out, f32)] + [_shape(out, bf16)] * (n_far - 1), [],
        )(info, sums, *got)

    def to_far(parts):
        return [parts[0]] + [_xor(parts[j], n_dp, NEAR * j) for j in range(1, n_far)]

    def through(info, first, wide, with_sums):
        sums = _shape((n_far, ten_dev * rank, NEAR * CAP * rank), bf16)
        return _call(
            functools.partial(through_kernel, z, first), "through", (1,), [VMEM] * 2,
            [VMEM] * (1 + with_sums), [_shape((rows, wide), f32)] + [sums] * with_sums, [],
        )(info, g_full, base_weight)

    half = width // 2
    wide_a = half
    sends_a = pack(_tie(info, *ready), 0, wide_a)
    got_a = to_near(sends_a)
    low, sums = through(_tie(info, sends_a[0]), 0, half, 1)

    if shared:
        block = (nb * rank, quarter)
        chosen = _call(
            functools.partial(choose_kernel, z), "choose", (1,),
            [VMEM] * 3, [_whole(block)] * 4, [_shape(block, bf16)] * 4, [],
            n_scalars=2,
        )(_tie(info, low), info_x, shard, shard_far, farther)
        sends_b = pack(_tie(info, chosen[0]), wide_a, width - wide_a)
        got_y = _xor(_tie(chosen[1], got_a[2], sends_b[0]), n_dp, 1)
        got_x = _swap(_tie(chosen[2], sends_b[0]), "groups")
        got_d = lax.ppermute(
            _tie(chosen[3], sends_b[0]),
            ("groups", "dp"),
            [(g * n_dp + d, (1 - g) * n_dp + (d ^ 1)) for g in range(2) for d in range(n_dp)],
        )
    else:
        every = lax.all_gather(down_t, "dp", axis=0, tiled=True)
        slots = jnp.take(tenant_slot, block_tenant, axis=0)
        got_down = [jnp.take(every, slots, axis=0).reshape(nb * rank, width)]
        sends_b = pack(_tie(info, low), wide_a, width - wide_a)

    base_own = _call(
        functools.partial(own_kernel, z), "base_own", (1,),
        [VMEM] * 3, VMEM, _shape((rows, cols), f32), [],
    )(_tie(info, sends_b[0]), x_in, base_weight, base_arrived)
    dense_a = dense(_tie(info, base_own), got_a)
    far_a = to_far(dense_a)

    (high,) = through(_tie(info, dense_a[1]), half, width - half, 0)
    gate = [high] + ([got_y] if shared else [])
    got_b = to_near(
        [_tie(b, *gate) if k in (1, 3) else _tie(b, dense_a[1]) for k, b in enumerate(sends_b)]
    )

    if shared:
        got_down = [chosen[0], got_y, got_x, got_d]
    block_down, shrink_part = _call(
        functools.partial(shrink_kernel, z, n_parts), "shrink", (1,),
        [VMEM] * (1 + n_parts), [VMEM, _whole(part)],
        [_shape((nb * rank, width), bf16), _shape(part, f32)], [],
    )(_tie(info, high), x_in, *got_down)
    shrink_other = _swap(shrink_part, "tensor")


    step = min(512, width // 8)

    def token_grads(info, product, first, so_far):
        steps = product.shape[1] // step
        return _call(
            functools.partial(tokens_kernel, z, first), "token_grads", (steps,),
            [VMEM] * 4 + [pl.BlockSpec(memory_space=pl.ANY)] * len(so_far),
            pl.BlockSpec((rows, step), lambda i, *_: (0, first + i)),
            _shape((rows, width), bf16), [pltpu.VMEM((nb * rank, rows), bf16)],
            {5: 0} if so_far else None,
        )(info, product, back_part, back_other, block_down, *so_far)

    grad_tokens = token_grads(_tie(info, shrink_part), low, 0, [])

    up_sends = _call(
        functools.partial(pack_up_kernel, z, NEAR), "pack_up", (1,),
        [VMEM] * 3, [_whole((near_rows, cols))] * NEAR,
        [_shape((near_rows, cols), bf16)] * NEAR,
        [pltpu.VMEM((packed_rows, rows), bf16)],
    )(_tie(info, grad_tokens), shrink_part, shrink_other, g_full)
    got_u = to_near(up_sends)

    dense_b = dense(_tie(info, up_sends[0]), got_b)
    far_b = to_far(dense_b)

    grad_tokens = token_grads(_tie(info, dense_b[1]), high, half // step, [grad_tokens])
    dense_u = dense(_tie(info, grad_tokens), got_u)
    far_u = to_far(dense_u)

    projected = _call(
        functools.partial(projected_kernel, z), "projected", (1,),
        [VMEM] * 4, _whole((rows, cols)), _shape((rows, cols), bf16),
        [pltpu.VMEM((nb * rank, rows), bf16)],
    )(
        _tie(info, dense_u[1]),
        base_own, shrink_part, shrink_other, block_up,
    )

    outs = [(ten_dev * rank, width), (ten_dev * rank, cols)]
    grad_down, grad_up = _call(
        functools.partial(final_kernel, (2, 1), n_far), "final", (1,),
        [VMEM] * (3 * n_far), [_whole(o) for o in outs], [_shape(o, f32) for o in outs], [],
    )(info, *far_a, *far_b, *far_u)
    grad_down = jnp.swapaxes(grad_down.reshape(ten_dev, rank, width), 1, 2)
    return projected, grad_tokens, grad_down, grad_up.reshape(ten_dev, rank, cols)


def solution(mesh):
    n_groups, n_dp = mesh.shape["groups"], mesh.shape["dp"]
    in_specs = (
        P(("groups", "dp"), "tensor"),
        P("tensor", None),
        P("dp", "tensor", None),
        P("dp", None, "tensor"),
        P(("groups", "dp"), "tensor"),
        P(("groups", "dp")),
        P(("groups", "dp")),
        P("groups"),
    )
    out_specs = (
        P(("groups", "dp"), "tensor"),
        P(("groups", "dp"), "tensor"),
        P(("groups", "dp"), "tensor", None),
        P(("groups", "dp"), None, "tensor"),
    )

    def run(*args):
        return on_device(n_groups, n_dp, *args)

    return jax.shard_map(
        run, mesh=mesh, in_specs=in_specs, out_specs=out_specs, check_vma=False
    )
```

```python
import functools

import jax
import jax.numpy as jnp
from jax import lax
from jax.experimental import pallas as pl
from jax.experimental.pallas import tpu as pltpu
from jax.sharding import PartitionSpec as P

TENANT_BLOCK = 128
CAP = 2
NEAR = 4
VMEM_LIMIT = 9 * 1024 * 1024
BIG_VMEM = 36 * 1024 * 1024
LANES = 128

adapter_scale = 2.0
f32 = jnp.float32
bf16 = jnp.bfloat16
i32 = jnp.int32

NT = (((1,), (1,)), ((), ()))
TN = (((0,), (0,)), ((), ()))
NN = (((1,), (0,)), ((), ()))


def _dot(a, b, dims):
    return lax.dot_general(a, b, dims, preferred_element_type=f32)


def _swap(x, axis):
    return lax.ppermute(x, axis, [(0, 1), (1, 0)])


def _xor(x, n, k):
    return lax.ppermute(x, "dp", [(i, i ^ k) for i in range(n)])


def _tie(x, *after):
    return lax.optimization_barrier((x,) + after)[0]


def _div(a, n):
    return a >> (n.bit_length() - 1) if n & (n - 1) == 0 else lax.div(a, jnp.int32(n))


def _rem(a, n):
    return a & (n - 1) if n & (n - 1) == 0 else lax.rem(a, jnp.int32(n))


VMEM = pl.BlockSpec(memory_space=pltpu.VMEM)


def _shape(shape, dtype):
    return jax.ShapeDtypeStruct(shape, dtype)


def _call(
    body, name, grid, in_specs, out_specs, out_shape, scratch, aliases=None, vmem=VMEM_LIMIT,
    n_scalars=1,
):
    return pl.pallas_call(
        body,
        name=name,
        grid_spec=pltpu.PrefetchScalarGridSpec(
            num_scalar_prefetch=n_scalars,
            grid=grid,
            in_specs=in_specs,
            out_specs=out_specs,
            scratch_shapes=scratch,
        ),
        out_shape=out_shape,
        input_output_aliases=aliases or {},
        compiler_params=pltpu.CompilerParams(vmem_limit_bytes=vmem),
        cost_estimate=pl.CostEstimate(flops=1, bytes_accessed=1, transcendentals=0),
    )


def _whole(shape):
    return pl.BlockSpec(shape, lambda *_: (0,) * len(shape))


class Sizes:
    def __init__(self, n_dp, nb, ten_dev, rank, cols, width):
        self.n_dp, self.nb, self.ten_dev = n_dp, nb, ten_dev
        self.rank, self.cols, self.width = rank, cols, width
        self.n_far = n_dp // NEAR
        self.rows = nb * TENANT_BLOCK
        self.me, self.core, self.quarter = (8, 0), (8, 1), (8, 2)

    def block(self, b):
        return slice(b * TENANT_BLOCK, (b + 1) * TENANT_BLOCK)

    def ranks(self, b):
        return slice(b * self.rank, (b + 1) * self.rank)

    def slot(self, info, which, b):
        return info[6, info[which, b]]

    def valid(self, info, b):
        return info[9, b]

    def owner_and_order(self, info, which):
        owners = [_div(self.slot(info, which, b), self.ten_dev) for b in range(self.nb)]
        orders = []
        for b in range(self.nb):
            n = jnp.int32(0)
            for c in range(b):
                n = n + jnp.where(owners[c] == owners[b], 1, 0)
            orders.append(n)
        return owners, orders

    def places(self, info):
        owners, orders = self.owner_and_order(info, 0)
        out = []
        for o, r in zip(owners, orders):
            rel = o ^ info[self.me]
            place = (_rem(rel, NEAR) * self.n_far + _div(rel, NEAR)) * CAP + r
            out.append(pl.ds(pl.multiple_of(place * self.rank, self.rank), self.rank))
        return out


def _masked(x, valid):
    row = lax.broadcasted_iota(i32, x.shape, 0)
    return jnp.where(row < valid, x, jnp.zeros((), x.dtype))


def base_kernel(
    z, info, x_hbm, w_hbm, g_hbm, h_ref, far_ref, full_ref, x_ref, w_ref, g_ref, x_sem, w_sem, g_sem
):
    own = pl.ds(pl.multiple_of(info[z.core] * z.cols, z.cols), z.cols)
    far = pl.ds(pl.multiple_of((1 - info[z.core]) * z.cols, z.cols), z.cols)
    unit = z.width // 8
    g = pltpu.make_async_copy(g_hbm, g_ref, g_sem)
    g.start()
    copies = []
    for i, (first, last) in enumerate(((0, 1), (1, 3), (3, 5), (5, 7), (7, 8))):
        cut = pl.ds(first * unit, (last - first) * unit)
        x = pltpu.make_async_copy(x_hbm.at[:, cut], x_ref.at[:, cut], x_sem.at[i])
        w = pltpu.make_async_copy(w_hbm.at[cut, far], w_ref.at[cut], w_sem.at[i])
        x.start()
        w.start()
        copies.append((x, w, cut))
    g.wait()
    for b in range(z.nb):
        cut = z.block(b)
        full_ref[cut, own] = _masked(g_ref[cut, :], z.valid(info, b))
        full_ref[cut, far] = _masked(h_ref[cut, :], z.valid(info, b))
    total = None
    for x, w, cut in copies:
        x.wait()
        w.wait()
        term = _dot(x_ref[:, cut], w_ref[cut, :], NN)
        total = term if total is None else total + term
    far_ref[...] = total.astype(bf16)


def own_kernel(z, info, x_ref, w_ref, far_ref, out_ref):
    own = pl.ds(pl.multiple_of(info[z.core] * z.cols, z.cols), z.cols)
    out_ref[...] = _dot(x_ref[...], w_ref[:, own], NN) + far_ref[...].astype(f32)


def back_kernel(z, info, g_ref, *refs):
    packets, (up_ref, part_ref) = refs[:NEAR], refs[NEAR:]
    own = pl.ds(pl.multiple_of(info[z.core] * z.cols, z.cols), z.cols)
    for b in range(z.nb):
        s = z.slot(info, 0, b)
        rel = _div(s, z.ten_dev) ^ info[z.me]
        at = _div(rel, NEAR) * z.ten_dev + _rem(s, z.ten_dev)
        at = pl.ds(pl.multiple_of(at * z.rank, z.rank), z.rank)
        near = _rem(rel, NEAR)
        u = packets[0][at, :]
        for k in range(1, NEAR):
            u = jnp.where(near == k, packets[k][at, :], u)
        up_ref[z.ranks(b), :] = u
        part_ref[:, z.block(b)] = _dot(u, g_ref[z.block(b), own], NT)


def pack_kernel(z, n_out, start, info, mine_ref, other_ref, x_ref, *refs):
    outs, packed = refs[:n_out], refs[n_out]
    packed[...] = jnp.zeros_like(packed)
    for b, place in enumerate(z.places(info)):
        cut = z.block(b)
        v = (mine_ref[:, cut] + other_ref[:, cut]) * adapter_scale
        packed[place, cut] = v.astype(bf16)
    wide = outs[0].shape[1]
    res = _dot(packed[...], x_ref[:, start : start + wide], NN).astype(bf16)
    each = res.shape[0] // n_out
    for k in range(n_out):
        outs[k][...] = res[k * each : (k + 1) * each]


def pack_up_kernel(z, n_out, info, mine_ref, other_ref, g_ref, *refs):
    outs, packed = refs[:n_out], refs[n_out]
    own = pl.ds(pl.multiple_of(info[z.core] * z.cols, z.cols), z.cols)
    packed[...] = jnp.zeros_like(packed)
    for b, place in enumerate(z.places(info)):
        cut = z.block(b)
        packed[place, cut] = (mine_ref[:, cut] + other_ref[:, cut]).astype(bf16)
    res = (adapter_scale * _dot(packed[...], g_ref[:, own], NN)).astype(bf16)
    each = res.shape[0] // n_out
    for k in range(n_out):
        outs[k][...] = res[k * each : (k + 1) * each]


def one_hot_sums(z, info, sums_ref):
    n = CAP * z.rank
    shape = (z.ten_dev * z.rank, n)
    row = lax.broadcasted_iota(i32, shape, 0)
    col = lax.broadcasted_iota(i32, shape, 1)
    same = _rem(row, z.rank) == _rem(col, z.rank)
    row_slot = _div(row, z.rank)
    tables = [z.owner_and_order(info, k) for k in range(NEAR)]
    for j in range(z.n_far):
        holder = info[z.me] ^ (NEAR * j)
        parts = []
        for k in range(NEAR):
            owners, orders = tables[k]
            local = []
            for r in range(CAP):
                found = jnp.int32(0)
                for b in range(z.nb):
                    hit = (owners[b] == holder) & (orders[b] == r)
                    found = jnp.where(hit, _rem(z.slot(info, k, b), z.ten_dev), found)
                local.append(found)
            wanted = jnp.where(col < z.rank, local[0], local[1])
            parts.append(jnp.where(same & (row_slot == wanted), 1.0, 0.0))
        sums_ref[j] = jnp.concatenate(parts, axis=1).astype(bf16)


def dense_kernel(z, info, sums_ref, *refs):
    got, near_ref, far_refs = refs[:NEAR], refs[NEAR], refs[NEAR + 1 :]
    n = CAP * z.rank
    for j in range(z.n_far):
        stacked = jnp.concatenate([g[j * n : (j + 1) * n, :] for g in got], axis=0)
        total = _dot(sums_ref[j], stacked, NN)
        if j == 0:
            near_ref[...] = total
        else:
            far_refs[j - 1][...] = total.astype(bf16)


def final_kernel(parts, n_far, info, *refs):
    outs = refs[len(refs) - len(parts) :]
    i = 0
    for n, out in zip(parts, outs):
        at = 0
        for _ in range(n):
            total = refs[i][...]
            for r in refs[i + 1 : i + n_far]:
                total = total + r[...].astype(f32)
            out[:, at : at + total.shape[1]] = total
            at += total.shape[1]
            i += n_far


def choose_kernel(z, info, info_x, own_ref, far_ref, pair_ref, *outs):
    half = own_ref.shape[0]
    sources = (own_ref, pair_ref.at[:half], far_ref, pair_ref.at[half:])
    wanted = ((info, 0), (info, 1), (info_x, 0), (info_x, 1))
    for (table, which), out in zip(wanted, outs):
        for b in range(z.nb):
            s = z.slot(table, which, b)
            rel = _div(s, z.ten_dev) ^ info[z.me]
            at = _rem(rel, 2) * z.ten_dev + _rem(s, z.ten_dev)
            line = _div(rel, 2)
            v = sources[0][at]
            for k in range(1, 4):
                v = jnp.where(line == k, sources[k][at], v)
            out[z.ranks(b), :] = v


def shrink_kernel(z, n_parts, info, x_ref, *refs):
    parts, (full_ref, out_ref) = refs[:n_parts], refs[n_parts:]
    wide = z.width // n_parts
    total = None
    for j in range(n_parts):
        if n_parts == 1:
            cut = slice(0, wide)
        else:
            cut = pl.ds(pl.multiple_of((info[z.quarter] ^ j) * wide, wide), wide)
        full_ref[:, cut] = parts[j][...]
        term = _dot(x_ref[:, cut], parts[j][...], NT)
        total = term if total is None else total + term
    for b in range(z.nb):
        out_ref[:, z.block(b)] = total[z.block(b), :].T[z.ranks(b), :]


def projected_kernel(z, info, base_ref, mine_ref, other_ref, up_ref, out_ref, spread):
    spread[...] = jnp.zeros_like(spread)
    for b in range(z.nb):
        cut = z.block(b)
        spread[z.ranks(b), cut] = (mine_ref[:, cut] + other_ref[:, cut]).astype(bf16)
    wide = _dot(spread[...], up_ref[...], TN)
    for b in range(z.nb):
        cut = z.block(b)
        full = base_ref[cut, :] + adapter_scale * wide[cut]
        out_ref[cut, :] = _masked(full, z.valid(info, b)).astype(bf16)


def through_kernel(z, first, info, g_ref, w_ref, out_ref, *sums):
    step = out_ref.shape[1] // 4
    for h in range(4):
        cut = slice(h * step, (h + 1) * step)
        rows = slice(first + h * step, first + (h + 1) * step)
        out_ref[:, cut] = _dot(g_ref[...], w_ref[rows, :], NT)
    for s in sums:
        one_hot_sums(z, info, s)


def tokens_kernel(z, first, info, through_ref, mine_ref, other_ref, d_ref, *refs):
    out_ref, spread = refs[-2:]
    step = pl.program_id(0)
    wide = out_ref.shape[1]

    @pl.when(step == 0)
    def _():
        spread[...] = jnp.zeros_like(spread)
        for b in range(z.nb):
            cut = z.block(b)
            v = (mine_ref[:, cut] + other_ref[:, cut]) * adapter_scale
            spread[z.ranks(b), cut] = v.astype(bf16)

    here = pl.ds(pl.multiple_of(step * wide, wide), wide)
    cut = pl.ds(pl.multiple_of((first + step) * wide, wide), wide)
    added = _dot(spread[...], d_ref[:, cut], TN)
    out_ref[...] = (through_ref[:, here] + added).astype(bf16)


def on_device(
    n_groups,
    n_dp,
    tokens,
    base_weight,
    adapter_down,
    adapter_up,
    out_cotangent,
    block_tenant,
    block_valid,
    tenant_slot,
):
    nb = block_tenant.shape[0]
    rows, width = tokens.shape
    cols = out_cotangent.shape[1]
    tenants = tenant_slot.shape[0]
    ten_dev, _, rank = adapter_down.shape
    z = Sizes(n_dp, nb, ten_dev, rank, cols, width)
    n_far = z.n_far
    me = lax.axis_index("dp")
    core = lax.axis_index("tensor")
    group = lax.axis_index("groups")
    shared = n_groups == 2 and n_dp == 8
    n_parts = 4 if shared else 1
    mine_q = group * 2 + me % 2 if shared else jnp.int32(0)
    quarter = width // n_parts

    cotangent_other = _swap(out_cotangent, "tensor")

    down_t = jnp.swapaxes(adapter_down, 1, 2)
    if shared:
        to_y = lax.dynamic_slice_in_dim(down_t, (mine_q ^ 1) * quarter, quarter, axis=2)
        from_y = _xor(to_y, n_dp, 1)
    far_up = [_xor(adapter_up, n_dp, NEAR * j) for j in range(1, n_far)]
    lane = jnp.arange(LANES, dtype=i32)

    def spread_out(x):
        hit = lane[:, None] == jnp.arange(x.shape[0], dtype=i32)[None, :]
        return jnp.sum(jnp.where(hit, x[None, :], 0), axis=1).astype(i32)

    own_tenants = spread_out(block_tenant)
    tag = jnp.broadcast_to(own_tenants[None, :], (16, LANES)).astype(bf16)
    tag = jnp.pad(tag, ((0, 0), (0, cols - LANES)))
    ups = [u.reshape(ten_dev * rank, cols) for u in [adapter_up] + far_up]
    packet = jnp.concatenate(ups + [tag], axis=0)
    packets = [packet] + [_xor(packet, n_dp, k) for k in range(1, NEAR)]

    if shared:
        own = lax.dynamic_slice_in_dim(down_t, mine_q * quarter, quarter, axis=2)
        shard = jnp.concatenate([own, from_y], axis=0)
        shard_far = _xor(shard, n_dp, 4)

    line = lax.broadcasted_iota(i32, (16, LANES), 0)
    place = jnp.where(lane == 0, me, jnp.where(lane == 1, core, mine_q))
    info = jnp.where(line == 8, place[None, :], spread_out(block_valid)[None, :])
    info = jnp.where(line == 6, spread_out(tenant_slot)[None, :], info)
    info = jnp.where(line == 0, own_tenants[None, :], info)

    base_other, g_full, x_in = _call(
        functools.partial(base_kernel, z), "base", (1,),
        [pl.BlockSpec(memory_space=pl.ANY)] * 3 + [VMEM],
        [_whole((rows, cols))] + [VMEM] * 2,
        [
            _shape((rows, cols), bf16), _shape((rows, 2 * cols), bf16), _shape(tokens.shape, bf16),
        ],
        [
            pltpu.VMEM((width, cols), bf16), pltpu.VMEM((rows, cols), bf16),
            pltpu.SemaphoreType.DMA((5,)), pltpu.SemaphoreType.DMA((5,)),
            pltpu.SemaphoreType.DMA,
        ],
        vmem=BIG_VMEM,
    )(
        _tie(info, shard if shared else packet),
        tokens, base_weight, out_cotangent, cotangent_other,
    )
    base_arrived = _swap(base_other, "tensor")
    packets = [_tie(p, base_other) for p in packets]

    for k in range(1, NEAR):
        info = jnp.where(line == k, packets[k][-16, :LANES].astype(i32)[None, :], info)

    if shared:
        shard_far = _tie(shard_far, base_other)
        info = _tie(info, shard_far)
        farther = _xor(jnp.concatenate([shard, shard_far], axis=0), n_dp, 2)

    part = (rank, rows)
    block_up, back_part = _call(
        functools.partial(back_kernel, z), "back", (1,),
        [VMEM] * (1 + NEAR), [VMEM, _whole(part)],
        [_shape((nb * rank, cols), bf16), _shape(part, f32)], [],
    )(info, g_full, *packets)
    back_other = _swap(back_part, "tensor")
    ready = [base_arrived]
    if shared:
        info_x = _swap(info, "groups")

    packed_rows = n_dp * CAP * rank
    near_rows = packed_rows // NEAR

    def pack(info, start, wide):
        return _call(
            functools.partial(pack_kernel, z, NEAR, start), "pack_down", (1,),
            [VMEM] * 3, [_whole((near_rows, wide))] * NEAR,
            [_shape((near_rows, wide), bf16)] * NEAR,
            [pltpu.VMEM((packed_rows, rows), bf16)],
        )(info, back_part, back_other, x_in)

    def to_near(sends):
        return [sends[0]] + [_xor(sends[k], n_dp, k) for k in range(1, NEAR)]

    def dense(info, got):
        wide = got[0].shape[1]
        out = (ten_dev * rank, wide)
        return _call(
            functools.partial(dense_kernel, z), "dense", (1,),
            [VMEM] * (1 + NEAR), [VMEM] + [_whole(out)] * (n_far - 1),
            [_shape(out, f32)] + [_shape(out, bf16)] * (n_far - 1), [],
        )(info, sums, *got)

    def to_far(parts):
        return [parts[0]] + [_xor(parts[j], n_dp, NEAR * j) for j in range(1, n_far)]

    def through(info, first, wide, with_sums):
        sums = _shape((n_far, ten_dev * rank, NEAR * CAP * rank), bf16)
        return _call(
            functools.partial(through_kernel, z, first), "through", (1,), [VMEM] * 2,
            [VMEM] * (1 + with_sums), [_shape((rows, wide), f32)] + [sums] * with_sums, [],
        )(info, g_full, base_weight)

    half = width // 2
    wide_a = width * 5 // 8
    sends_a = pack(_tie(info, *ready), 0, wide_a)
    got_a = to_near(sends_a)
    low, sums = through(_tie(info, sends_a[0]), 0, half, 1)

    if shared:
        block = (nb * rank, quarter)
        chosen = _call(
            functools.partial(choose_kernel, z), "choose", (1,),
            [VMEM] * 3, [_whole(block)] * 4, [_shape(block, bf16)] * 4, [],
            n_scalars=2,
        )(_tie(info, low), info_x, shard, shard_far, farther)
        sends_b = pack(_tie(info, chosen[0]), wide_a, width - wide_a)
        got_y = _xor(_tie(chosen[1], got_a[2], sends_b[0]), n_dp, 1)
        got_x = _swap(_tie(chosen[2], sends_b[0]), "groups")
        got_d = lax.ppermute(
            _tie(chosen[3], sends_b[0]),
            ("groups", "dp"),
            [(g * n_dp + d, (1 - g) * n_dp + (d ^ 1)) for g in range(2) for d in range(n_dp)],
        )
    else:
        every = lax.all_gather(down_t, "dp", axis=0, tiled=True)
        slots = jnp.take(tenant_slot, block_tenant, axis=0)
        got_down = [jnp.take(every, slots, axis=0).reshape(nb * rank, width)]
        sends_b = pack(_tie(info, low), wide_a, width - wide_a)

    base_own = _call(
        functools.partial(own_kernel, z), "base_own", (1,),
        [VMEM] * 3, VMEM, _shape((rows, cols), f32), [],
    )(_tie(info, sends_b[0]), x_in, base_weight, base_arrived)
    dense_a = dense(_tie(info, base_own), got_a)
    far_a = to_far(dense_a)

    (high,) = through(_tie(info, dense_a[1]), half, width - half, 0)
    gate = [high] + ([got_y, got_x, got_d] if shared else [])
    got_b = to_near(
        [_tie(b, *gate) for k, b in enumerate(sends_b)]
    )

    if shared:
        got_down = [chosen[0], got_y, got_x, got_d]
    block_down, shrink_part = _call(
        functools.partial(shrink_kernel, z, n_parts), "shrink", (1,),
        [VMEM] * (1 + n_parts), [VMEM, _whole(part)],
        [_shape((nb * rank, width), bf16), _shape(part, f32)], [],
    )(_tie(info, high), x_in, *got_down)
    shrink_other = _swap(shrink_part, "tensor")


    step = min(512, width // 8)

    def token_grads(info, product, first, so_far):
        steps = product.shape[1] // step
        return _call(
            functools.partial(tokens_kernel, z, first), "token_grads", (steps,),
            [VMEM] * 4 + [pl.BlockSpec(memory_space=pl.ANY)] * len(so_far),
            pl.BlockSpec((rows, step), lambda i, *_: (0, first + i)),
            _shape((rows, width), bf16), [pltpu.VMEM((nb * rank, rows), bf16)],
            {5: 0} if so_far else None,
        )(info, product, back_part, back_other, block_down, *so_far)

    grad_tokens = token_grads(_tie(info, shrink_part), low, 0, [])

    up_sends = _call(
        functools.partial(pack_up_kernel, z, NEAR), "pack_up", (1,),
        [VMEM] * 3, [_whole((near_rows, cols))] * NEAR,
        [_shape((near_rows, cols), bf16)] * NEAR,
        [pltpu.VMEM((packed_rows, rows), bf16)],
    )(_tie(info, grad_tokens, far_a[1]), shrink_part, shrink_other, g_full)
    got_u = to_near(up_sends)

    dense_b = dense(_tie(info, up_sends[0]), got_b)
    far_b = to_far(dense_b)

    grad_tokens = token_grads(_tie(info, dense_b[1]), high, half // step, [grad_tokens])
    dense_u = dense(_tie(info, grad_tokens), got_u)
    far_u = to_far(dense_u)

    projected = _call(
        functools.partial(projected_kernel, z), "projected", (1,),
        [VMEM] * 4, _whole((rows, cols)), _shape((rows, cols), bf16),
        [pltpu.VMEM((nb * rank, rows), bf16)],
    )(
        _tie(info, dense_u[1]),
        base_own, shrink_part, shrink_other, block_up,
    )

    outs = [(ten_dev * rank, width), (ten_dev * rank, cols)]
    grad_down, grad_up = _call(
        functools.partial(final_kernel, (2, 1), n_far), "final", (1,),
        [VMEM] * (3 * n_far), [_whole(o) for o in outs], [_shape(o, f32) for o in outs], [],
    )(info, *far_a, *far_b, *far_u)
    grad_down = jnp.swapaxes(grad_down.reshape(ten_dev, rank, width), 1, 2)
    return projected, grad_tokens, grad_down, grad_up.reshape(ten_dev, rank, cols)


def solution(mesh):
    n_groups, n_dp = mesh.shape["groups"], mesh.shape["dp"]
    in_specs = (
        P(("groups", "dp"), "tensor"),
        P("tensor", None),
        P("dp", "tensor", None),
        P("dp", None, "tensor"),
        P(("groups", "dp"), "tensor"),
        P(("groups", "dp")),
        P(("groups", "dp")),
        P("groups"),
    )
    out_specs = (
        P(("groups", "dp"), "tensor"),
        P(("groups", "dp"), "tensor"),
        P(("groups", "dp"), "tensor", None),
        P(("groups", "dp"), None, "tensor"),
    )

    def run(*args):
        return on_device(n_groups, n_dp, *args)

    return jax.shard_map(
        run, mesh=mesh, in_specs=in_specs, out_specs=out_specs, check_vma=False
    )
```

```python
import functools

import jax
import jax.numpy as jnp
from jax import lax
from jax.experimental import pallas as pl
from jax.experimental.pallas import tpu as pltpu
from jax.sharding import PartitionSpec as P

TENANT_BLOCK = 128
CAP = 2
NEAR = 4
VMEM_LIMIT = 9 * 1024 * 1024
BIG_VMEM = 36 * 1024 * 1024
LANES = 128

adapter_scale = 2.0
f32 = jnp.float32
bf16 = jnp.bfloat16
i32 = jnp.int32

NT = (((1,), (1,)), ((), ()))
TN = (((0,), (0,)), ((), ()))
NN = (((1,), (0,)), ((), ()))


def _dot(a, b, dims):
    return lax.dot_general(a, b, dims, preferred_element_type=f32)


def _swap(x, axis):
    return lax.ppermute(x, axis, [(0, 1), (1, 0)])


def _xor(x, n, k):
    return lax.ppermute(x, "dp", [(i, i ^ k) for i in range(n)])


def _tie(x, *after):
    return lax.optimization_barrier((x,) + after)[0]


def _div(a, n):
    return a >> (n.bit_length() - 1) if n & (n - 1) == 0 else lax.div(a, jnp.int32(n))


def _rem(a, n):
    return a & (n - 1) if n & (n - 1) == 0 else lax.rem(a, jnp.int32(n))


VMEM = pl.BlockSpec(memory_space=pltpu.VMEM)


def _shape(shape, dtype):
    return jax.ShapeDtypeStruct(shape, dtype)


def _call(
    body, name, grid, in_specs, out_specs, out_shape, scratch, aliases=None, vmem=VMEM_LIMIT,
    n_scalars=1,
):
    return pl.pallas_call(
        body,
        name=name,
        grid_spec=pltpu.PrefetchScalarGridSpec(
            num_scalar_prefetch=n_scalars,
            grid=grid,
            in_specs=in_specs,
            out_specs=out_specs,
            scratch_shapes=scratch,
        ),
        out_shape=out_shape,
        input_output_aliases=aliases or {},
        compiler_params=pltpu.CompilerParams(vmem_limit_bytes=vmem),
        cost_estimate=pl.CostEstimate(flops=1, bytes_accessed=1, transcendentals=0),
    )


def _whole(shape):
    return pl.BlockSpec(shape, lambda *_: (0,) * len(shape))


class Sizes:
    def __init__(self, n_dp, nb, ten_dev, rank, cols, width):
        self.n_dp, self.nb, self.ten_dev = n_dp, nb, ten_dev
        self.rank, self.cols, self.width = rank, cols, width
        self.n_far = n_dp // NEAR
        self.rows = nb * TENANT_BLOCK
        self.me, self.core, self.quarter = (8, 0), (8, 1), (8, 2)

    def block(self, b):
        return slice(b * TENANT_BLOCK, (b + 1) * TENANT_BLOCK)

    def ranks(self, b):
        return slice(b * self.rank, (b + 1) * self.rank)

    def slot(self, info, which, b):
        return info[6, info[which, b]]

    def valid(self, info, b):
        return info[9, b]

    def owner_and_order(self, info, which):
        owners = [_div(self.slot(info, which, b), self.ten_dev) for b in range(self.nb)]
        orders = []
        for b in range(self.nb):
            n = jnp.int32(0)
            for c in range(b):
                n = n + jnp.where(owners[c] == owners[b], 1, 0)
            orders.append(n)
        return owners, orders

    def places(self, info):
        owners, orders = self.owner_and_order(info, 0)
        out = []
        for o, r in zip(owners, orders):
            rel = o ^ info[self.me]
            place = (_rem(rel, NEAR) * self.n_far + _div(rel, NEAR)) * CAP + r
            out.append(pl.ds(pl.multiple_of(place * self.rank, self.rank), self.rank))
        return out


def _masked(x, valid):
    row = lax.broadcasted_iota(i32, x.shape, 0)
    return jnp.where(row < valid, x, jnp.zeros((), x.dtype))


def base_kernel(
    z, info, x_hbm, w_hbm, g_hbm, h_ref, far_ref, full_ref, x_ref, w_ref, g_ref, x_sem, w_sem, g_sem
):
    own = pl.ds(pl.multiple_of(info[z.core] * z.cols, z.cols), z.cols)
    far = pl.ds(pl.multiple_of((1 - info[z.core]) * z.cols, z.cols), z.cols)
    unit = z.width // 8
    g = pltpu.make_async_copy(g_hbm, g_ref, g_sem)
    g.start()
    copies = []
    for i, (first, last) in enumerate(((0, 1), (1, 3), (3, 5), (5, 7), (7, 8))):
        cut = pl.ds(first * unit, (last - first) * unit)
        x = pltpu.make_async_copy(x_hbm.at[:, cut], x_ref.at[:, cut], x_sem.at[i])
        w = pltpu.make_async_copy(w_hbm.at[cut, far], w_ref.at[cut], w_sem.at[i])
        x.start()
        w.start()
        copies.append((x, w, cut))
    g.wait()
    for b in range(z.nb):
        cut = z.block(b)
        full_ref[cut, own] = _masked(g_ref[cut, :], z.valid(info, b))
        full_ref[cut, far] = _masked(h_ref[cut, :], z.valid(info, b))
    total = None
    for x, w, cut in copies:
        x.wait()
        w.wait()
        term = _dot(x_ref[:, cut], w_ref[cut, :], NN)
        total = term if total is None else total + term
    far_ref[...] = total.astype(bf16)


def own_kernel(z, info, x_ref, w_ref, far_ref, out_ref):
    own = pl.ds(pl.multiple_of(info[z.core] * z.cols, z.cols), z.cols)
    out_ref[...] = _dot(x_ref[...], w_ref[:, own], NN) + far_ref[...].astype(f32)


def back_kernel(z, info, g_ref, *refs):
    packets, (up_ref, part_ref) = refs[:NEAR], refs[NEAR:]
    own = pl.ds(pl.multiple_of(info[z.core] * z.cols, z.cols), z.cols)
    for b in range(z.nb):
        s = z.slot(info, 0, b)
        rel = _div(s, z.ten_dev) ^ info[z.me]
        at = _div(rel, NEAR) * z.ten_dev + _rem(s, z.ten_dev)
        at = pl.ds(pl.multiple_of(at * z.rank, z.rank), z.rank)
        near = _rem(rel, NEAR)
        u = packets[0][at, :]
        for k in range(1, NEAR):
            u = jnp.where(near == k, packets[k][at, :], u)
        up_ref[z.ranks(b), :] = u
        part_ref[:, z.block(b)] = _dot(u, g_ref[z.block(b), own], NT)


def pack_kernel(z, n_out, start, info, mine_ref, other_ref, x_ref, *refs):
    outs, packed = refs[:n_out], refs[n_out]
    packed[...] = jnp.zeros_like(packed)
    for b, place in enumerate(z.places(info)):
        cut = z.block(b)
        v = (mine_ref[:, cut] + other_ref[:, cut]) * adapter_scale
        packed[place, cut] = v.astype(bf16)
    wide = outs[0].shape[1]
    res = _dot(packed[...], x_ref[:, start : start + wide], NN).astype(bf16)
    each = res.shape[0] // n_out
    for k in range(n_out):
        outs[k][...] = res[k * each : (k + 1) * each]


def pack_up_kernel(z, n_out, info, mine_ref, other_ref, g_ref, *refs):
    outs, packed = refs[:n_out], refs[n_out]
    own = pl.ds(pl.multiple_of(info[z.core] * z.cols, z.cols), z.cols)
    packed[...] = jnp.zeros_like(packed)
    for b, place in enumerate(z.places(info)):
        cut = z.block(b)
        packed[place, cut] = (mine_ref[:, cut] + other_ref[:, cut]).astype(bf16)
    res = (adapter_scale * _dot(packed[...], g_ref[:, own], NN)).astype(bf16)
    each = res.shape[0] // n_out
    for k in range(n_out):
        outs[k][...] = res[k * each : (k + 1) * each]


def one_hot_sums(z, info, sums_ref):
    n = CAP * z.rank
    shape = (z.ten_dev * z.rank, n)
    row = lax.broadcasted_iota(i32, shape, 0)
    col = lax.broadcasted_iota(i32, shape, 1)
    same = _rem(row, z.rank) == _rem(col, z.rank)
    row_slot = _div(row, z.rank)
    tables = [z.owner_and_order(info, k) for k in range(NEAR)]
    for j in range(z.n_far):
        holder = info[z.me] ^ (NEAR * j)
        parts = []
        for k in range(NEAR):
            owners, orders = tables[k]
            local = []
            for r in range(CAP):
                found = jnp.int32(0)
                for b in range(z.nb):
                    hit = (owners[b] == holder) & (orders[b] == r)
                    found = jnp.where(hit, _rem(z.slot(info, k, b), z.ten_dev), found)
                local.append(found)
            wanted = jnp.where(col < z.rank, local[0], local[1])
            parts.append(jnp.where(same & (row_slot == wanted), 1.0, 0.0))
        sums_ref[j] = jnp.concatenate(parts, axis=1).astype(bf16)


def dense_kernel(z, info, sums_ref, *refs):
    got, near_ref, far_refs = refs[:NEAR], refs[NEAR], refs[NEAR + 1 :]
    n = CAP * z.rank
    for j in range(z.n_far):
        stacked = jnp.concatenate([g[j * n : (j + 1) * n, :] for g in got], axis=0)
        total = _dot(sums_ref[j], stacked, NN)
        if j == 0:
            near_ref[...] = total
        else:
            far_refs[j - 1][...] = total.astype(bf16)


def final_kernel(parts, n_far, info, *refs):
    outs = refs[len(refs) - len(parts) :]
    i = 0
    for n, out in zip(parts, outs):
        at = 0
        for _ in range(n):
            total = refs[i][...]
            for r in refs[i + 1 : i + n_far]:
                total = total + r[...].astype(f32)
            out[:, at : at + total.shape[1]] = total
            at += total.shape[1]
            i += n_far


def choose_kernel(z, info, info_x, own_ref, far_ref, pair_ref, *outs):
    half = own_ref.shape[0]
    sources = (own_ref, pair_ref.at[:half], far_ref, pair_ref.at[half:])
    wanted = ((info, 0), (info, 1), (info_x, 0), (info_x, 1))
    for (table, which), out in zip(wanted, outs):
        for b in range(z.nb):
            s = z.slot(table, which, b)
            rel = _div(s, z.ten_dev) ^ info[z.me]
            at = _rem(rel, 2) * z.ten_dev + _rem(s, z.ten_dev)
            line = _div(rel, 2)
            v = sources[0][at]
            for k in range(1, 4):
                v = jnp.where(line == k, sources[k][at], v)
            out[z.ranks(b), :] = v


def shrink_kernel(z, n_parts, info, x_ref, *refs):
    parts, (full_ref, out_ref) = refs[:n_parts], refs[n_parts:]
    wide = z.width // n_parts
    total = None
    for j in range(n_parts):
        if n_parts == 1:
            cut = slice(0, wide)
        else:
            cut = pl.ds(pl.multiple_of((info[z.quarter] ^ j) * wide, wide), wide)
        full_ref[:, cut] = parts[j][...]
        term = _dot(x_ref[:, cut], parts[j][...], NT)
        total = term if total is None else total + term
    for b in range(z.nb):
        out_ref[:, z.block(b)] = total[z.block(b), :].T[z.ranks(b), :]


def projected_kernel(z, info, base_ref, mine_ref, other_ref, up_ref, out_ref, spread):
    spread[...] = jnp.zeros_like(spread)
    for b in range(z.nb):
        cut = z.block(b)
        spread[z.ranks(b), cut] = (mine_ref[:, cut] + other_ref[:, cut]).astype(bf16)
    wide = _dot(spread[...], up_ref[...], TN)
    for b in range(z.nb):
        cut = z.block(b)
        full = base_ref[cut, :] + adapter_scale * wide[cut]
        out_ref[cut, :] = _masked(full, z.valid(info, b)).astype(bf16)


def through_kernel(z, first, info, g_ref, w_ref, out_ref, *sums):
    step = out_ref.shape[1] // 4
    for h in range(4):
        cut = slice(h * step, (h + 1) * step)
        rows = slice(first + h * step, first + (h + 1) * step)
        out_ref[:, cut] = _dot(g_ref[...], w_ref[rows, :], NT)
    for s in sums:
        one_hot_sums(z, info, s)


def tokens_kernel(z, first, info, through_ref, mine_ref, other_ref, d_ref, *refs):
    out_ref, spread = refs[-2:]
    step = pl.program_id(0)
    wide = out_ref.shape[1]

    @pl.when(step == 0)
    def _():
        spread[...] = jnp.zeros_like(spread)
        for b in range(z.nb):
            cut = z.block(b)
            v = (mine_ref[:, cut] + other_ref[:, cut]) * adapter_scale
            spread[z.ranks(b), cut] = v.astype(bf16)

    here = pl.ds(pl.multiple_of(step * wide, wide), wide)
    cut = pl.ds(pl.multiple_of((first + step) * wide, wide), wide)
    added = _dot(spread[...], d_ref[:, cut], TN)
    out_ref[...] = (through_ref[:, here] + added).astype(bf16)


def on_device(
    n_groups,
    n_dp,
    tokens,
    base_weight,
    adapter_down,
    adapter_up,
    out_cotangent,
    block_tenant,
    block_valid,
    tenant_slot,
):
    nb = block_tenant.shape[0]
    rows, width = tokens.shape
    cols = out_cotangent.shape[1]
    tenants = tenant_slot.shape[0]
    ten_dev, _, rank = adapter_down.shape
    z = Sizes(n_dp, nb, ten_dev, rank, cols, width)
    n_far = z.n_far
    me = lax.axis_index("dp")
    core = lax.axis_index("tensor")
    group = lax.axis_index("groups")
    shared = n_groups == 2 and n_dp == 8
    n_parts = 4 if shared else 1
    mine_q = group * 2 + me % 2 if shared else jnp.int32(0)
    quarter = width // n_parts

    cotangent_other = _swap(out_cotangent, "tensor")

    down_t = jnp.swapaxes(adapter_down, 1, 2)
    if shared:
        to_y = lax.dynamic_slice_in_dim(down_t, (mine_q ^ 1) * quarter, quarter, axis=2)
        from_y = _xor(to_y, n_dp, 1)
    far_up = [_xor(adapter_up, n_dp, NEAR * j) for j in range(1, n_far)]
    lane = jnp.arange(LANES, dtype=i32)

    def spread_out(x):
        hit = lane[:, None] == jnp.arange(x.shape[0], dtype=i32)[None, :]
        return jnp.sum(jnp.where(hit, x[None, :], 0), axis=1).astype(i32)

    own_tenants = spread_out(block_tenant)
    tag = jnp.broadcast_to(own_tenants[None, :], (16, LANES)).astype(bf16)
    tag = jnp.pad(tag, ((0, 0), (0, cols - LANES)))
    ups = [u.reshape(ten_dev * rank, cols) for u in [adapter_up] + far_up]
    packet = jnp.concatenate(ups + [tag], axis=0)
    packets = [packet] + [_xor(packet, n_dp, k) for k in range(1, NEAR)]

    if shared:
        own = lax.dynamic_slice_in_dim(down_t, mine_q * quarter, quarter, axis=2)
        shard = jnp.concatenate([own, from_y], axis=0)
        shard_far = _xor(shard, n_dp, 4)

    line = lax.broadcasted_iota(i32, (16, LANES), 0)
    place = jnp.where(lane == 0, me, jnp.where(lane == 1, core, mine_q))
    info = jnp.where(line == 8, place[None, :], spread_out(block_valid)[None, :])
    info = jnp.where(line == 6, spread_out(tenant_slot)[None, :], info)
    info = jnp.where(line == 0, own_tenants[None, :], info)

    base_other, g_full, x_in = _call(
        functools.partial(base_kernel, z), "base", (1,),
        [pl.BlockSpec(memory_space=pl.ANY)] * 3 + [VMEM],
        [_whole((rows, cols))] + [VMEM] * 2,
        [
            _shape((rows, cols), bf16), _shape((rows, 2 * cols), bf16), _shape(tokens.shape, bf16),
        ],
        [
            pltpu.VMEM((width, cols), bf16), pltpu.VMEM((rows, cols), bf16),
            pltpu.SemaphoreType.DMA((5,)), pltpu.SemaphoreType.DMA((5,)),
            pltpu.SemaphoreType.DMA,
        ],
        vmem=BIG_VMEM,
    )(
        _tie(info, shard if shared else packet),
        tokens, base_weight, out_cotangent, cotangent_other,
    )
    base_arrived = _swap(base_other, "tensor")
    packets = [_tie(p, base_other) for p in packets]

    for k in range(1, NEAR):
        info = jnp.where(line == k, packets[k][-16, :LANES].astype(i32)[None, :], info)

    if shared:
        shard_far = _tie(shard_far, base_other)
        info = _tie(info, shard_far)
        farther = _xor(jnp.concatenate([shard, shard_far], axis=0), n_dp, 2)

    part = (rank, rows)
    block_up, back_part = _call(
        functools.partial(back_kernel, z), "back", (1,),
        [VMEM] * (1 + NEAR), [VMEM, _whole(part)],
        [_shape((nb * rank, cols), bf16), _shape(part, f32)], [],
    )(info, g_full, *packets)
    back_other = _swap(back_part, "tensor")
    ready = [base_arrived]
    if shared:
        info_x = _swap(info, "groups")

    packed_rows = n_dp * CAP * rank
    near_rows = packed_rows // NEAR

    def pack(info, start, wide):
        return _call(
            functools.partial(pack_kernel, z, NEAR, start), "pack_down", (1,),
            [VMEM] * 3, [_whole((near_rows, wide))] * NEAR,
            [_shape((near_rows, wide), bf16)] * NEAR,
            [pltpu.VMEM((packed_rows, rows), bf16)],
        )(info, back_part, back_other, x_in)

    def to_near(sends):
        return [sends[0]] + [_xor(sends[k], n_dp, k) for k in range(1, NEAR)]

    def dense(info, got):
        wide = got[0].shape[1]
        out = (ten_dev * rank, wide)
        return _call(
            functools.partial(dense_kernel, z), "dense", (1,),
            [VMEM] * (1 + NEAR), [VMEM] + [_whole(out)] * (n_far - 1),
            [_shape(out, f32)] + [_shape(out, bf16)] * (n_far - 1), [],
        )(info, sums, *got)

    def to_far(parts):
        return [parts[0]] + [_xor(parts[j], n_dp, NEAR * j) for j in range(1, n_far)]

    def through(info, first, wide, with_sums):
        sums = _shape((n_far, ten_dev * rank, NEAR * CAP * rank), bf16)
        return _call(
            functools.partial(through_kernel, z, first), "through", (1,), [VMEM] * 2,
            [VMEM] * (1 + with_sums), [_shape((rows, wide), f32)] + [sums] * with_sums, [],
        )(info, g_full, base_weight)

    half = width // 2
    wide_a = half
    sends_a = pack(_tie(info, *ready), 0, wide_a)
    got_a = to_near(sends_a)
    low, sums = through(_tie(info, sends_a[0]), 0, half, 1)

    if shared:
        block = (nb * rank, quarter)
        chosen = _call(
            functools.partial(choose_kernel, z), "choose", (1,),
            [VMEM] * 3, [_whole(block)] * 4, [_shape(block, bf16)] * 4, [],
            n_scalars=2,
        )(_tie(info, low), info_x, shard, shard_far, farther)
        sends_b = pack(_tie(info, chosen[0]), wide_a, width - wide_a)
        got_y = _xor(_tie(chosen[1], got_a[2], sends_b[0]), n_dp, 1)
        got_x = _swap(_tie(chosen[2], sends_b[0]), "groups")
        got_d = lax.ppermute(
            _tie(chosen[3], sends_b[0]),
            ("groups", "dp"),
            [(g * n_dp + d, (1 - g) * n_dp + (d ^ 1)) for g in range(2) for d in range(n_dp)],
        )
    else:
        every = lax.all_gather(down_t, "dp", axis=0, tiled=True)
        slots = jnp.take(tenant_slot, block_tenant, axis=0)
        got_down = [jnp.take(every, slots, axis=0).reshape(nb * rank, width)]
        sends_b = pack(_tie(info, low), wide_a, width - wide_a)

    base_own = _call(
        functools.partial(own_kernel, z), "base_own", (1,),
        [VMEM] * 3, VMEM, _shape((rows, cols), f32), [],
    )(_tie(info, sends_b[0]), x_in, base_weight, base_arrived)
    dense_a = dense(_tie(info, base_own), got_a)
    far_a = to_far(dense_a)

    (high,) = through(_tie(info, dense_a[1]), half, width - half, 0)
    gate = [high] + ([got_y] if shared else [])
    got_b = to_near(
        [_tie(b, *gate) if k in (1, 3) else _tie(b, dense_a[1]) for k, b in enumerate(sends_b)]
    )

    if shared:
        got_down = [chosen[0], got_y, got_x, got_d]
    block_down, shrink_part = _call(
        functools.partial(shrink_kernel, z, n_parts), "shrink", (1,),
        [VMEM] * (1 + n_parts), [VMEM, _whole(part)],
        [_shape((nb * rank, width), bf16), _shape(part, f32)], [],
    )(_tie(info, high), x_in, *got_down)
    shrink_other = _swap(shrink_part, "tensor")


    step = min(512, width // 8)

    def token_grads(info, product, first, so_far):
        steps = product.shape[1] // step
        return _call(
            functools.partial(tokens_kernel, z, first), "token_grads", (steps,),
            [VMEM] * 4 + [pl.BlockSpec(memory_space=pl.ANY)] * len(so_far),
            pl.BlockSpec((rows, step), lambda i, *_: (0, first + i)),
            _shape((rows, width), bf16), [pltpu.VMEM((nb * rank, rows), bf16)],
            {5: 0} if so_far else None,
        )(info, product, back_part, back_other, block_down, *so_far)

    grad_tokens = token_grads(_tie(info, shrink_part), low, 0, [])

    up_sends = _call(
        functools.partial(pack_up_kernel, z, NEAR), "pack_up", (1,),
        [VMEM] * 3, [_whole((near_rows, cols))] * NEAR,
        [_shape((near_rows, cols), bf16)] * NEAR,
        [pltpu.VMEM((packed_rows, rows), bf16)],
    )(_tie(info, grad_tokens, far_a[1]), shrink_part, shrink_other, g_full)
    got_u = to_near(up_sends)

    dense_b = dense(_tie(info, up_sends[0]), got_b)
    far_b = to_far(dense_b)

    grad_tokens = token_grads(_tie(info, dense_b[1]), high, half // step, [grad_tokens])
    dense_u = dense(_tie(info, grad_tokens), got_u)
    far_u = to_far(dense_u)

    projected = _call(
        functools.partial(projected_kernel, z), "projected", (1,),
        [VMEM] * 4, _whole((rows, cols)), _shape((rows, cols), bf16),
        [pltpu.VMEM((nb * rank, rows), bf16)],
    )(
        _tie(info, dense_u[1]),
        base_own, shrink_part, shrink_other, block_up,
    )

    outs = [(ten_dev * rank, width), (ten_dev * rank, cols)]
    grad_down, grad_up = _call(
        functools.partial(final_kernel, (2, 1), n_far), "final", (1,),
        [VMEM] * (3 * n_far), [_whole(o) for o in outs], [_shape(o, f32) for o in outs], [],
    )(info, *far_a, *far_b, *far_u)
    grad_down = jnp.swapaxes(grad_down.reshape(ten_dev, rank, width), 1, 2)
    return projected, grad_tokens, grad_down, grad_up.reshape(ten_dev, rank, cols)


def solution(mesh):
    n_groups, n_dp = mesh.shape["groups"], mesh.shape["dp"]
    in_specs = (
        P(("groups", "dp"), "tensor"),
        P("tensor", None),
        P("dp", "tensor", None),
        P("dp", None, "tensor"),
        P(("groups", "dp"), "tensor"),
        P(("groups", "dp")),
        P(("groups", "dp")),
        P("groups"),
    )
    out_specs = (
        P(("groups", "dp"), "tensor"),
        P(("groups", "dp"), "tensor"),
        P(("groups", "dp"), "tensor", None),
        P(("groups", "dp"), None, "tensor"),
    )

    def run(*args):
        return on_device(n_groups, n_dp, *args)

    return jax.shard_map(
        run, mesh=mesh, in_specs=in_specs, out_specs=out_specs, check_vma=False
    )
```

```python
import functools

import jax
import jax.numpy as jnp
from jax import lax
from jax.experimental import pallas as pl
from jax.experimental.pallas import tpu as pltpu
from jax.sharding import PartitionSpec as P

TENANT_BLOCK = 128
CAP = 2
NEAR = 4
VMEM_LIMIT = 9 * 1024 * 1024
BIG_VMEM = 36 * 1024 * 1024
LANES = 128

adapter_scale = 2.0
f32 = jnp.float32
bf16 = jnp.bfloat16
i32 = jnp.int32

NT = (((1,), (1,)), ((), ()))
TN = (((0,), (0,)), ((), ()))
NN = (((1,), (0,)), ((), ()))


def _dot(a, b, dims):
    return lax.dot_general(a, b, dims, preferred_element_type=f32)


def _swap(x, axis):
    return lax.ppermute(x, axis, [(0, 1), (1, 0)])


def _xor(x, n, k):
    return lax.ppermute(x, "dp", [(i, i ^ k) for i in range(n)])


def _tie(x, *after):
    return lax.optimization_barrier((x,) + after)[0]


def _div(a, n):
    return a >> (n.bit_length() - 1) if n & (n - 1) == 0 else lax.div(a, jnp.int32(n))


def _rem(a, n):
    return a & (n - 1) if n & (n - 1) == 0 else lax.rem(a, jnp.int32(n))


VMEM = pl.BlockSpec(memory_space=pltpu.VMEM)


def _shape(shape, dtype):
    return jax.ShapeDtypeStruct(shape, dtype)


def _call(
    body, name, grid, in_specs, out_specs, out_shape, scratch, aliases=None, vmem=VMEM_LIMIT,
    n_scalars=1,
):
    return pl.pallas_call(
        body,
        name=name,
        grid_spec=pltpu.PrefetchScalarGridSpec(
            num_scalar_prefetch=n_scalars,
            grid=grid,
            in_specs=in_specs,
            out_specs=out_specs,
            scratch_shapes=scratch,
        ),
        out_shape=out_shape,
        input_output_aliases=aliases or {},
        compiler_params=pltpu.CompilerParams(vmem_limit_bytes=vmem),
        cost_estimate=pl.CostEstimate(flops=1, bytes_accessed=1, transcendentals=0),
    )


def _whole(shape):
    return pl.BlockSpec(shape, lambda *_: (0,) * len(shape))


class Sizes:
    def __init__(self, n_dp, nb, ten_dev, rank, cols, width):
        self.n_dp, self.nb, self.ten_dev = n_dp, nb, ten_dev
        self.rank, self.cols, self.width = rank, cols, width
        self.n_far = n_dp // NEAR
        self.rows = nb * TENANT_BLOCK
        self.me, self.core, self.quarter = (8, 0), (8, 1), (8, 2)

    def block(self, b):
        return slice(b * TENANT_BLOCK, (b + 1) * TENANT_BLOCK)

    def ranks(self, b):
        return slice(b * self.rank, (b + 1) * self.rank)

    def slot(self, info, which, b):
        return info[6, info[which, b]]

    def valid(self, info, b):
        return info[9, b]

    def owner_and_order(self, info, which):
        owners = [_div(self.slot(info, which, b), self.ten_dev) for b in range(self.nb)]
        orders = []
        for b in range(self.nb):
            n = jnp.int32(0)
            for c in range(b):
                n = n + jnp.where(owners[c] == owners[b], 1, 0)
            orders.append(n)
        return owners, orders

    def places(self, info):
        owners, orders = self.owner_and_order(info, 0)
        out = []
        for o, r in zip(owners, orders):
            rel = o ^ info[self.me]
            place = (_rem(rel, NEAR) * self.n_far + _div(rel, NEAR)) * CAP + r
            out.append(pl.ds(pl.multiple_of(place * self.rank, self.rank), self.rank))
        return out


def _masked(x, valid):
    row = lax.broadcasted_iota(i32, x.shape, 0)
    return jnp.where(row < valid, x, jnp.zeros((), x.dtype))


def base_kernel(
    z, info, x_hbm, w_hbm, g_hbm, h_ref, far_ref, full_ref, x_ref, w_ref, g_ref, x_sem, w_sem, g_sem
):
    own = pl.ds(pl.multiple_of(info[z.core] * z.cols, z.cols), z.cols)
    far = pl.ds(pl.multiple_of((1 - info[z.core]) * z.cols, z.cols), z.cols)
    unit = z.width // 8
    g = pltpu.make_async_copy(g_hbm, g_ref, g_sem)
    g.start()
    copies = []
    for i, (first, last) in enumerate(((0, 1), (1, 3), (3, 5), (5, 7), (7, 8))):
        cut = pl.ds(first * unit, (last - first) * unit)
        x = pltpu.make_async_copy(x_hbm.at[:, cut], x_ref.at[:, cut], x_sem.at[i])
        w = pltpu.make_async_copy(w_hbm.at[cut, far], w_ref.at[cut], w_sem.at[i])
        x.start()
        w.start()
        copies.append((x, w, cut))
    g.wait()
    for b in range(z.nb):
        cut = z.block(b)
        full_ref[cut, own] = _masked(g_ref[cut, :], z.valid(info, b))
        full_ref[cut, far] = _masked(h_ref[cut, :], z.valid(info, b))
    total = None
    for x, w, cut in copies:
        x.wait()
        w.wait()
        term = _dot(x_ref[:, cut], w_ref[cut, :], NN)
        total = term if total is None else total + term
    far_ref[...] = total.astype(bf16)


def own_kernel(z, info, x_ref, w_ref, far_ref, out_ref):
    own = pl.ds(pl.multiple_of(info[z.core] * z.cols, z.cols), z.cols)
    out_ref[...] = _dot(x_ref[...], w_ref[:, own], NN) + far_ref[...].astype(f32)


def back_kernel(z, info, g_ref, *refs):
    packets, (up_ref, part_ref) = refs[:NEAR], refs[NEAR:]
    own = pl.ds(pl.multiple_of(info[z.core] * z.cols, z.cols), z.cols)
    for b in range(z.nb):
        s = z.slot(info, 0, b)
        rel = _div(s, z.ten_dev) ^ info[z.me]
        at = _div(rel, NEAR) * z.ten_dev + _rem(s, z.ten_dev)
        at = pl.ds(pl.multiple_of(at * z.rank, z.rank), z.rank)
        near = _rem(rel, NEAR)
        u = packets[0][at, :]
        for k in range(1, NEAR):
            u = jnp.where(near == k, packets[k][at, :], u)
        up_ref[z.ranks(b), :] = u
        part_ref[:, z.block(b)] = _dot(u, g_ref[z.block(b), own], NT)


def pack_kernel(z, n_out, start, info, mine_ref, other_ref, x_ref, *refs):
    outs, packed = refs[:n_out], refs[n_out]
    packed[...] = jnp.zeros_like(packed)
    for b, place in enumerate(z.places(info)):
        cut = z.block(b)
        v = (mine_ref[:, cut] + other_ref[:, cut]) * adapter_scale
        packed[place, cut] = v.astype(bf16)
    wide = outs[0].shape[1]
    res = _dot(packed[...], x_ref[:, start : start + wide], NN).astype(bf16)
    each = res.shape[0] // n_out
    for k in range(n_out):
        outs[k][...] = res[k * each : (k + 1) * each]


def pack_up_kernel(z, n_out, info, mine_ref, other_ref, g_ref, *refs):
    outs, packed = refs[:n_out], refs[n_out]
    own = pl.ds(pl.multiple_of(info[z.core] * z.cols, z.cols), z.cols)
    packed[...] = jnp.zeros_like(packed)
    for b, place in enumerate(z.places(info)):
        cut = z.block(b)
        packed[place, cut] = (mine_ref[:, cut] + other_ref[:, cut]).astype(bf16)
    res = (adapter_scale * _dot(packed[...], g_ref[:, own], NN)).astype(bf16)
    each = res.shape[0] // n_out
    for k in range(n_out):
        outs[k][...] = res[k * each : (k + 1) * each]


def one_hot_sums(z, info, sums_ref):
    n = CAP * z.rank
    shape = (z.ten_dev * z.rank, n)
    row = lax.broadcasted_iota(i32, shape, 0)
    col = lax.broadcasted_iota(i32, shape, 1)
    same = _rem(row, z.rank) == _rem(col, z.rank)
    row_slot = _div(row, z.rank)
    tables = [z.owner_and_order(info, k) for k in range(NEAR)]
    for j in range(z.n_far):
        holder = info[z.me] ^ (NEAR * j)
        parts = []
        for k in range(NEAR):
            owners, orders = tables[k]
            local = []
            for r in range(CAP):
                found = jnp.int32(0)
                for b in range(z.nb):
                    hit = (owners[b] == holder) & (orders[b] == r)
                    found = jnp.where(hit, _rem(z.slot(info, k, b), z.ten_dev), found)
                local.append(found)
            wanted = jnp.where(col < z.rank, local[0], local[1])
            parts.append(jnp.where(same & (row_slot == wanted), 1.0, 0.0))
        sums_ref[j] = jnp.concatenate(parts, axis=1).astype(bf16)


def dense_kernel(z, info, sums_ref, *refs):
    got, near_ref, far_refs = refs[:NEAR], refs[NEAR], refs[NEAR + 1 :]
    n = CAP * z.rank
    for j in range(z.n_far):
        stacked = jnp.concatenate([g[j * n : (j + 1) * n, :] for g in got], axis=0)
        total = _dot(sums_ref[j], stacked, NN)
        if j == 0:
            near_ref[...] = total
        else:
            far_refs[j - 1][...] = total.astype(bf16)


def final_kernel(parts, n_far, info, *refs):
    outs = refs[len(refs) - len(parts) :]
    i = 0
    for n, out in zip(parts, outs):
        at = 0
        for _ in range(n):
            total = refs[i][...]
            for r in refs[i + 1 : i + n_far]:
                total = total + r[...].astype(f32)
            out[:, at : at + total.shape[1]] = total
            at += total.shape[1]
            i += n_far


def choose_kernel(z, info, info_x, own_ref, far_ref, pair_ref, *outs):
    half = own_ref.shape[0]
    sources = (own_ref, pair_ref.at[:half], far_ref, pair_ref.at[half:])
    wanted = ((info, 0), (info, 1), (info_x, 0), (info_x, 1))
    for (table, which), out in zip(wanted, outs):
        for b in range(z.nb):
            s = z.slot(table, which, b)
            rel = _div(s, z.ten_dev) ^ info[z.me]
            at = _rem(rel, 2) * z.ten_dev + _rem(s, z.ten_dev)
            line = _div(rel, 2)
            v = sources[0][at]
            for k in range(1, 4):
                v = jnp.where(line == k, sources[k][at], v)
            out[z.ranks(b), :] = v


def shrink_kernel(z, n_parts, info, x_ref, *refs):
    parts, (full_ref, out_ref) = refs[:n_parts], refs[n_parts:]
    wide = z.width // n_parts
    total = None
    for j in range(n_parts):
        if n_parts == 1:
            cut = slice(0, wide)
        else:
            cut = pl.ds(pl.multiple_of((info[z.quarter] ^ j) * wide, wide), wide)
        full_ref[:, cut] = parts[j][...]
        term = _dot(x_ref[:, cut], parts[j][...], NT)
        total = term if total is None else total + term
    for b in range(z.nb):
        out_ref[:, z.block(b)] = total[z.block(b), :].T[z.ranks(b), :]


def projected_kernel(z, info, base_ref, mine_ref, other_ref, up_ref, out_ref, spread):
    spread[...] = jnp.zeros_like(spread)
    for b in range(z.nb):
        cut = z.block(b)
        spread[z.ranks(b), cut] = (mine_ref[:, cut] + other_ref[:, cut]).astype(bf16)
    wide = _dot(spread[...], up_ref[...], TN)
    for b in range(z.nb):
        cut = z.block(b)
        full = base_ref[cut, :] + adapter_scale * wide[cut]
        out_ref[cut, :] = _masked(full, z.valid(info, b)).astype(bf16)


def through_kernel(z, first, info, g_ref, w_ref, out_ref, *sums):
    step = out_ref.shape[1] // 4
    for h in range(4):
        cut = slice(h * step, (h + 1) * step)
        rows = slice(first + h * step, first + (h + 1) * step)
        out_ref[:, cut] = _dot(g_ref[...], w_ref[rows, :], NT)
    for s in sums:
        one_hot_sums(z, info, s)


def tokens_kernel(z, first, info, through_ref, mine_ref, other_ref, d_ref, *refs):
    out_ref, spread = refs[-2:]
    step = pl.program_id(0)
    wide = out_ref.shape[1]

    @pl.when(step == 0)
    def _():
        spread[...] = jnp.zeros_like(spread)
        for b in range(z.nb):
            cut = z.block(b)
            v = (mine_ref[:, cut] + other_ref[:, cut]) * adapter_scale
            spread[z.ranks(b), cut] = v.astype(bf16)

    here = pl.ds(pl.multiple_of(step * wide, wide), wide)
    cut = pl.ds(pl.multiple_of((first + step) * wide, wide), wide)
    added = _dot(spread[...], d_ref[:, cut], TN)
    out_ref[...] = (through_ref[:, here] + added).astype(bf16)


def on_device(
    n_groups,
    n_dp,
    tokens,
    base_weight,
    adapter_down,
    adapter_up,
    out_cotangent,
    block_tenant,
    block_valid,
    tenant_slot,
):
    nb = block_tenant.shape[0]
    rows, width = tokens.shape
    cols = out_cotangent.shape[1]
    tenants = tenant_slot.shape[0]
    ten_dev, _, rank = adapter_down.shape
    z = Sizes(n_dp, nb, ten_dev, rank, cols, width)
    n_far = z.n_far
    me = lax.axis_index("dp")
    core = lax.axis_index("tensor")
    group = lax.axis_index("groups")
    shared = n_groups == 2 and n_dp == 8
    n_parts = 4 if shared else 1
    mine_q = group * 2 + me % 2 if shared else jnp.int32(0)
    quarter = width // n_parts

    cotangent_other = _swap(out_cotangent, "tensor")

    down_t = jnp.swapaxes(adapter_down, 1, 2)
    if shared:
        to_y = lax.dynamic_slice_in_dim(down_t, (mine_q ^ 1) * quarter, quarter, axis=2)
        from_y = _xor(to_y, n_dp, 1)
    far_up = [_xor(adapter_up, n_dp, NEAR * j) for j in range(1, n_far)]
    lane = jnp.arange(LANES, dtype=i32)

    def spread_out(x):
        hit = lane[:, None] == jnp.arange(x.shape[0], dtype=i32)[None, :]
        return jnp.sum(jnp.where(hit, x[None, :], 0), axis=1).astype(i32)

    own_tenants = spread_out(block_tenant)
    tag = jnp.broadcast_to(own_tenants[None, :], (16, LANES)).astype(bf16)
    tag = jnp.pad(tag, ((0, 0), (0, cols - LANES)))
    ups = [u.reshape(ten_dev * rank, cols) for u in [adapter_up] + far_up]
    packet = jnp.concatenate(ups + [tag], axis=0)
    packets = [packet] + [_xor(packet, n_dp, k) for k in range(1, NEAR)]

    if shared:
        own = lax.dynamic_slice_in_dim(down_t, mine_q * quarter, quarter, axis=2)
        shard = jnp.concatenate([own, from_y], axis=0)
        shard_far = _xor(shard, n_dp, 4)

    line = lax.broadcasted_iota(i32, (16, LANES), 0)
    place = jnp.where(lane == 0, me, jnp.where(lane == 1, core, mine_q))
    info = jnp.where(line == 8, place[None, :], spread_out(block_valid)[None, :])
    info = jnp.where(line == 6, spread_out(tenant_slot)[None, :], info)
    info = jnp.where(line == 0, own_tenants[None, :], info)

    base_other, g_full, x_in = _call(
        functools.partial(base_kernel, z), "base", (1,),
        [pl.BlockSpec(memory_space=pl.ANY)] * 3 + [VMEM],
        [_whole((rows, cols))] + [VMEM] * 2,
        [
            _shape((rows, cols), bf16), _shape((rows, 2 * cols), bf16), _shape(tokens.shape, bf16),
        ],
        [
            pltpu.VMEM((width, cols), bf16), pltpu.VMEM((rows, cols), bf16),
            pltpu.SemaphoreType.DMA((5,)), pltpu.SemaphoreType.DMA((5,)),
            pltpu.SemaphoreType.DMA,
        ],
        vmem=BIG_VMEM,
    )(
        _tie(info, shard if shared else packet),
        tokens, base_weight, out_cotangent, cotangent_other,
    )
    base_arrived = _swap(base_other, "tensor")
    packets = [_tie(p, base_other) for p in packets]

    for k in range(1, NEAR):
        info = jnp.where(line == k, packets[k][-16, :LANES].astype(i32)[None, :], info)

    if shared:
        shard_far = _tie(shard_far, base_other)
        info = _tie(info, shard_far)
        farther = _xor(jnp.concatenate([shard, shard_far], axis=0), n_dp, 2)

    part = (rank, rows)
    block_up, back_part = _call(
        functools.partial(back_kernel, z), "back", (1,),
        [VMEM] * (1 + NEAR), [VMEM, _whole(part)],
        [_shape((nb * rank, cols), bf16), _shape(part, f32)], [],
    )(info, g_full, *packets)
    back_other = _swap(back_part, "tensor")
    ready = [base_arrived]
    if shared:
        info_x = _swap(info, "groups")

    packed_rows = n_dp * CAP * rank
    near_rows = packed_rows // NEAR

    def pack(info, start, wide):
        return _call(
            functools.partial(pack_kernel, z, NEAR, start), "pack_down", (1,),
            [VMEM] * 3, [_whole((near_rows, wide))] * NEAR,
            [_shape((near_rows, wide), bf16)] * NEAR,
            [pltpu.VMEM((packed_rows, rows), bf16)],
        )(info, back_part, back_other, x_in)

    def to_near(sends):
        return [sends[0]] + [_xor(sends[k], n_dp, k) for k in range(1, NEAR)]

    def dense(info, got):
        wide = got[0].shape[1]
        out = (ten_dev * rank, wide)
        return _call(
            functools.partial(dense_kernel, z), "dense", (1,),
            [VMEM] * (1 + NEAR), [VMEM] + [_whole(out)] * (n_far - 1),
            [_shape(out, f32)] + [_shape(out, bf16)] * (n_far - 1), [],
        )(info, sums, *got)

    def to_far(parts):
        return [parts[0]] + [_xor(parts[j], n_dp, NEAR * j) for j in range(1, n_far)]

    def through(info, first, wide, with_sums):
        sums = _shape((n_far, ten_dev * rank, NEAR * CAP * rank), bf16)
        return _call(
            functools.partial(through_kernel, z, first), "through", (1,), [VMEM] * 2,
            [VMEM] * (1 + with_sums), [_shape((rows, wide), f32)] + [sums] * with_sums, [],
        )(info, g_full, base_weight)

    half = width // 2
    wide_a = width * 9 // 16
    sends_a = pack(_tie(info, *ready), 0, wide_a)
    got_a = to_near(sends_a)
    low, sums = through(_tie(info, sends_a[0]), 0, half, 1)

    if shared:
        block = (nb * rank, quarter)
        chosen = _call(
            functools.partial(choose_kernel, z), "choose", (1,),
            [VMEM] * 3, [_whole(block)] * 4, [_shape(block, bf16)] * 4, [],
            n_scalars=2,
        )(_tie(info, low), info_x, shard, shard_far, farther)
        sends_b = pack(_tie(info, chosen[0]), wide_a, width - wide_a)
        got_y = _xor(_tie(chosen[1], got_a[2], sends_b[0]), n_dp, 1)
        got_x = _swap(_tie(chosen[2], sends_b[0]), "groups")
        got_d = lax.ppermute(
            _tie(chosen[3], sends_b[0]),
            ("groups", "dp"),
            [(g * n_dp + d, (1 - g) * n_dp + (d ^ 1)) for g in range(2) for d in range(n_dp)],
        )
    else:
        every = lax.all_gather(down_t, "dp", axis=0, tiled=True)
        slots = jnp.take(tenant_slot, block_tenant, axis=0)
        got_down = [jnp.take(every, slots, axis=0).reshape(nb * rank, width)]
        sends_b = pack(_tie(info, low), wide_a, width - wide_a)

    base_own = _call(
        functools.partial(own_kernel, z), "base_own", (1,),
        [VMEM] * 3, VMEM, _shape((rows, cols), f32), [],
    )(_tie(info, sends_b[0]), x_in, base_weight, base_arrived)
    dense_a = dense(_tie(info, base_own), got_a)
    far_a = to_far(dense_a)

    (high,) = through(_tie(info, dense_a[1]), half, width - half, 0)
    gate = [high] + ([got_y] if shared else [])
    got_b = to_near(
        [_tie(b, *gate) if k in (1, 3) else _tie(b, dense_a[1]) for k, b in enumerate(sends_b)]
    )

    if shared:
        got_down = [chosen[0], got_y, got_x, got_d]
    block_down, shrink_part = _call(
        functools.partial(shrink_kernel, z, n_parts), "shrink", (1,),
        [VMEM] * (1 + n_parts), [VMEM, _whole(part)],
        [_shape((nb * rank, width), bf16), _shape(part, f32)], [],
    )(_tie(info, high), x_in, *got_down)
    shrink_other = _swap(shrink_part, "tensor")


    step = min(512, width // 8)

    def token_grads(info, product, first, so_far):
        steps = product.shape[1] // step
        return _call(
            functools.partial(tokens_kernel, z, first), "token_grads", (steps,),
            [VMEM] * 4 + [pl.BlockSpec(memory_space=pl.ANY)] * len(so_far),
            pl.BlockSpec((rows, step), lambda i, *_: (0, first + i)),
            _shape((rows, width), bf16), [pltpu.VMEM((nb * rank, rows), bf16)],
            {5: 0} if so_far else None,
        )(info, product, back_part, back_other, block_down, *so_far)

    grad_tokens = token_grads(_tie(info, shrink_part), low, 0, [])

    up_sends = _call(
        functools.partial(pack_up_kernel, z, NEAR), "pack_up", (1,),
        [VMEM] * 3, [_whole((near_rows, cols))] * NEAR,
        [_shape((near_rows, cols), bf16)] * NEAR,
        [pltpu.VMEM((packed_rows, rows), bf16)],
    )(_tie(info, grad_tokens, far_a[1]), shrink_part, shrink_other, g_full)
    got_u = to_near(up_sends)

    dense_b = dense(_tie(info, up_sends[0]), got_b)
    far_b = to_far(dense_b)

    grad_tokens = token_grads(_tie(info, dense_b[1]), high, half // step, [grad_tokens])
    dense_u = dense(_tie(info, grad_tokens), got_u)
    far_u = to_far(dense_u)

    projected = _call(
        functools.partial(projected_kernel, z), "projected", (1,),
        [VMEM] * 4, _whole((rows, cols)), _shape((rows, cols), bf16),
        [pltpu.VMEM((nb * rank, rows), bf16)],
    )(
        _tie(info, dense_u[1]),
        base_own, shrink_part, shrink_other, block_up,
    )

    outs = [(ten_dev * rank, width), (ten_dev * rank, cols)]
    grad_down, grad_up = _call(
        functools.partial(final_kernel, (2, 1), n_far), "final", (1,),
        [VMEM] * (3 * n_far), [_whole(o) for o in outs], [_shape(o, f32) for o in outs], [],
    )(info, *far_a, *far_b, *far_u)
    grad_down = jnp.swapaxes(grad_down.reshape(ten_dev, rank, width), 1, 2)
    return projected, grad_tokens, grad_down, grad_up.reshape(ten_dev, rank, cols)


def solution(mesh):
    n_groups, n_dp = mesh.shape["groups"], mesh.shape["dp"]
    in_specs = (
        P(("groups", "dp"), "tensor"),
        P("tensor", None),
        P("dp", "tensor", None),
        P("dp", None, "tensor"),
        P(("groups", "dp"), "tensor"),
        P(("groups", "dp")),
        P(("groups", "dp")),
        P("groups"),
    )
    out_specs = (
        P(("groups", "dp"), "tensor"),
        P(("groups", "dp"), "tensor"),
        P(("groups", "dp"), "tensor", None),
        P(("groups", "dp"), None, "tensor"),
    )

    def run(*args):
        return on_device(n_groups, n_dp, *args)

    return jax.shard_map(
        run, mesh=mesh, in_specs=in_specs, out_specs=out_specs, check_vma=False
    )
```

```python
import functools

import jax
import jax.numpy as jnp
from jax import lax
from jax.experimental import pallas as pl
from jax.experimental.pallas import tpu as pltpu
from jax.sharding import PartitionSpec as P

TENANT_BLOCK = 128
CAP = 2
NEAR = 4
VMEM_LIMIT = 9 * 1024 * 1024
BIG_VMEM = 36 * 1024 * 1024
LANES = 128

adapter_scale = 2.0
f32 = jnp.float32
bf16 = jnp.bfloat16
i32 = jnp.int32

NT = (((1,), (1,)), ((), ()))
TN = (((0,), (0,)), ((), ()))
NN = (((1,), (0,)), ((), ()))


def _dot(a, b, dims):
    return lax.dot_general(a, b, dims, preferred_element_type=f32)


def _swap(x, axis):
    return lax.ppermute(x, axis, [(0, 1), (1, 0)])


def _xor(x, n, k):
    return lax.ppermute(x, "dp", [(i, i ^ k) for i in range(n)])


def _tie(x, *after):
    return lax.optimization_barrier((x,) + after)[0]


def _div(a, n):
    return a >> (n.bit_length() - 1) if n & (n - 1) == 0 else lax.div(a, jnp.int32(n))


def _rem(a, n):
    return a & (n - 1) if n & (n - 1) == 0 else lax.rem(a, jnp.int32(n))


VMEM = pl.BlockSpec(memory_space=pltpu.VMEM)


def _shape(shape, dtype):
    return jax.ShapeDtypeStruct(shape, dtype)


def _call(
    body, name, grid, in_specs, out_specs, out_shape, scratch, aliases=None, vmem=VMEM_LIMIT,
    n_scalars=1,
):
    return pl.pallas_call(
        body,
        name=name,
        grid_spec=pltpu.PrefetchScalarGridSpec(
            num_scalar_prefetch=n_scalars,
            grid=grid,
            in_specs=in_specs,
            out_specs=out_specs,
            scratch_shapes=scratch,
        ),
        out_shape=out_shape,
        input_output_aliases=aliases or {},
        compiler_params=pltpu.CompilerParams(vmem_limit_bytes=vmem),
        cost_estimate=pl.CostEstimate(flops=1, bytes_accessed=1, transcendentals=0),
    )


def _whole(shape):
    return pl.BlockSpec(shape, lambda *_: (0,) * len(shape))


class Sizes:
    def __init__(self, n_dp, nb, ten_dev, rank, cols, width):
        self.n_dp, self.nb, self.ten_dev = n_dp, nb, ten_dev
        self.rank, self.cols, self.width = rank, cols, width
        self.n_far = n_dp // NEAR
        self.rows = nb * TENANT_BLOCK
        self.me, self.core, self.quarter = (8, 0), (8, 1), (8, 2)

    def block(self, b):
        return slice(b * TENANT_BLOCK, (b + 1) * TENANT_BLOCK)

    def ranks(self, b):
        return slice(b * self.rank, (b + 1) * self.rank)

    def slot(self, info, which, b):
        return info[6, info[which, b]]

    def valid(self, info, b):
        return info[9, b]

    def owner_and_order(self, info, which):
        owners = [_div(self.slot(info, which, b), self.ten_dev) for b in range(self.nb)]
        orders = []
        for b in range(self.nb):
            n = jnp.int32(0)
            for c in range(b):
                n = n + jnp.where(owners[c] == owners[b], 1, 0)
            orders.append(n)
        return owners, orders

    def places(self, info):
        owners, orders = self.owner_and_order(info, 0)
        out = []
        for o, r in zip(owners, orders):
            rel = o ^ info[self.me]
            place = (_rem(rel, NEAR) * self.n_far + _div(rel, NEAR)) * CAP + r
            out.append(pl.ds(pl.multiple_of(place * self.rank, self.rank), self.rank))
        return out


def _masked(x, valid):
    row = lax.broadcasted_iota(i32, x.shape, 0)
    return jnp.where(row < valid, x, jnp.zeros((), x.dtype))


def base_kernel(
    z, info, x_hbm, w_hbm, g_hbm, h_ref, far_ref, full_ref, x_ref, w_ref, g_ref, x_sem, w_sem, g_sem
):
    own = pl.ds(pl.multiple_of(info[z.core] * z.cols, z.cols), z.cols)
    far = pl.ds(pl.multiple_of((1 - info[z.core]) * z.cols, z.cols), z.cols)
    unit = z.width // 8
    g = pltpu.make_async_copy(g_hbm, g_ref, g_sem)
    g.start()
    copies = []
    for i, (first, last) in enumerate(((0, 1), (1, 3), (3, 5), (5, 7), (7, 8))):
        cut = pl.ds(first * unit, (last - first) * unit)
        x = pltpu.make_async_copy(x_hbm.at[:, cut], x_ref.at[:, cut], x_sem.at[i])
        w = pltpu.make_async_copy(w_hbm.at[cut, far], w_ref.at[cut], w_sem.at[i])
        x.start()
        w.start()
        copies.append((x, w, cut))
    g.wait()
    for b in range(z.nb):
        cut = z.block(b)
        full_ref[cut, own] = _masked(g_ref[cut, :], z.valid(info, b))
        full_ref[cut, far] = _masked(h_ref[cut, :], z.valid(info, b))
    total = None
    for x, w, cut in copies:
        x.wait()
        w.wait()
        term = _dot(x_ref[:, cut], w_ref[cut, :], NN)
        total = term if total is None else total + term
    far_ref[...] = total.astype(bf16)


def own_kernel(z, info, x_ref, w_ref, far_ref, out_ref):
    own = pl.ds(pl.multiple_of(info[z.core] * z.cols, z.cols), z.cols)
    out_ref[...] = _dot(x_ref[...], w_ref[:, own], NN) + far_ref[...].astype(f32)


def back_kernel(z, info, g_ref, *refs):
    packets, (up_ref, part_ref) = refs[:NEAR], refs[NEAR:]
    own = pl.ds(pl.multiple_of(info[z.core] * z.cols, z.cols), z.cols)
    for b in range(z.nb):
        s = z.slot(info, 0, b)
        rel = _div(s, z.ten_dev) ^ info[z.me]
        at = _div(rel, NEAR) * z.ten_dev + _rem(s, z.ten_dev)
        at = pl.ds(pl.multiple_of(at * z.rank, z.rank), z.rank)
        near = _rem(rel, NEAR)
        u = packets[0][at, :]
        for k in range(1, NEAR):
            u = jnp.where(near == k, packets[k][at, :], u)
        up_ref[z.ranks(b), :] = u
        part_ref[:, z.block(b)] = _dot(u, g_ref[z.block(b), own], NT)


def pack_kernel(z, n_out, start, info, mine_ref, other_ref, x_ref, *refs):
    outs, packed = refs[:n_out], refs[n_out]
    packed[...] = jnp.zeros_like(packed)
    for b, place in enumerate(z.places(info)):
        cut = z.block(b)
        v = (mine_ref[:, cut] + other_ref[:, cut]) * adapter_scale
        packed[place, cut] = v.astype(bf16)
    wide = outs[0].shape[1]
    res = _dot(packed[...], x_ref[:, start : start + wide], NN).astype(bf16)
    each = res.shape[0] // n_out
    for k in range(n_out):
        outs[k][...] = res[k * each : (k + 1) * each]


def pack_up_kernel(z, n_out, info, mine_ref, other_ref, g_ref, *refs):
    outs, packed = refs[:n_out], refs[n_out]
    own = pl.ds(pl.multiple_of(info[z.core] * z.cols, z.cols), z.cols)
    packed[...] = jnp.zeros_like(packed)
    for b, place in enumerate(z.places(info)):
        cut = z.block(b)
        packed[place, cut] = (mine_ref[:, cut] + other_ref[:, cut]).astype(bf16)
    res = (adapter_scale * _dot(packed[...], g_ref[:, own], NN)).astype(bf16)
    each = res.shape[0] // n_out
    for k in range(n_out):
        outs[k][...] = res[k * each : (k + 1) * each]


def one_hot_sums(z, info, sums_ref):
    n = CAP * z.rank
    shape = (z.ten_dev * z.rank, n)
    row = lax.broadcasted_iota(i32, shape, 0)
    col = lax.broadcasted_iota(i32, shape, 1)
    same = _rem(row, z.rank) == _rem(col, z.rank)
    row_slot = _div(row, z.rank)
    tables = [z.owner_and_order(info, k) for k in range(NEAR)]
    for j in range(z.n_far):
        holder = info[z.me] ^ (NEAR * j)
        parts = []
        for k in range(NEAR):
            owners, orders = tables[k]
            local = []
            for r in range(CAP):
                found = jnp.int32(0)
                for b in range(z.nb):
                    hit = (owners[b] == holder) & (orders[b] == r)
                    found = jnp.where(hit, _rem(z.slot(info, k, b), z.ten_dev), found)
                local.append(found)
            wanted = jnp.where(col < z.rank, local[0], local[1])
            parts.append(jnp.where(same & (row_slot == wanted), 1.0, 0.0))
        sums_ref[j] = jnp.concatenate(parts, axis=1).astype(bf16)


def dense_kernel(z, info, sums_ref, *refs):
    got, near_ref, far_refs = refs[:NEAR], refs[NEAR], refs[NEAR + 1 :]
    n = CAP * z.rank
    for j in range(z.n_far):
        stacked = jnp.concatenate([g[j * n : (j + 1) * n, :] for g in got], axis=0)
        total = _dot(sums_ref[j], stacked, NN)
        if j == 0:
            near_ref[...] = total
        else:
            far_refs[j - 1][...] = total.astype(bf16)


def final_kernel(parts, n_far, info, *refs):
    outs = refs[len(refs) - len(parts) :]
    i = 0
    for n, out in zip(parts, outs):
        at = 0
        for _ in range(n):
            total = refs[i][...]
            for r in refs[i + 1 : i + n_far]:
                total = total + r[...].astype(f32)
            out[:, at : at + total.shape[1]] = total
            at += total.shape[1]
            i += n_far


def choose_kernel(z, info, info_x, own_ref, far_ref, pair_ref, *outs):
    half = own_ref.shape[0]
    sources = (own_ref, pair_ref.at[:half], far_ref, pair_ref.at[half:])
    wanted = ((info, 0), (info, 1), (info_x, 0), (info_x, 1))
    for (table, which), out in zip(wanted, outs):
        for b in range(z.nb):
            s = z.slot(table, which, b)
            rel = _div(s, z.ten_dev) ^ info[z.me]
            at = _rem(rel, 2) * z.ten_dev + _rem(s, z.ten_dev)
            line = _div(rel, 2)
            v = sources[0][at]
            for k in range(1, 4):
                v = jnp.where(line == k, sources[k][at], v)
            out[z.ranks(b), :] = v


def shrink_kernel(z, n_parts, info, x_ref, *refs):
    parts, (full_ref, out_ref) = refs[:n_parts], refs[n_parts:]
    wide = z.width // n_parts
    total = None
    for j in range(n_parts):
        if n_parts == 1:
            cut = slice(0, wide)
        else:
            cut = pl.ds(pl.multiple_of((info[z.quarter] ^ j) * wide, wide), wide)
        full_ref[:, cut] = parts[j][...]
        term = _dot(x_ref[:, cut], parts[j][...], NT)
        total = term if total is None else total + term
    for b in range(z.nb):
        out_ref[:, z.block(b)] = total[z.block(b), :].T[z.ranks(b), :]


def projected_kernel(z, info, base_ref, mine_ref, other_ref, up_ref, out_ref, spread):
    spread[...] = jnp.zeros_like(spread)
    for b in range(z.nb):
        cut = z.block(b)
        spread[z.ranks(b), cut] = (mine_ref[:, cut] + other_ref[:, cut]).astype(bf16)
    wide = _dot(spread[...], up_ref[...], TN)
    for b in range(z.nb):
        cut = z.block(b)
        full = base_ref[cut, :] + adapter_scale * wide[cut]
        out_ref[cut, :] = _masked(full, z.valid(info, b)).astype(bf16)


def through_kernel(z, first, info, g_ref, w_ref, out_ref, *sums):
    step = out_ref.shape[1] // 4
    for h in range(4):
        cut = slice(h * step, (h + 1) * step)
        rows = slice(first + h * step, first + (h + 1) * step)
        out_ref[:, cut] = _dot(g_ref[...], w_ref[rows, :], NT)
    for s in sums:
        one_hot_sums(z, info, s)


def tokens_kernel(z, first, info, through_ref, mine_ref, other_ref, d_ref, *refs):
    out_ref, spread = refs[-2:]
    step = pl.program_id(0)
    wide = out_ref.shape[1]

    @pl.when(step == 0)
    def _():
        spread[...] = jnp.zeros_like(spread)
        for b in range(z.nb):
            cut = z.block(b)
            v = (mine_ref[:, cut] + other_ref[:, cut]) * adapter_scale
            spread[z.ranks(b), cut] = v.astype(bf16)

    here = pl.ds(pl.multiple_of(step * wide, wide), wide)
    cut = pl.ds(pl.multiple_of((first + step) * wide, wide), wide)
    added = _dot(spread[...], d_ref[:, cut], TN)
    out_ref[...] = (through_ref[:, here] + added).astype(bf16)


def on_device(
    n_groups,
    n_dp,
    tokens,
    base_weight,
    adapter_down,
    adapter_up,
    out_cotangent,
    block_tenant,
    block_valid,
    tenant_slot,
):
    nb = block_tenant.shape[0]
    rows, width = tokens.shape
    cols = out_cotangent.shape[1]
    tenants = tenant_slot.shape[0]
    ten_dev, _, rank = adapter_down.shape
    z = Sizes(n_dp, nb, ten_dev, rank, cols, width)
    n_far = z.n_far
    me = lax.axis_index("dp")
    core = lax.axis_index("tensor")
    group = lax.axis_index("groups")
    shared = n_groups == 2 and n_dp == 8
    n_parts = 4 if shared else 1
    mine_q = group * 2 + me % 2 if shared else jnp.int32(0)
    quarter = width // n_parts

    cotangent_other = _swap(out_cotangent, "tensor")

    down_t = jnp.swapaxes(adapter_down, 1, 2)
    if shared:
        to_y = lax.dynamic_slice_in_dim(down_t, (mine_q ^ 1) * quarter, quarter, axis=2)
        from_y = _xor(to_y, n_dp, 1)
    far_up = [_xor(adapter_up, n_dp, NEAR * j) for j in range(1, n_far)]
    lane = jnp.arange(LANES, dtype=i32)

    def spread_out(x):
        hit = lane[:, None] == jnp.arange(x.shape[0], dtype=i32)[None, :]
        return jnp.sum(jnp.where(hit, x[None, :], 0), axis=1).astype(i32)

    own_tenants = spread_out(block_tenant)
    tag = jnp.broadcast_to(own_tenants[None, :], (16, LANES)).astype(bf16)
    tag = jnp.pad(tag, ((0, 0), (0, cols - LANES)))
    ups = [u.reshape(ten_dev * rank, cols) for u in [adapter_up] + far_up]
    packet = jnp.concatenate(ups + [tag], axis=0)
    packets = [packet] + [_xor(packet, n_dp, k) for k in range(1, NEAR)]

    if shared:
        own = lax.dynamic_slice_in_dim(down_t, mine_q * quarter, quarter, axis=2)
        shard = jnp.concatenate([own, from_y], axis=0)
        shard_far = _xor(shard, n_dp, 4)

    line = lax.broadcasted_iota(i32, (16, LANES), 0)
    place = jnp.where(lane == 0, me, jnp.where(lane == 1, core, mine_q))
    info = jnp.where(line == 8, place[None, :], spread_out(block_valid)[None, :])
    info = jnp.where(line == 6, spread_out(tenant_slot)[None, :], info)
    info = jnp.where(line == 0, own_tenants[None, :], info)

    base_other, g_full, x_in = _call(
        functools.partial(base_kernel, z), "base", (1,),
        [pl.BlockSpec(memory_space=pl.ANY)] * 3 + [VMEM],
        [_whole((rows, cols))] + [VMEM] * 2,
        [
            _shape((rows, cols), bf16), _shape((rows, 2 * cols), bf16), _shape(tokens.shape, bf16),
        ],
        [
            pltpu.VMEM((width, cols), bf16), pltpu.VMEM((rows, cols), bf16),
            pltpu.SemaphoreType.DMA((5,)), pltpu.SemaphoreType.DMA((5,)),
            pltpu.SemaphoreType.DMA,
        ],
        vmem=BIG_VMEM,
    )(
        _tie(info, shard if shared else packet),
        tokens, base_weight, out_cotangent, cotangent_other,
    )
    base_arrived = _swap(base_other, "tensor")
    packets = [_tie(p, base_other) for p in packets]

    for k in range(1, NEAR):
        info = jnp.where(line == k, packets[k][-16, :LANES].astype(i32)[None, :], info)

    if shared:
        shard_far = _tie(shard_far, base_other)
        info = _tie(info, shard_far)
        farther = _xor(jnp.concatenate([shard, shard_far], axis=0), n_dp, 2)

    part = (rank, rows)
    block_up, back_part = _call(
        functools.partial(back_kernel, z), "back", (1,),
        [VMEM] * (1 + NEAR), [VMEM, _whole(part)],
        [_shape((nb * rank, cols), bf16), _shape(part, f32)], [],
    )(info, g_full, *packets)
    back_other = _swap(back_part, "tensor")
    ready = [base_arrived]
    if shared:
        info_x = _swap(info, "groups")

    packed_rows = n_dp * CAP * rank
    near_rows = packed_rows // NEAR

    def pack(info, start, wide):
        return _call(
            functools.partial(pack_kernel, z, NEAR, start), "pack_down", (1,),
            [VMEM] * 3, [_whole((near_rows, wide))] * NEAR,
            [_shape((near_rows, wide), bf16)] * NEAR,
            [pltpu.VMEM((packed_rows, rows), bf16)],
        )(info, back_part, back_other, x_in)

    def to_near(sends):
        return [sends[0]] + [_xor(sends[k], n_dp, k) for k in range(1, NEAR)]

    def dense(info, got):
        wide = got[0].shape[1]
        out = (ten_dev * rank, wide)
        return _call(
            functools.partial(dense_kernel, z), "dense", (1,),
            [VMEM] * (1 + NEAR), [VMEM] + [_whole(out)] * (n_far - 1),
            [_shape(out, f32)] + [_shape(out, bf16)] * (n_far - 1), [],
        )(info, sums, *got)

    def to_far(parts):
        return [parts[0]] + [_xor(parts[j], n_dp, NEAR * j) for j in range(1, n_far)]

    def through(info, first, wide, with_sums):
        sums = _shape((n_far, ten_dev * rank, NEAR * CAP * rank), bf16)
        return _call(
            functools.partial(through_kernel, z, first), "through", (1,), [VMEM] * 2,
            [VMEM] * (1 + with_sums), [_shape((rows, wide), f32)] + [sums] * with_sums, [],
        )(info, g_full, base_weight)

    half = width // 2
    wide_a = width * 9 // 16
    sends_a = pack(_tie(info, *ready), 0, wide_a)
    got_a = to_near(sends_a)
    wide_low = width * 5 // 8
    low, sums = through(_tie(info, sends_a[0]), 0, wide_low, 1)

    if shared:
        block = (nb * rank, quarter)
        chosen = _call(
            functools.partial(choose_kernel, z), "choose", (1,),
            [VMEM] * 3, [_whole(block)] * 4, [_shape(block, bf16)] * 4, [],
            n_scalars=2,
        )(_tie(info, low), info_x, shard, shard_far, farther)
        sends_b = pack(_tie(info, chosen[0]), wide_a, width - wide_a)
        got_y = _xor(_tie(chosen[1], got_a[2], sends_b[0]), n_dp, 1)
        got_x = _swap(_tie(chosen[2], sends_b[0]), "groups")
        got_d = lax.ppermute(
            _tie(chosen[3], sends_b[0]),
            ("groups", "dp"),
            [(g * n_dp + d, (1 - g) * n_dp + (d ^ 1)) for g in range(2) for d in range(n_dp)],
        )
    else:
        every = lax.all_gather(down_t, "dp", axis=0, tiled=True)
        slots = jnp.take(tenant_slot, block_tenant, axis=0)
        got_down = [jnp.take(every, slots, axis=0).reshape(nb * rank, width)]
        sends_b = pack(_tie(info, low), wide_a, width - wide_a)

    base_own = _call(
        functools.partial(own_kernel, z), "base_own", (1,),
        [VMEM] * 3, VMEM, _shape((rows, cols), f32), [],
    )(_tie(info, sends_b[0]), x_in, base_weight, base_arrived)
    dense_a = dense(_tie(info, base_own), got_a)
    far_a = to_far(dense_a)

    (high,) = through(_tie(info, dense_a[1]), wide_low, width - wide_low, 0)
    gate = [high] + ([got_y] if shared else [])
    got_b = to_near(
        [_tie(b, *gate) if k in (1, 3) else _tie(b, dense_a[1]) for k, b in enumerate(sends_b)]
    )

    if shared:
        got_down = [chosen[0], got_y, got_x, got_d]
    block_down, shrink_part = _call(
        functools.partial(shrink_kernel, z, n_parts), "shrink", (1,),
        [VMEM] * (1 + n_parts), [VMEM, _whole(part)],
        [_shape((nb * rank, width), bf16), _shape(part, f32)], [],
    )(_tie(info, high), x_in, *got_down)
    shrink_other = _swap(shrink_part, "tensor")


    step = min(512, width // 8)

    def token_grads(info, product, first, so_far):
        steps = product.shape[1] // step
        return _call(
            functools.partial(tokens_kernel, z, first), "token_grads", (steps,),
            [VMEM] * 4 + [pl.BlockSpec(memory_space=pl.ANY)] * len(so_far),
            pl.BlockSpec((rows, step), lambda i, *_: (0, first + i)),
            _shape((rows, width), bf16), [pltpu.VMEM((nb * rank, rows), bf16)],
            {5: 0} if so_far else None,
        )(info, product, back_part, back_other, block_down, *so_far)

    grad_tokens = token_grads(_tie(info, shrink_part), low, 0, [])

    up_sends = _call(
        functools.partial(pack_up_kernel, z, NEAR), "pack_up", (1,),
        [VMEM] * 3, [_whole((near_rows, cols))] * NEAR,
        [_shape((near_rows, cols), bf16)] * NEAR,
        [pltpu.VMEM((packed_rows, rows), bf16)],
    )(_tie(info, grad_tokens, far_a[1]), shrink_part, shrink_other, g_full)
    got_u = to_near(up_sends)

    dense_b = dense(_tie(info, up_sends[0]), got_b)
    far_b = to_far(dense_b)

    grad_tokens = token_grads(_tie(info, dense_b[1]), high, wide_low // step, [grad_tokens])
    dense_u = dense(_tie(info, grad_tokens), got_u)
    far_u = to_far(dense_u)

    projected = _call(
        functools.partial(projected_kernel, z), "projected", (1,),
        [VMEM] * 4, _whole((rows, cols)), _shape((rows, cols), bf16),
        [pltpu.VMEM((nb * rank, rows), bf16)],
    )(
        _tie(info, dense_u[1]),
        base_own, shrink_part, shrink_other, block_up,
    )

    outs = [(ten_dev * rank, width), (ten_dev * rank, cols)]
    grad_down, grad_up = _call(
        functools.partial(final_kernel, (2, 1), n_far), "final", (1,),
        [VMEM] * (3 * n_far), [_whole(o) for o in outs], [_shape(o, f32) for o in outs], [],
    )(info, *far_a, *far_b, *far_u)
    grad_down = jnp.swapaxes(grad_down.reshape(ten_dev, rank, width), 1, 2)
    return projected, grad_tokens, grad_down, grad_up.reshape(ten_dev, rank, cols)


def solution(mesh):
    n_groups, n_dp = mesh.shape["groups"], mesh.shape["dp"]
    in_specs = (
        P(("groups", "dp"), "tensor"),
        P("tensor", None),
        P("dp", "tensor", None),
        P("dp", None, "tensor"),
        P(("groups", "dp"), "tensor"),
        P(("groups", "dp")),
        P(("groups", "dp")),
        P("groups"),
    )
    out_specs = (
        P(("groups", "dp"), "tensor"),
        P(("groups", "dp"), "tensor"),
        P(("groups", "dp"), "tensor", None),
        P(("groups", "dp"), None, "tensor"),
    )

    def run(*args):
        return on_device(n_groups, n_dp, *args)

    return jax.shard_map(
        run, mesh=mesh, in_specs=in_specs, out_specs=out_specs, check_vma=False
    )
```

```python
import functools

import jax
import jax.numpy as jnp
from jax import lax
from jax.experimental import pallas as pl
from jax.experimental.pallas import tpu as pltpu
from jax.sharding import PartitionSpec as P

TENANT_BLOCK = 128
CAP = 2
NEAR = 4
VMEM_LIMIT = 9 * 1024 * 1024
BIG_VMEM = 36 * 1024 * 1024
LANES = 128

adapter_scale = 2.0
f32 = jnp.float32
bf16 = jnp.bfloat16
i32 = jnp.int32

NT = (((1,), (1,)), ((), ()))
TN = (((0,), (0,)), ((), ()))
NN = (((1,), (0,)), ((), ()))


def _dot(a, b, dims):
    return lax.dot_general(a, b, dims, preferred_element_type=f32)


def _swap(x, axis):
    return lax.ppermute(x, axis, [(0, 1), (1, 0)])


def _xor(x, n, k):
    return lax.ppermute(x, "dp", [(i, i ^ k) for i in range(n)])


def _tie(x, *after):
    return lax.optimization_barrier((x,) + after)[0]


def _div(a, n):
    return a >> (n.bit_length() - 1) if n & (n - 1) == 0 else lax.div(a, jnp.int32(n))


def _rem(a, n):
    return a & (n - 1) if n & (n - 1) == 0 else lax.rem(a, jnp.int32(n))


VMEM = pl.BlockSpec(memory_space=pltpu.VMEM)


def _shape(shape, dtype):
    return jax.ShapeDtypeStruct(shape, dtype)


def _call(
    body, name, grid, in_specs, out_specs, out_shape, scratch, aliases=None, vmem=VMEM_LIMIT,
    n_scalars=1,
):
    return pl.pallas_call(
        body,
        name=name,
        grid_spec=pltpu.PrefetchScalarGridSpec(
            num_scalar_prefetch=n_scalars,
            grid=grid,
            in_specs=in_specs,
            out_specs=out_specs,
            scratch_shapes=scratch,
        ),
        out_shape=out_shape,
        input_output_aliases=aliases or {},
        compiler_params=pltpu.CompilerParams(vmem_limit_bytes=vmem),
        cost_estimate=pl.CostEstimate(flops=1, bytes_accessed=1, transcendentals=0),
    )


def _whole(shape):
    return pl.BlockSpec(shape, lambda *_: (0,) * len(shape))


class Sizes:
    def __init__(self, n_dp, nb, ten_dev, rank, cols, width):
        self.n_dp, self.nb, self.ten_dev = n_dp, nb, ten_dev
        self.rank, self.cols, self.width = rank, cols, width
        self.n_far = n_dp // NEAR
        self.rows = nb * TENANT_BLOCK
        self.me, self.core, self.quarter = (8, 0), (8, 1), (8, 2)

    def block(self, b):
        return slice(b * TENANT_BLOCK, (b + 1) * TENANT_BLOCK)

    def ranks(self, b):
        return slice(b * self.rank, (b + 1) * self.rank)

    def slot(self, info, which, b):
        return info[6, info[which, b]]

    def valid(self, info, b):
        return info[9, b]

    def owner_and_order(self, info, which):
        owners = [_div(self.slot(info, which, b), self.ten_dev) for b in range(self.nb)]
        orders = []
        for b in range(self.nb):
            n = jnp.int32(0)
            for c in range(b):
                n = n + jnp.where(owners[c] == owners[b], 1, 0)
            orders.append(n)
        return owners, orders

    def places(self, info):
        owners, orders = self.owner_and_order(info, 0)
        out = []
        for o, r in zip(owners, orders):
            rel = o ^ info[self.me]
            place = (_rem(rel, NEAR) * self.n_far + _div(rel, NEAR)) * CAP + r
            out.append(pl.ds(pl.multiple_of(place * self.rank, self.rank), self.rank))
        return out


def _masked(x, valid):
    row = lax.broadcasted_iota(i32, x.shape, 0)
    return jnp.where(row < valid, x, jnp.zeros((), x.dtype))


def base_kernel(
    z, info, x_hbm, w_hbm, g_hbm, h_ref, far_ref, full_ref, x_ref, w_ref, g_ref, x_sem, w_sem, g_sem
):
    own = pl.ds(pl.multiple_of(info[z.core] * z.cols, z.cols), z.cols)
    far = pl.ds(pl.multiple_of((1 - info[z.core]) * z.cols, z.cols), z.cols)
    unit = z.width // 8
    g = pltpu.make_async_copy(g_hbm, g_ref, g_sem)
    g.start()
    copies = []
    for i, (first, last) in enumerate(((0, 1), (1, 3), (3, 5), (5, 7), (7, 8))):
        cut = pl.ds(first * unit, (last - first) * unit)
        x = pltpu.make_async_copy(x_hbm.at[:, cut], x_ref.at[:, cut], x_sem.at[i])
        w = pltpu.make_async_copy(w_hbm.at[cut, far], w_ref.at[cut], w_sem.at[i])
        x.start()
        w.start()
        copies.append((x, w, cut))
    g.wait()
    for b in range(z.nb):
        cut = z.block(b)
        full_ref[cut, own] = _masked(g_ref[cut, :], z.valid(info, b))
        full_ref[cut, far] = _masked(h_ref[cut, :], z.valid(info, b))
    total = None
    for x, w, cut in copies:
        x.wait()
        w.wait()
        term = _dot(x_ref[:, cut], w_ref[cut, :], NN)
        total = term if total is None else total + term
    far_ref[...] = total.astype(bf16)


def own_kernel(z, info, x_ref, w_ref, far_ref, out_ref):
    own = pl.ds(pl.multiple_of(info[z.core] * z.cols, z.cols), z.cols)
    out_ref[...] = _dot(x_ref[...], w_ref[:, own], NN) + far_ref[...].astype(f32)


def back_kernel(z, info, g_ref, *refs):
    packets, (up_ref, part_ref) = refs[:NEAR], refs[NEAR:]
    own = pl.ds(pl.multiple_of(info[z.core] * z.cols, z.cols), z.cols)
    for b in range(z.nb):
        s = z.slot(info, 0, b)
        rel = _div(s, z.ten_dev) ^ info[z.me]
        at = _div(rel, NEAR) * z.ten_dev + _rem(s, z.ten_dev)
        at = pl.ds(pl.multiple_of(at * z.rank, z.rank), z.rank)
        near = _rem(rel, NEAR)
        u = packets[0][at, :]
        for k in range(1, NEAR):
            u = jnp.where(near == k, packets[k][at, :], u)
        up_ref[z.ranks(b), :] = u
        part_ref[:, z.block(b)] = _dot(u, g_ref[z.block(b), own], NT)


def pack_kernel(z, n_out, start, info, mine_ref, other_ref, x_ref, *refs):
    outs, packed = refs[:n_out], refs[n_out]
    packed[...] = jnp.zeros_like(packed)
    for b, place in enumerate(z.places(info)):
        cut = z.block(b)
        v = (mine_ref[:, cut] + other_ref[:, cut]) * adapter_scale
        packed[place, cut] = v.astype(bf16)
    wide = outs[0].shape[1]
    res = _dot(packed[...], x_ref[:, start : start + wide], NN).astype(bf16)
    each = res.shape[0] // n_out
    for k in range(n_out):
        outs[k][...] = res[k * each : (k + 1) * each]


def pack_up_kernel(z, n_out, info, mine_ref, other_ref, g_ref, *refs):
    outs, packed = refs[:n_out], refs[n_out]
    own = pl.ds(pl.multiple_of(info[z.core] * z.cols, z.cols), z.cols)
    packed[...] = jnp.zeros_like(packed)
    for b, place in enumerate(z.places(info)):
        cut = z.block(b)
        packed[place, cut] = (mine_ref[:, cut] + other_ref[:, cut]).astype(bf16)
    res = (adapter_scale * _dot(packed[...], g_ref[:, own], NN)).astype(bf16)
    each = res.shape[0] // n_out
    for k in range(n_out):
        outs[k][...] = res[k * each : (k + 1) * each]


def one_hot_sums(z, info, sums_ref):
    n = CAP * z.rank
    shape = (z.ten_dev * z.rank, n)
    row = lax.broadcasted_iota(i32, shape, 0)
    col = lax.broadcasted_iota(i32, shape, 1)
    same = _rem(row, z.rank) == _rem(col, z.rank)
    row_slot = _div(row, z.rank)
    tables = [z.owner_and_order(info, k) for k in range(NEAR)]
    for j in range(z.n_far):
        holder = info[z.me] ^ (NEAR * j)
        parts = []
        for k in range(NEAR):
            owners, orders = tables[k]
            local = []
            for r in range(CAP):
                found = jnp.int32(0)
                for b in range(z.nb):
                    hit = (owners[b] == holder) & (orders[b] == r)
                    found = jnp.where(hit, _rem(z.slot(info, k, b), z.ten_dev), found)
                local.append(found)
            wanted = jnp.where(col < z.rank, local[0], local[1])
            parts.append(jnp.where(same & (row_slot == wanted), 1.0, 0.0))
        sums_ref[j] = jnp.concatenate(parts, axis=1).astype(bf16)


def dense_kernel(z, info, sums_ref, *refs):
    got, near_ref, far_refs = refs[:NEAR], refs[NEAR], refs[NEAR + 1 :]
    n = CAP * z.rank
    for j in range(z.n_far):
        stacked = jnp.concatenate([g[j * n : (j + 1) * n, :] for g in got], axis=0)
        total = _dot(sums_ref[j], stacked, NN)
        if j == 0:
            near_ref[...] = total
        else:
            far_refs[j - 1][...] = total.astype(bf16)


def final_kernel(parts, n_far, info, *refs):
    outs = refs[len(refs) - len(parts) :]
    i = 0
    for n, out in zip(parts, outs):
        at = 0
        for _ in range(n):
            total = refs[i][...]
            for r in refs[i + 1 : i + n_far]:
                total = total + r[...].astype(f32)
            out[:, at : at + total.shape[1]] = total
            at += total.shape[1]
            i += n_far


def choose_kernel(z, info, info_x, own_ref, far_ref, pair_ref, *outs):
    half = own_ref.shape[0]
    sources = (own_ref, pair_ref.at[:half], far_ref, pair_ref.at[half:])
    wanted = ((info, 0), (info, 1), (info_x, 0), (info_x, 1))
    for (table, which), out in zip(wanted, outs):
        for b in range(z.nb):
            s = z.slot(table, which, b)
            rel = _div(s, z.ten_dev) ^ info[z.me]
            at = _rem(rel, 2) * z.ten_dev + _rem(s, z.ten_dev)
            line = _div(rel, 2)
            v = sources[0][at]
            for k in range(1, 4):
                v = jnp.where(line == k, sources[k][at], v)
            out[z.ranks(b), :] = v


def shrink_kernel(z, n_parts, info, x_ref, *refs):
    parts, (full_ref, out_ref) = refs[:n_parts], refs[n_parts:]
    wide = z.width // n_parts
    total = None
    for j in range(n_parts):
        if n_parts == 1:
            cut = slice(0, wide)
        else:
            cut = pl.ds(pl.multiple_of((info[z.quarter] ^ j) * wide, wide), wide)
        full_ref[:, cut] = parts[j][...]
        term = _dot(x_ref[:, cut], parts[j][...], NT)
        total = term if total is None else total + term
    for b in range(z.nb):
        out_ref[:, z.block(b)] = total[z.block(b), :].T[z.ranks(b), :]


def projected_kernel(z, info, base_ref, mine_ref, other_ref, up_ref, out_ref, spread):
    spread[...] = jnp.zeros_like(spread)
    for b in range(z.nb):
        cut = z.block(b)
        spread[z.ranks(b), cut] = (mine_ref[:, cut] + other_ref[:, cut]).astype(bf16)
    wide = _dot(spread[...], up_ref[...], TN)
    for b in range(z.nb):
        cut = z.block(b)
        full = base_ref[cut, :] + adapter_scale * wide[cut]
        out_ref[cut, :] = _masked(full, z.valid(info, b)).astype(bf16)


def through_kernel(z, first, info, g_ref, w_ref, out_ref, *sums):
    step = out_ref.shape[1] // 4
    for h in range(4):
        cut = slice(h * step, (h + 1) * step)
        rows = slice(first + h * step, first + (h + 1) * step)
        out_ref[:, cut] = _dot(g_ref[...], w_ref[rows, :], NT)
    for s in sums:
        one_hot_sums(z, info, s)


def tokens_kernel(z, first, info, through_ref, mine_ref, other_ref, d_ref, *refs):
    out_ref, spread = refs[-2:]
    step = pl.program_id(0)
    wide = out_ref.shape[1]

    @pl.when(step == 0)
    def _():
        spread[...] = jnp.zeros_like(spread)
        for b in range(z.nb):
            cut = z.block(b)
            v = (mine_ref[:, cut] + other_ref[:, cut]) * adapter_scale
            spread[z.ranks(b), cut] = v.astype(bf16)

    here = pl.ds(pl.multiple_of(step * wide, wide), wide)
    cut = pl.ds(pl.multiple_of((first + step) * wide, wide), wide)
    added = _dot(spread[...], d_ref[:, cut], TN)
    out_ref[...] = (through_ref[:, here] + added).astype(bf16)


def on_device(
    n_groups,
    n_dp,
    tokens,
    base_weight,
    adapter_down,
    adapter_up,
    out_cotangent,
    block_tenant,
    block_valid,
    tenant_slot,
):
    nb = block_tenant.shape[0]
    rows, width = tokens.shape
    cols = out_cotangent.shape[1]
    tenants = tenant_slot.shape[0]
    ten_dev, _, rank = adapter_down.shape
    z = Sizes(n_dp, nb, ten_dev, rank, cols, width)
    n_far = z.n_far
    me = lax.axis_index("dp")
    core = lax.axis_index("tensor")
    group = lax.axis_index("groups")
    shared = n_groups == 2 and n_dp == 8
    n_parts = 4 if shared else 1
    mine_q = group * 2 + me % 2 if shared else jnp.int32(0)
    quarter = width // n_parts

    cotangent_other = _swap(out_cotangent, "tensor")

    down_t = jnp.swapaxes(adapter_down, 1, 2)
    if shared:
        to_y = lax.dynamic_slice_in_dim(down_t, (mine_q ^ 1) * quarter, quarter, axis=2)
        from_y = _xor(to_y, n_dp, 1)
    far_up = [_xor(adapter_up, n_dp, NEAR * j) for j in range(1, n_far)]
    lane = jnp.arange(LANES, dtype=i32)

    def spread_out(x):
        hit = lane[:, None] == jnp.arange(x.shape[0], dtype=i32)[None, :]
        return jnp.sum(jnp.where(hit, x[None, :], 0), axis=1).astype(i32)

    own_tenants = spread_out(block_tenant)
    tag = jnp.broadcast_to(own_tenants[None, :], (16, LANES)).astype(bf16)
    tag = jnp.pad(tag, ((0, 0), (0, cols - LANES)))
    ups = [u.reshape(ten_dev * rank, cols) for u in [adapter_up] + far_up]
    packet = jnp.concatenate(ups + [tag], axis=0)
    packets = [packet] + [_xor(packet, n_dp, k) for k in range(1, NEAR)]

    if shared:
        own = lax.dynamic_slice_in_dim(down_t, mine_q * quarter, quarter, axis=2)
        shard = jnp.concatenate([own, from_y], axis=0)
        shard_far = _xor(shard, n_dp, 4)

    line = lax.broadcasted_iota(i32, (16, LANES), 0)
    place = jnp.where(lane == 0, me, jnp.where(lane == 1, core, mine_q))
    info = jnp.where(line == 8, place[None, :], spread_out(block_valid)[None, :])
    info = jnp.where(line == 6, spread_out(tenant_slot)[None, :], info)
    info = jnp.where(line == 0, own_tenants[None, :], info)

    base_other, g_full, x_in = _call(
        functools.partial(base_kernel, z), "base", (1,),
        [pl.BlockSpec(memory_space=pl.ANY)] * 3 + [VMEM],
        [_whole((rows, cols))] + [VMEM] * 2,
        [
            _shape((rows, cols), bf16), _shape((rows, 2 * cols), bf16), _shape(tokens.shape, bf16),
        ],
        [
            pltpu.VMEM((width, cols), bf16), pltpu.VMEM((rows, cols), bf16),
            pltpu.SemaphoreType.DMA((5,)), pltpu.SemaphoreType.DMA((5,)),
            pltpu.SemaphoreType.DMA,
        ],
        vmem=BIG_VMEM,
    )(
        _tie(info, shard if shared else packet),
        tokens, base_weight, out_cotangent, cotangent_other,
    )
    base_arrived = _swap(base_other, "tensor")
    packets = [_tie(p, base_other) for p in packets]

    for k in range(1, NEAR):
        info = jnp.where(line == k, packets[k][-16, :LANES].astype(i32)[None, :], info)

    if shared:
        shard_far = _tie(shard_far, base_other)
        info = _tie(info, shard_far)
        farther = _xor(jnp.concatenate([shard, shard_far], axis=0), n_dp, 2)

    part = (rank, rows)
    block_up, back_part = _call(
        functools.partial(back_kernel, z), "back", (1,),
        [VMEM] * (1 + NEAR), [VMEM, _whole(part)],
        [_shape((nb * rank, cols), bf16), _shape(part, f32)], [],
    )(info, g_full, *packets)
    back_other = _swap(back_part, "tensor")
    ready = [base_arrived]
    if shared:
        info_x = _swap(info, "groups")

    packed_rows = n_dp * CAP * rank
    near_rows = packed_rows // NEAR

    def pack(info, start, wide):
        return _call(
            functools.partial(pack_kernel, z, NEAR, start), "pack_down", (1,),
            [VMEM] * 3, [_whole((near_rows, wide))] * NEAR,
            [_shape((near_rows, wide), bf16)] * NEAR,
            [pltpu.VMEM((packed_rows, rows), bf16)],
        )(info, back_part, back_other, x_in)

    def to_near(sends):
        return [sends[0]] + [_xor(sends[k], n_dp, k) for k in range(1, NEAR)]

    def dense(info, got):
        wide = got[0].shape[1]
        out = (ten_dev * rank, wide)
        return _call(
            functools.partial(dense_kernel, z), "dense", (1,),
            [VMEM] * (1 + NEAR), [VMEM] + [_whole(out)] * (n_far - 1),
            [_shape(out, f32)] + [_shape(out, bf16)] * (n_far - 1), [],
        )(info, sums, *got)

    def to_far(parts):
        return [parts[0]] + [_xor(parts[j], n_dp, NEAR * j) for j in range(1, n_far)]

    def through(info, first, wide, with_sums):
        sums = _shape((n_far, ten_dev * rank, NEAR * CAP * rank), bf16)
        return _call(
            functools.partial(through_kernel, z, first), "through", (1,), [VMEM] * 2,
            [VMEM] * (1 + with_sums), [_shape((rows, wide), f32)] + [sums] * with_sums, [],
        )(info, g_full, base_weight)

    half = width // 2
    wide_a = width * 9 // 16
    sends_a = pack(_tie(info, *ready), 0, wide_a)
    got_a = to_near(sends_a)
    low, sums = through(_tie(info, sends_a[0]), 0, half, 1)

    if shared:
        block = (nb * rank, quarter)
        chosen = _call(
            functools.partial(choose_kernel, z), "choose", (1,),
            [VMEM] * 3, [_whole(block)] * 4, [_shape(block, bf16)] * 4, [],
            n_scalars=2,
        )(_tie(info, low), info_x, shard, shard_far, farther)
        sends_b = pack(_tie(info, chosen[0]), wide_a, width - wide_a)
        got_y = _xor(_tie(chosen[1], got_a[2], sends_b[0]), n_dp, 1)
        got_x = _swap(_tie(chosen[2], sends_b[0]), "groups")
        got_d = lax.ppermute(
            _tie(chosen[3], sends_b[0]),
            ("groups", "dp"),
            [(g * n_dp + d, (1 - g) * n_dp + (d ^ 1)) for g in range(2) for d in range(n_dp)],
        )
    else:
        every = lax.all_gather(down_t, "dp", axis=0, tiled=True)
        slots = jnp.take(tenant_slot, block_tenant, axis=0)
        got_down = [jnp.take(every, slots, axis=0).reshape(nb * rank, width)]
        sends_b = pack(_tie(info, low), wide_a, width - wide_a)

    base_own = _call(
        functools.partial(own_kernel, z), "base_own", (1,),
        [VMEM] * 3, VMEM, _shape((rows, cols), f32), [],
    )(_tie(info, sends_b[0]), x_in, base_weight, base_arrived)
    dense_a = dense(_tie(info, base_own), got_a)
    far_a = to_far(dense_a)

    (high,) = through(_tie(info, dense_a[1]), half, width - half, 0)
    gate = [high] + ([got_y, got_x, got_d] if shared else [])
    got_b = to_near(
        [_tie(b, *gate) if k in (1, 3) else _tie(b, dense_a[1]) for k, b in enumerate(sends_b)]
    )

    if shared:
        got_down = [chosen[0], got_y, got_x, got_d]
    block_down, shrink_part = _call(
        functools.partial(shrink_kernel, z, n_parts), "shrink", (1,),
        [VMEM] * (1 + n_parts), [VMEM, _whole(part)],
        [_shape((nb * rank, width), bf16), _shape(part, f32)], [],
    )(_tie(info, high), x_in, *got_down)
    shrink_other = _swap(shrink_part, "tensor")


    step = min(512, width // 8)

    def token_grads(info, product, first, so_far):
        steps = product.shape[1] // step
        return _call(
            functools.partial(tokens_kernel, z, first), "token_grads", (steps,),
            [VMEM] * 4 + [pl.BlockSpec(memory_space=pl.ANY)] * len(so_far),
            pl.BlockSpec((rows, step), lambda i, *_: (0, first + i)),
            _shape((rows, width), bf16), [pltpu.VMEM((nb * rank, rows), bf16)],
            {5: 0} if so_far else None,
        )(info, product, back_part, back_other, block_down, *so_far)

    grad_tokens = token_grads(_tie(info, shrink_part), low, 0, [])

    up_sends = _call(
        functools.partial(pack_up_kernel, z, NEAR), "pack_up", (1,),
        [VMEM] * 3, [_whole((near_rows, cols))] * NEAR,
        [_shape((near_rows, cols), bf16)] * NEAR,
        [pltpu.VMEM((packed_rows, rows), bf16)],
    )(_tie(info, grad_tokens, far_a[1]), shrink_part, shrink_other, g_full)
    got_u = to_near(up_sends)

    dense_b = dense(_tie(info, up_sends[0]), got_b)
    far_b = to_far(dense_b)

    grad_tokens = token_grads(_tie(info, dense_b[1]), high, half // step, [grad_tokens])
    dense_u = dense(_tie(info, grad_tokens), got_u)
    far_u = to_far(dense_u)

    projected = _call(
        functools.partial(projected_kernel, z), "projected", (1,),
        [VMEM] * 4, _whole((rows, cols)), _shape((rows, cols), bf16),
        [pltpu.VMEM((nb * rank, rows), bf16)],
    )(
        _tie(info, dense_u[1]),
        base_own, shrink_part, shrink_other, block_up,
    )

    outs = [(ten_dev * rank, width), (ten_dev * rank, cols)]
    grad_down, grad_up = _call(
        functools.partial(final_kernel, (2, 1), n_far), "final", (1,),
        [VMEM] * (3 * n_far), [_whole(o) for o in outs], [_shape(o, f32) for o in outs], [],
    )(info, *far_a, *far_b, *far_u)
    grad_down = jnp.swapaxes(grad_down.reshape(ten_dev, rank, width), 1, 2)
    return projected, grad_tokens, grad_down, grad_up.reshape(ten_dev, rank, cols)


def solution(mesh):
    n_groups, n_dp = mesh.shape["groups"], mesh.shape["dp"]
    in_specs = (
        P(("groups", "dp"), "tensor"),
        P("tensor", None),
        P("dp", "tensor", None),
        P("dp", None, "tensor"),
        P(("groups", "dp"), "tensor"),
        P(("groups", "dp")),
        P(("groups", "dp")),
        P("groups"),
    )
    out_specs = (
        P(("groups", "dp"), "tensor"),
        P(("groups", "dp"), "tensor"),
        P(("groups", "dp"), "tensor", None),
        P(("groups", "dp"), None, "tensor"),
    )

    def run(*args):
        return on_device(n_groups, n_dp, *args)

    return jax.shard_map(
        run, mesh=mesh, in_specs=in_specs, out_specs=out_specs, check_vma=False
    )
```
